32 devices in a mesh: section: 4 (over y, core), frames: 8 (over z, x).
Axes of the slice: x: 2, y: 2, z: 4, core: 2. Of those that a mesh axis runs over, the one named last changes fastest.
Arguments:
- frames_in: bfloat16 [1024, 4, 1024], P('frames', 'section'), may hold values from -6 to 6
- segment_ids: int32 [1024], P('frames'), may hold values from 0 to 8, as said below
- cotangent: bfloat16 [1024, 4, 1024], P('frames', 'section'), may hold values from -6 to 6
- norm_attn: float32 [1, 4, 1024], P(None, 'section', 'frames'), may hold values from 0.1 to 1.9
- w_query: bfloat16 [1, 4, 1024, 1024], P(None, 'section', 'frames'), may hold values from -0.1875 to 0.1875
- w_key: bfloat16 [1, 4, 1024, 1024], P(None, 'section', 'frames'), may hold values from -0.1875 to 0.1875
- w_value: bfloat16 [1, 4, 1024, 1024], P(None, 'section', 'frames'), may hold values from -0.1875 to 0.1875
- w_out: bfloat16 [1, 4, 1024, 1024], P(None, 'section', 'frames'), may hold values from -0.25 to 0.25
- norm_ffn: float32 [1, 4, 1024], P(None, 'section', 'frames'), may hold values from 0.1 to 1.9
- w_gate: bfloat16 [1, 4, 1024, 4096], P(None, 'section', 'frames'), may hold values from -0.1875 to 0.1875
- w_up: bfloat16 [1, 4, 1024, 4096], P(None, 'section', 'frames'), may hold values from -0.1875 to 0.1875
- w_down: bfloat16 [1, 4, 4096, 1024], P(None, 'section', 'frames'), may hold values from -0.1875 to 0.1875
Outputs:
- output: bfloat16 [1024, 4, 1024], P('frames', 'section')
- input_grad: float32 [1024, 4, 1024], P('frames', 'section')
- norm_attn_grad: float32 [1, 4, 1024], P(None, 'section', 'frames')
- w_query_grad: float32 [1, 4, 1024, 1024], P(None, 'section', 'frames')
- w_key_grad: float32 [1, 4, 1024, 1024], P(None, 'section', 'frames')
- w_value_grad: float32 [1, 4, 1024, 1024], P(None, 'section', 'frames')
- w_out_grad: float32 [1, 4, 1024, 1024], P(None, 'section', 'frames')
- norm_ffn_grad: float32 [1, 4, 1024], P(None, 'section', 'frames')
- w_gate_grad: float32 [1, 4, 1024, 4096], P(None, 'section', 'frames')
- w_up_grad: float32 [1, 4, 1024, 4096], P(None, 'section', 'frames')
- w_down_grad: float32 [1, 4, 4096, 1024], P(None, 'section', 'frames')
The draws below stay inside these ranges and needn't reach their ends.
Inputs may be any that keep to these rules, and one draw needn't show every extreme that they name: `segment_ids`: frames come in packed rows of 32; within a row the ids never fall except to the padding value 0, which fills a row's end. Only whether an id is 0 enters the computation.
All inputs are finite; a program needn't handle non-finite values.
Results may differ from the reference program's by a relative error of at most 0.03.
Values may be sent and summed in bfloat16 or wider, within the bound.
A program may use at most 256 MiB of HBM per device.

```python
import math
import jax
import jax.numpy as jnp
from jax import lax

D = 1024
HEADS = 16
HEAD_DIM = 64
FF = 4096
LAYERS = 1
ROW_FRAMES = 32
SEGS = 8
POS = 4
TOTAL_FRAMES = 1024


def draw_segment_ids(key, part):
    key = jax.random.fold_in(key, 11)
    first_random_key, second_random_key = jax.random.split(key)
    packed_row_count = TOTAL_FRAMES // ROW_FRAMES
    column_index = jnp.arange(ROW_FRAMES)[None, :]
    row_number = jnp.arange(packed_row_count)[:, None]
    segment_starts = jnp.where(jax.random.randint(first_random_key, (packed_row_count, ROW_FRAMES), 0, 4) == 0, 1, 0)
    segment_starts = jnp.where(column_index == 0, 0, segment_starts)
    forced = (row_number == 0) & (column_index >= 1) & (column_index < SEGS)
    segment_starts = jnp.where(forced, 1, segment_starts)
    frame_numbers = jnp.minimum(1 + jnp.cumsum(segment_starts, axis=1), SEGS)
    padding_frames = jax.random.randint(second_random_key, (packed_row_count, 1), 0, ROW_FRAMES // 4 + 1)
    padding_frames = jnp.maximum(padding_frames, jnp.where(row_number == 0, 1, 0))
    frame_numbers = jnp.where(column_index >= ROW_FRAMES - padding_frames, 0, frame_numbers)
    return frame_numbers.reshape(TOTAL_FRAMES).astype(jnp.int32)


def levels(rng, dims, shards, smallest, top_value):
    level = 1.0
    for dim, blocks in shards:
        heights = jax.random.uniform(jax.random.fold_in(jax.random.fold_in(rng, 6), dim), (blocks,), jnp.float32, smallest / len(shards), top_value / len(shards))
        level = level * jnp.repeat(jnp.exp(heights), dims[dim] // blocks).reshape((-1,) + (1,) * (len(dims) - 1 - dim))
    return level


def normal_values(stream_key, extent, scale, limit, cuts=(), kind=jnp.bfloat16):
    level = levels(stream_key, extent, cuts, -0.22, 0.18) if cuts else 1.0
    entries = jax.random.normal(stream_key, extent, jnp.float32) * scale * level
    return jnp.minimum(jnp.maximum(entries, -limit), limit).astype(kind)


def setup_inputs(seed: int = 0) -> dict:
    keys = jax.random.split(jax.random.key(seed), 13)
    frames_in = normal_values(keys[0], (TOTAL_FRAMES, POS, D), 1.0, 6.0, ((0, 8), (1, 4)))
    segment_ids = draw_segment_ids(jax.random.fold_in(keys[12], 71), 0)
    cotangent = normal_values(keys[2], (TOTAL_FRAMES, POS, D), 1.0, 6.0, ((0, 8), (1, 4)))
    norm_attn = jnp.clip(1.0 + 0.18 * jax.random.normal(keys[3], (LAYERS, POS, D), jnp.float32), 0.1, 1.9)
    w_query = normal_values(keys[4], (LAYERS, POS, D, D), D ** -0.5, 0.1875, ((1, 4), (2, 8)))
    w_key = normal_values(keys[5], (LAYERS, POS, D, D), D ** -0.5, 0.1875, ((1, 4), (2, 8)))
    w_value = normal_values(keys[6], (LAYERS, POS, D, D), D ** -0.5, 0.1875, ((1, 4), (2, 8)))
    w_out = normal_values(keys[7], (LAYERS, POS, D, D), (D // 2) ** -0.5, 0.25, ((1, 4), (2, 8)))
    norm_ffn = jnp.clip(1.0 + 0.18 * jax.random.normal(keys[8], (LAYERS, POS, D), jnp.float32), 0.1, 1.9)
    w_gate = normal_values(keys[9], (LAYERS, POS, D, FF), D ** -0.5, 0.1875, ((1, 4), (2, 8)))
    w_up = normal_values(keys[10], (LAYERS, POS, D, FF), D ** -0.5, 0.1875, ((1, 4), (2, 8)))
    w_down = normal_values(keys[11], (LAYERS, POS, FF, D), (FF // 4) ** -0.5, 0.1875, ((1, 4), (2, 8)))
    return {"frames_in": frames_in, "segment_ids": segment_ids, "cotangent": cotangent, "norm_attn": norm_attn, "w_query": w_query, "w_key": w_key, "w_value": w_value, "w_out": w_out, "norm_ffn": norm_ffn, "w_gate": w_gate, "w_up": w_up, "w_down": w_down}


epsilon = 1e-05

@jax.custom_vjp
def low(v):
    return lax.optimization_barrier(v.astype(jnp.bfloat16)).astype(jnp.float32)

@jax.custom_vjp
def low_back(v):
    return v

def low_keep(v):
    return (low(v), None)

def low_pass(kept, grad):
    return (grad,)

def back_keep(v):
    return (v, None)

def back_low(kept, grad):
    return (low(grad),)
low.defvjp(low_keep, low_pass)
low_back.defvjp(back_keep, back_low)

def rms_scale(values, gain):
    return values * lax.rsqrt(lax.optimization_barrier(jnp.mean(values * values, axis=-1, keepdims=True)) + epsilon) * gain

def per_position(left, weight):
    return jnp.einsum('bpd,pde->bpe', left, weight, precision=lax.Precision.HIGHEST)

def attend_all(query_vec, key_all, values):
    scores = jnp.einsum('bphe,bqhe->bhpq', query_vec, key_all, precision=lax.Precision.HIGHEST) * HEAD_DIM ** (-0.5)
    length = query_vec.shape[1]
    allowed = jnp.arange(length)[:, None] >= jnp.arange(length)[None, :]
    scores = jnp.where(allowed, scores, -1e+30)
    largest = lax.optimization_barrier(jnp.max(scores, axis=-1, keepdims=True))
    expo_terms = jnp.exp(scores - largest)
    weights = expo_terms / lax.optimization_barrier(jnp.sum(expo_terms, axis=-1, keepdims=True))
    return jnp.einsum('bhpq,bqhe->bphe', weights, values, precision=lax.Precision.HIGHEST)

def forward(stream, params_in):
    batch_rows = stream.shape[0]
    for layer_idx in range(LAYERS):
        gain_one, wq_l, wk_l, wv_l, wo_l, gain_two, wg_l, wu_l, wd_l = [item[layer_idx] for item in params_in]
        normed = low(rms_scale(stream, gain_one))
        query_vec = low_back(low(per_position(normed, wq_l))).reshape(batch_rows, POS, HEADS, HEAD_DIM)
        key_all = low_back(low(per_position(normed, wk_l))).reshape(batch_rows, POS, HEADS, HEAD_DIM)
        values = low_back(low(per_position(normed, wv_l))).reshape(batch_rows, POS, HEADS, HEAD_DIM)
        mixed_out = low(attend_all(query_vec, key_all, values).reshape(batch_rows, POS, D))
        middle = stream + low_back(per_position(mixed_out, wo_l))
        normed2 = low(rms_scale(middle, gain_two))
        gate_act = low_back(per_position(normed2, wg_l))
        up_act = low_back(per_position(normed2, wu_l))
        hidden = low(jax.nn.silu(gate_act) * up_act)
        stream = middle + low_back(per_position(hidden, wd_l))
    return stream

def reference(frames_in, segment_ids, cotangent, norm_attn, w_query, w_key, w_value, w_out, norm_ffn, w_gate, w_up, w_down):
    block_rows = math.gcd(TOTAL_FRAMES, 1024)
    block_count = TOTAL_FRAMES // block_rows
    params_in = tuple((item.astype(jnp.float32) for item in (norm_attn, w_query, w_key, w_value, w_out, norm_ffn, w_gate, w_up, w_down)))
    frame_mask = (segment_ids != 0).astype(jnp.float32)[:, None, None]
    stream = frames_in.astype(jnp.float32).reshape(block_count, block_rows, POS, D)
    cot_all = (cotangent.astype(jnp.float32) * frame_mask).reshape(block_count, block_rows, POS, D)

    def step(accumulated, batch):
        frame_block, cot_block = batch
        block_out, pullback = jax.vjp(forward, frame_block, params_in)
        block_grad, param_grads = pullback(cot_block)
        accumulated = tuple((first + second for first, second in zip(accumulated, param_grads)))
        return (accumulated, (block_out.astype(jnp.bfloat16), block_grad))
    start = tuple((jnp.zeros(item.shape, jnp.float32) for item in params_in))
    totals, (outputs, grads_in) = lax.scan(step, start, (stream, cot_all))
    output = outputs.reshape(TOTAL_FRAMES, POS, D)
    input_grad = grads_in.reshape(TOTAL_FRAMES, POS, D)
    return (output, input_grad, totals[0], totals[1], totals[2], totals[3], totals[4], totals[5], totals[6], totals[7], totals[8])
```

```python
import jax
import jax.numpy as jnp
from jax import lax
from jax.sharding import PartitionSpec as P

HEAD_DIM = 64
MICRO = 2


epsilon = 1e-05


def carried_in(shard, axis, combine, identity):
    devices, place = (lax.axis_size(axis), lax.axis_index(axis))
    everything = lax.all_gather(shard, axis)
    start = jnp.broadcast_to(jnp.asarray(identity, shard.dtype), shard.shape)

    def hop(k, before):
        reached = k < place
        new = combine(before, everything[k])
        return jnp.where(reached, new, before)

    return lax.fori_loop(0, devices, hop, start)


def carried_in_2(shard, axis, combine, identity):
    devices, place = (lax.axis_size(axis), lax.axis_index(axis))
    everything = lax.all_gather(shard.astype(jnp.bfloat16), axis)
    start = jnp.broadcast_to(jnp.asarray(identity, shard.dtype), shard.shape)

    def hop(k, before):
        at = devices - 1 - k
        reached = at > place
        new = combine(before, everything[at].astype(shard.dtype))
        return jnp.where(reached, new, before)

    return lax.fori_loop(0, devices, hop, start)


def rms_scale(values, gain):
    return values * lax.rsqrt(jnp.mean(values * values, axis=-1, keepdims=True) + epsilon) * gain


def project(left, weight):
    return jnp.dot(left, weight, preferred_element_type=jnp.float32)


def left_product(left, right):
    return lax.dot_general(
        left, right, (((0,), (0,)), ((), ())), preferred_element_type=jnp.float32
    )


def right_product(left, weight):
    return lax.dot_general(
        left, weight, (((1,), (1,)), ((), ())), preferred_element_type=jnp.float32
    )


def add_pair(first_part, second_part):
    return first_part + second_part


def attend(query_vec, key_all, values, section_idx):
    scores = jnp.einsum(
        "mhe,mphe->mhp", query_vec, key_all, precision=lax.Precision.HIGHEST
    ) * HEAD_DIM ** (-0.5)
    allowed = jnp.arange(key_all.shape[1]) <= section_idx
    scores = jnp.where(allowed, scores, -1e30)
    largest = jnp.max(scores, axis=-1, keepdims=True)
    expo_terms = jnp.exp(scores - largest)
    weights = expo_terms / jnp.sum(expo_terms, axis=-1, keepdims=True)
    return jnp.einsum("mhp,mphe->mhe", weights, values, precision=lax.Precision.HIGHEST)


def share_kv(own_kv, slot_mask):
    placed = jnp.where(slot_mask[None, :, None], own_kv[:, None, :], jnp.zeros((), jnp.bfloat16))
    earlier = carried_in(placed, "section", add_pair, jnp.zeros_like(placed))
    return earlier + placed


def return_kv_grads(grad_kv, section_idx):
    later_sum = carried_in_2(grad_kv, "section", add_pair, jnp.zeros_like(grad_kv))
    return lax.dynamic_index_in_dim(later_sum + grad_kv, section_idx, 1, keepdims=False)


def layer_rest(frame_rows, weights, query_vec, full_kv, section_idx):
    gain_one, wq_l, wk_l, wv_l, wo_l, gain_two, wg_l, wu_l, wd_l = weights
    packed_row_count = frame_rows.shape[0]
    model_width = frame_rows.shape[1]
    head_count = model_width // HEAD_DIM
    positions = full_kv.shape[1]
    key_all = (
        full_kv[:, :, :model_width]
        .astype(jnp.float32)
        .reshape(packed_row_count, positions, head_count, HEAD_DIM)
    )
    values = (
        full_kv[:, :, model_width:]
        .astype(jnp.float32)
        .reshape(packed_row_count, positions, head_count, HEAD_DIM)
    )
    query_f = query_vec.astype(jnp.float32).reshape(packed_row_count, head_count, HEAD_DIM)
    mixed_out = (
        attend(query_f, key_all, values, section_idx)
        .reshape(packed_row_count, model_width)
        .astype(jnp.bfloat16)
    )
    middle = frame_rows + project(mixed_out, wo_l)
    normed2 = rms_scale(middle, gain_two).astype(jnp.bfloat16)
    gate_act = project(normed2, wg_l)
    up_act = project(normed2, wu_l)
    hidden = (jax.nn.silu(gate_act) * up_act).astype(jnp.bfloat16)
    result = middle + project(hidden, wd_l)
    return (query_f, key_all, values, mixed_out, middle, normed2, gate_act, up_act, hidden, result)


def gather_plan(
    frames_in,
    segment_ids,
    cotangent,
    norm_attn,
    w_query,
    w_key,
    w_value,
    w_out,
    norm_ffn,
    w_gate,
    w_up,
    w_down,
):
    section_idx = lax.axis_index("section")
    frame_count = frames_in.shape[0]
    model_width = frames_in.shape[2]
    head_count = model_width // HEAD_DIM
    micro_rows = frame_count // MICRO
    positions = lax.axis_size("section") * frames_in.shape[1]
    layer_count = w_query.shape[0]
    slot_mask = jnp.arange(positions) == section_idx
    stream = frames_in[:, 0, :].astype(jnp.float32)
    layer_idx = 0
    pieces = (
        norm_attn[layer_idx],
        w_query[layer_idx],
        w_key[layer_idx],
        w_value[layer_idx],
        w_out[layer_idx],
        norm_ffn[layer_idx],
        w_gate[layer_idx],
        w_up[layer_idx],
        w_down[layer_idx],
    )
    gathered = (
        lax.all_gather(pieces[0].astype(jnp.bfloat16), "frames", axis=1, tiled=True).astype(
            jnp.float32
        ),
        lax.all_gather(pieces[1], "frames", axis=1, tiled=True),
        lax.all_gather(pieces[2], "frames", axis=1, tiled=True),
        lax.all_gather(pieces[3], "frames", axis=1, tiled=True),
        lax.all_gather(pieces[4], "frames", axis=1, tiled=True),
        lax.all_gather(pieces[5].astype(jnp.bfloat16), "frames", axis=1, tiled=True).astype(
            jnp.float32
        ),
        lax.all_gather(pieces[6], "frames", axis=1, tiled=True),
        lax.all_gather(pieces[7], "frames", axis=1, tiled=True),
        lax.all_gather(pieces[8], "frames", axis=1, tiled=True),
    )
    weights = tuple((gathered_item[0] for gathered_item in gathered))
    layer_inputs = []
    layer_kv = []
    results = []
    for micro_idx in range(MICRO):
        frame_rows = stream[micro_idx * micro_rows : (micro_idx + 1) * micro_rows]
        normed = rms_scale(frame_rows, weights[0]).astype(jnp.bfloat16)
        query_vec = project(normed, weights[1]).astype(jnp.bfloat16)
        own_kv = jnp.concatenate(
            [
                project(normed, weights[2]).astype(jnp.bfloat16),
                project(normed, weights[3]).astype(jnp.bfloat16),
            ],
            axis=-1,
        )
        full_kv = share_kv(own_kv, slot_mask)
        outcome = layer_rest(frame_rows, weights, query_vec, full_kv, section_idx)
        layer_inputs.append(frame_rows)
        layer_kv.append(full_kv)
        results.append(outcome[-1])
    kept_inputs = [layer_inputs]
    kept_kv = [layer_kv]
    stream = jnp.concatenate(results, axis=0)
    output = stream.astype(jnp.bfloat16)[:, None, :]
    frame_mask = (segment_ids != 0).astype(jnp.float32)[:, None]
    upstream_all = cotangent[:, 0, :].astype(jnp.float32) * frame_mask
    upstream = [
        upstream_all[micro_idx * micro_rows : (micro_idx + 1) * micro_rows]
        for micro_idx in range(MICRO)
    ]
    layer_grads = [None] * layer_count
    for layer_idx in reversed(range(layer_count)):
        pieces = (
            norm_attn[layer_idx],
            w_query[layer_idx],
            w_key[layer_idx],
            w_value[layer_idx],
            w_out[layer_idx],
            norm_ffn[layer_idx],
            w_gate[layer_idx],
            w_up[layer_idx],
            w_down[layer_idx],
        )
        gathered = (
            lax.all_gather(pieces[0].astype(jnp.bfloat16), "frames", axis=1, tiled=True).astype(
                jnp.float32
            ),
            lax.all_gather(pieces[1], "frames", axis=1, tiled=True),
            lax.all_gather(pieces[2], "frames", axis=1, tiled=True),
            lax.all_gather(pieces[3], "frames", axis=1, tiled=True),
            lax.all_gather(pieces[4], "frames", axis=1, tiled=True),
            lax.all_gather(pieces[5].astype(jnp.bfloat16), "frames", axis=1, tiled=True).astype(
                jnp.float32
            ),
            lax.all_gather(pieces[6], "frames", axis=1, tiled=True),
            lax.all_gather(pieces[7], "frames", axis=1, tiled=True),
            lax.all_gather(pieces[8], "frames", axis=1, tiled=True),
        )
        weights = tuple((gathered_item[0] for gathered_item in gathered))
        gain_one, wq_l, wk_l, wv_l, wo_l, gain_two, wg_l, wu_l, wd_l = weights
        totals = [jnp.zeros(item.shape, jnp.float32) for item in weights]
        for micro_idx in range(MICRO):
            micro_grads = [None] * 9
            frame_rows = kept_inputs[layer_idx][micro_idx]
            full_kv = kept_kv[layer_idx][micro_idx]
            grad_out = upstream[micro_idx]
            normed = rms_scale(frame_rows, gain_one).astype(jnp.bfloat16)
            query_vec = project(normed, wq_l).astype(jnp.bfloat16)
            (
                query_f,
                key_all,
                values,
                mixed_out,
                middle,
                normed2,
                gate_act,
                up_act,
                hidden,
                result,
            ) = layer_rest(frame_rows, weights, query_vec, full_kv, section_idx)
            down_in = grad_out.astype(jnp.bfloat16)
            micro_grads[8] = left_product(hidden, down_in)
            hidden_grad = right_product(down_in, wd_l)
            _, pullback = jax.vjp(
                lambda gate_in, up_in: jax.nn.silu(gate_in) * up_in, gate_act, up_act
            )
            gate_grad, up_grad = pullback(hidden_grad)
            gate_grad = gate_grad.astype(jnp.bfloat16)
            up_grad = up_grad.astype(jnp.bfloat16)
            micro_grads[6] = left_product(normed2, gate_grad)
            micro_grads[7] = left_product(normed2, up_grad)
            normed2_grad = right_product(gate_grad, wg_l) + right_product(up_grad, wu_l)
            _, pullback = jax.vjp(rms_scale, middle, gain_two)
            middle_part, gain_two_part = pullback(normed2_grad)
            middle_grad = grad_out + middle_part
            micro_grads[5] = gain_two_part
            branch_in = middle_grad.astype(jnp.bfloat16)
            micro_grads[4] = left_product(mixed_out, branch_in)
            mixed_grad = right_product(branch_in, wo_l)
            _, pullback = jax.vjp(
                lambda query_in, key_in, value_in: attend(query_in, key_in, value_in, section_idx),
                query_f,
                key_all,
                values,
            )
            query_grad, key_grad, value_grad = pullback(
                mixed_grad.reshape(micro_rows, head_count, HEAD_DIM)
            )
            grad_kv = jnp.concatenate(
                [
                    key_grad.reshape(micro_rows, positions, model_width),
                    value_grad.reshape(micro_rows, positions, model_width),
                ],
                axis=-1,
            )
            own_grad = return_kv_grads(grad_kv, section_idx)
            query_low = query_grad.reshape(micro_rows, model_width).astype(jnp.bfloat16)
            key_low = own_grad[:, :model_width].astype(jnp.bfloat16)
            value_low = own_grad[:, model_width:].astype(jnp.bfloat16)
            micro_grads[1] = left_product(normed, query_low)
            micro_grads[2] = left_product(normed, key_low)
            micro_grads[3] = left_product(normed, value_low)
            normed_grad = (
                right_product(query_low, wq_l)
                + right_product(key_low, wk_l)
                + right_product(value_low, wv_l)
            )
            _, pullback = jax.vjp(rms_scale, frame_rows, gain_one)
            rows_part, gain_one_part = pullback(normed_grad)
            micro_grads[0] = gain_one_part
            upstream[micro_idx] = middle_grad + rows_part
            totals = [first + second for first, second in zip(totals, micro_grads)]
        layer_grads[layer_idx] = lax.psum_scatter(
            tuple((item[None] for item in totals)), "frames", scatter_dimension=1, tiled=True
        )
    input_grad = jnp.concatenate(upstream, axis=0)[:, None, :]
    stacked = tuple((jnp.stack([layer_grads[0][which]]) for which in range(9)))
    return (
        output,
        input_grad,
        stacked[0],
        stacked[1],
        stacked[2],
        stacked[3],
        stacked[4],
        stacked[5],
        stacked[6],
        stacked[7],
        stacked[8],
    )


def to_columns(weight, axis):
    rows, cols = weight.shape
    n = lax.axis_size(axis)
    split = weight.reshape(rows, n, cols // n)
    moved = lax.all_to_all(split, axis, 1, 0, tiled=False)
    return moved.reshape(n * rows, cols // n)


def to_rows(grad, axis):
    rows, cols = grad.shape
    n = lax.axis_size(axis)
    split = grad.astype(jnp.bfloat16).reshape(n, rows // n, cols)
    moved = lax.all_to_all(split, axis, 0, 1, tiled=False)
    return moved.reshape(rows // n, n * cols).astype(jnp.float32)


def rms_back(grad, values, gain):
    inverse = lax.rsqrt(jnp.mean(values * values, axis=-1, keepdims=True) + epsilon)
    n = values * inverse
    scaled = grad * gain
    part = (scaled - n * jnp.mean(scaled * n, axis=-1, keepdims=True)) * inverse
    return part, jnp.sum(grad * n, axis=0)


def gather_rows(rows):
    return lax.all_gather(rows, "frames", axis=0, tiled=True)


def scatter_rows(partial):
    return lax.psum_scatter(
        partial.astype(jnp.bfloat16), "frames", scatter_dimension=0, tiled=True
    ).astype(jnp.float32)


def column_plan(
    frames_in,
    segment_ids,
    cotangent,
    norm_attn,
    w_query,
    w_key,
    w_value,
    w_out,
    norm_ffn,
    w_gate,
    w_up,
    w_down,
):
    section_idx = lax.axis_index("section")
    section_count = lax.axis_size("section")
    local_rows, _, width = frames_in.shape
    n = lax.axis_size("frames")
    rows = n * local_rows
    cols = width // n
    heads = cols // HEAD_DIM

    gain_one = lax.all_gather(norm_attn[0, 0], "frames", axis=0, tiled=True)
    gain_two = lax.all_gather(norm_ffn[0, 0], "frames", axis=0, tiled=True)
    wq = to_columns(w_query[0, 0], "frames")
    wk = to_columns(w_key[0, 0], "frames")
    wv = to_columns(w_value[0, 0], "frames")
    wg = to_columns(w_gate[0, 0], "frames")
    wu = to_columns(w_up[0, 0], "frames")
    wo = w_out[0, 0]
    wd = w_down[0, 0]

    stream = frames_in[:, 0, :].astype(jnp.float32)
    mask = (segment_ids != 0).astype(jnp.float32)[:, None]
    grad_out = cotangent[:, 0, :].astype(jnp.float32) * mask
    down_in = gather_rows(grad_out.astype(jnp.bfloat16))

    normed = gather_rows(rms_scale(stream, gain_one).astype(jnp.bfloat16))
    query = project(normed, wq).astype(jnp.bfloat16)
    kv = jnp.concatenate(
        [project(normed, wk).astype(jnp.bfloat16), project(normed, wv).astype(jnp.bfloat16)], axis=-1
    )
    kv_all = lax.all_gather(kv, "section", axis=0, tiled=False)

    def heads_of(item):
        return item.astype(jnp.float32).reshape(item.shape[:-1] + (heads, HEAD_DIM))

    query_f = heads_of(query)
    key_all = heads_of(kv_all[..., :cols])
    value_all = heads_of(kv_all[..., cols:])
    allowed = (jnp.arange(section_count) <= section_idx)[:, None, None]
    scores = jnp.sum(query_f[None] * key_all, axis=-1) * HEAD_DIM ** (-0.5)
    scores = jnp.where(allowed, scores, -1e30)
    expo = jnp.exp(scores - jnp.max(scores, axis=0, keepdims=True))
    attn = expo / jnp.sum(expo, axis=0, keepdims=True)
    mixed = jnp.sum(attn[..., None] * value_all, axis=0).reshape(rows, cols).astype(jnp.bfloat16)

    middle = stream + scatter_rows(project(mixed, wo))
    normed2 = gather_rows(rms_scale(middle, gain_two).astype(jnp.bfloat16))
    gate_act = project(normed2, wg)
    up_act = project(normed2, wu)
    sig = jax.nn.sigmoid(gate_act)
    silu = gate_act * sig
    hidden = (silu * up_act).astype(jnp.bfloat16)
    output = (middle + scatter_rows(project(hidden, wd))).astype(jnp.bfloat16)[:, None, :]

    w_down_grad = left_product(hidden, down_in)
    hidden_grad = right_product(down_in, wd)
    gate_grad = (hidden_grad * up_act * (sig * (1 + gate_act * (1 - sig)))).astype(jnp.bfloat16)
    up_grad = (hidden_grad * silu).astype(jnp.bfloat16)
    normed2_grad = scatter_rows(right_product(gate_grad, wg) + right_product(up_grad, wu))
    w_gate_grad = to_rows(left_product(normed2, gate_grad), "frames")
    w_up_grad = to_rows(left_product(normed2, up_grad), "frames")
    middle_part, gain_two_part = rms_back(normed2_grad, middle, gain_two)
    middle_grad = grad_out + middle_part
    branch_in = gather_rows(middle_grad.astype(jnp.bfloat16))
    w_out_grad = left_product(mixed, branch_in)
    mixed_grad = heads_of(right_product(branch_in, wo))

    inner = jnp.sum(mixed_grad[None] * value_all, axis=-1)
    score_grad = attn * (inner - jnp.sum(attn * inner, axis=0, keepdims=True)) * HEAD_DIM ** (-0.5)
    query_grad = jnp.sum(score_grad[..., None] * key_all, axis=0).reshape(rows, cols).astype(jnp.bfloat16)
    key_part = (score_grad[..., None] * query_f[None]).reshape(section_count, rows, cols)
    value_part = (attn[..., None] * mixed_grad[None]).reshape(section_count, rows, cols)
    kv_part = jnp.concatenate([key_part, value_part], axis=-1)
    kv_grad = lax.psum_scatter(kv_part.astype(jnp.bfloat16), "section", scatter_dimension=0, tiled=True)[0]
    key_grad = kv_grad[:, :cols]
    value_grad = kv_grad[:, cols:]
    normed_grad = scatter_rows(
        right_product(query_grad, wq) + right_product(key_grad, wk) + right_product(value_grad, wv)
    )
    w_query_grad = to_rows(left_product(normed, query_grad), "frames")
    w_key_grad = to_rows(left_product(normed, key_grad), "frames")
    w_value_grad = to_rows(left_product(normed, value_grad), "frames")
    rows_part, gain_one_part = rms_back(normed_grad, stream, gain_one)
    input_grad = (middle_grad + rows_part)[:, None, :]
    gains = lax.psum_scatter(
        jnp.stack([gain_one_part, gain_two_part]), "frames", scatter_dimension=1, tiled=True
    )
    return (
        output,
        input_grad,
        gains[0][None, None],
        w_query_grad[None, None],
        w_key_grad[None, None],
        w_value_grad[None, None],
        w_out_grad[None, None],
        gains[1][None, None],
        w_gate_grad[None, None],
        w_up_grad[None, None],
        w_down_grad[None, None],
    )


def solution(mesh):
    placed = (
        P("frames", "section", None),
        P("frames"),
        P("frames", "section", None),
        P(None, "section", "frames"),
        P(None, "section", "frames", None),
        P(None, "section", "frames", None),
        P(None, "section", "frames", None),
        P(None, "section", "frames", None),
        P(None, "section", "frames"),
        P(None, "section", "frames", None),
        P(None, "section", "frames", None),
        P(None, "section", "frames", None),
    )
    devices = mesh.shape["frames"]

    def per_device(*arrays):
        width = arrays[0].shape[2]
        fits = arrays[4].shape[0] == 1 and arrays[0].shape[1] == 1 and width % (devices * 128) == 0
        return column_plan(*arrays) if fits else gather_plan(*arrays)

    return jax.shard_map(
        per_device,
        mesh=mesh,
        in_specs=placed,
        out_specs=(
            P("frames", "section", None),
            P("frames", "section", None),
            P(None, "section", "frames"),
            P(None, "section", "frames", None),
            P(None, "section", "frames", None),
            P(None, "section", "frames", None),
            P(None, "section", "frames", None),
            P(None, "section", "frames"),
            P(None, "section", "frames", None),
            P(None, "section", "frames", None),
            P(None, "section", "frames", None),
        ),
        check_vma=False,
    )
```

```python
import functools

import jax
import jax.numpy as jnp
from jax import lax
from jax.experimental import pallas as pl
from jax.experimental.pallas import tpu as pltpu
from jax.sharding import PartitionSpec as P

HEAD_DIM = 64
MICRO = 2
VMEM_LIMIT = 63 * 1024 * 1024


epsilon = 1e-05


def carried_in(shard, axis, combine, identity):
    devices, place = (lax.axis_size(axis), lax.axis_index(axis))
    everything = lax.all_gather(shard, axis)
    start = jnp.broadcast_to(jnp.asarray(identity, shard.dtype), shard.shape)

    def hop(k, before):
        reached = k < place
        new = combine(before, everything[k])
        return jnp.where(reached, new, before)

    return lax.fori_loop(0, devices, hop, start)


def carried_in_2(shard, axis, combine, identity):
    devices, place = (lax.axis_size(axis), lax.axis_index(axis))
    everything = lax.all_gather(shard.astype(jnp.bfloat16), axis)
    start = jnp.broadcast_to(jnp.asarray(identity, shard.dtype), shard.shape)

    def hop(k, before):
        at = devices - 1 - k
        reached = at > place
        new = combine(before, everything[at].astype(shard.dtype))
        return jnp.where(reached, new, before)

    return lax.fori_loop(0, devices, hop, start)


def rms_scale(values, gain):
    return values * lax.rsqrt(jnp.mean(values * values, axis=-1, keepdims=True) + epsilon) * gain


def project(left, weight):
    return jnp.dot(left, weight, preferred_element_type=jnp.float32)


def left_product(left, right):
    return lax.dot_general(
        left, right, (((0,), (0,)), ((), ())), preferred_element_type=jnp.float32
    )


def right_product(left, weight):
    return lax.dot_general(
        left, weight, (((1,), (1,)), ((), ())), preferred_element_type=jnp.float32
    )


def add_pair(first_part, second_part):
    return first_part + second_part


def attend(query_vec, key_all, values, section_idx):
    scores = jnp.einsum(
        "mhe,mphe->mhp", query_vec, key_all, precision=lax.Precision.HIGHEST
    ) * HEAD_DIM ** (-0.5)
    allowed = jnp.arange(key_all.shape[1]) <= section_idx
    scores = jnp.where(allowed, scores, -1e30)
    largest = jnp.max(scores, axis=-1, keepdims=True)
    expo_terms = jnp.exp(scores - largest)
    weights = expo_terms / jnp.sum(expo_terms, axis=-1, keepdims=True)
    return jnp.einsum("mhp,mphe->mhe", weights, values, precision=lax.Precision.HIGHEST)


def share_kv(own_kv, slot_mask):
    placed = jnp.where(slot_mask[None, :, None], own_kv[:, None, :], jnp.zeros((), jnp.bfloat16))
    earlier = carried_in(placed, "section", add_pair, jnp.zeros_like(placed))
    return earlier + placed


def return_kv_grads(grad_kv, section_idx):
    later_sum = carried_in_2(grad_kv, "section", add_pair, jnp.zeros_like(grad_kv))
    return lax.dynamic_index_in_dim(later_sum + grad_kv, section_idx, 1, keepdims=False)


def layer_rest(frame_rows, weights, query_vec, full_kv, section_idx):
    gain_one, wq_l, wk_l, wv_l, wo_l, gain_two, wg_l, wu_l, wd_l = weights
    packed_row_count = frame_rows.shape[0]
    model_width = frame_rows.shape[1]
    head_count = model_width // HEAD_DIM
    positions = full_kv.shape[1]
    key_all = (
        full_kv[:, :, :model_width]
        .astype(jnp.float32)
        .reshape(packed_row_count, positions, head_count, HEAD_DIM)
    )
    values = (
        full_kv[:, :, model_width:]
        .astype(jnp.float32)
        .reshape(packed_row_count, positions, head_count, HEAD_DIM)
    )
    query_f = query_vec.astype(jnp.float32).reshape(packed_row_count, head_count, HEAD_DIM)
    mixed_out = (
        attend(query_f, key_all, values, section_idx)
        .reshape(packed_row_count, model_width)
        .astype(jnp.bfloat16)
    )
    middle = frame_rows + project(mixed_out, wo_l)
    normed2 = rms_scale(middle, gain_two).astype(jnp.bfloat16)
    gate_act = project(normed2, wg_l)
    up_act = project(normed2, wu_l)
    hidden = (jax.nn.silu(gate_act) * up_act).astype(jnp.bfloat16)
    result = middle + project(hidden, wd_l)
    return (query_f, key_all, values, mixed_out, middle, normed2, gate_act, up_act, hidden, result)


def gather_plan(
    frames_in,
    segment_ids,
    cotangent,
    norm_attn,
    w_query,
    w_key,
    w_value,
    w_out,
    norm_ffn,
    w_gate,
    w_up,
    w_down,
):
    section_idx = lax.axis_index("section")
    frame_count = frames_in.shape[0]
    model_width = frames_in.shape[2]
    head_count = model_width // HEAD_DIM
    micro_rows = frame_count // MICRO
    positions = lax.axis_size("section") * frames_in.shape[1]
    layer_count = w_query.shape[0]
    slot_mask = jnp.arange(positions) == section_idx
    stream = frames_in[:, 0, :].astype(jnp.float32)
    layer_idx = 0
    pieces = (
        norm_attn[layer_idx],
        w_query[layer_idx],
        w_key[layer_idx],
        w_value[layer_idx],
        w_out[layer_idx],
        norm_ffn[layer_idx],
        w_gate[layer_idx],
        w_up[layer_idx],
        w_down[layer_idx],
    )
    gathered = (
        lax.all_gather(pieces[0].astype(jnp.bfloat16), "frames", axis=1, tiled=True).astype(
            jnp.float32
        ),
        lax.all_gather(pieces[1], "frames", axis=1, tiled=True),
        lax.all_gather(pieces[2], "frames", axis=1, tiled=True),
        lax.all_gather(pieces[3], "frames", axis=1, tiled=True),
        lax.all_gather(pieces[4], "frames", axis=1, tiled=True),
        lax.all_gather(pieces[5].astype(jnp.bfloat16), "frames", axis=1, tiled=True).astype(
            jnp.float32
        ),
        lax.all_gather(pieces[6], "frames", axis=1, tiled=True),
        lax.all_gather(pieces[7], "frames", axis=1, tiled=True),
        lax.all_gather(pieces[8], "frames", axis=1, tiled=True),
    )
    weights = tuple((gathered_item[0] for gathered_item in gathered))
    layer_inputs = []
    layer_kv = []
    results = []
    for micro_idx in range(MICRO):
        frame_rows = stream[micro_idx * micro_rows : (micro_idx + 1) * micro_rows]
        normed = rms_scale(frame_rows, weights[0]).astype(jnp.bfloat16)
        query_vec = project(normed, weights[1]).astype(jnp.bfloat16)
        own_kv = jnp.concatenate(
            [
                project(normed, weights[2]).astype(jnp.bfloat16),
                project(normed, weights[3]).astype(jnp.bfloat16),
            ],
            axis=-1,
        )
        full_kv = share_kv(own_kv, slot_mask)
        outcome = layer_rest(frame_rows, weights, query_vec, full_kv, section_idx)
        layer_inputs.append(frame_rows)
        layer_kv.append(full_kv)
        results.append(outcome[-1])
    kept_inputs = [layer_inputs]
    kept_kv = [layer_kv]
    stream = jnp.concatenate(results, axis=0)
    output = stream.astype(jnp.bfloat16)[:, None, :]
    frame_mask = (segment_ids != 0).astype(jnp.float32)[:, None]
    upstream_all = cotangent[:, 0, :].astype(jnp.float32) * frame_mask
    upstream = [
        upstream_all[micro_idx * micro_rows : (micro_idx + 1) * micro_rows]
        for micro_idx in range(MICRO)
    ]
    layer_grads = [None] * layer_count
    for layer_idx in reversed(range(layer_count)):
        pieces = (
            norm_attn[layer_idx],
            w_query[layer_idx],
            w_key[layer_idx],
            w_value[layer_idx],
            w_out[layer_idx],
            norm_ffn[layer_idx],
            w_gate[layer_idx],
            w_up[layer_idx],
            w_down[layer_idx],
        )
        gathered = (
            lax.all_gather(pieces[0].astype(jnp.bfloat16), "frames", axis=1, tiled=True).astype(
                jnp.float32
            ),
            lax.all_gather(pieces[1], "frames", axis=1, tiled=True),
            lax.all_gather(pieces[2], "frames", axis=1, tiled=True),
            lax.all_gather(pieces[3], "frames", axis=1, tiled=True),
            lax.all_gather(pieces[4], "frames", axis=1, tiled=True),
            lax.all_gather(pieces[5].astype(jnp.bfloat16), "frames", axis=1, tiled=True).astype(
                jnp.float32
            ),
            lax.all_gather(pieces[6], "frames", axis=1, tiled=True),
            lax.all_gather(pieces[7], "frames", axis=1, tiled=True),
            lax.all_gather(pieces[8], "frames", axis=1, tiled=True),
        )
        weights = tuple((gathered_item[0] for gathered_item in gathered))
        gain_one, wq_l, wk_l, wv_l, wo_l, gain_two, wg_l, wu_l, wd_l = weights
        totals = [jnp.zeros(item.shape, jnp.float32) for item in weights]
        for micro_idx in range(MICRO):
            micro_grads = [None] * 9
            frame_rows = kept_inputs[layer_idx][micro_idx]
            full_kv = kept_kv[layer_idx][micro_idx]
            grad_out = upstream[micro_idx]
            normed = rms_scale(frame_rows, gain_one).astype(jnp.bfloat16)
            query_vec = project(normed, wq_l).astype(jnp.bfloat16)
            (
                query_f,
                key_all,
                values,
                mixed_out,
                middle,
                normed2,
                gate_act,
                up_act,
                hidden,
                result,
            ) = layer_rest(frame_rows, weights, query_vec, full_kv, section_idx)
            down_in = grad_out.astype(jnp.bfloat16)
            micro_grads[8] = left_product(hidden, down_in)
            hidden_grad = right_product(down_in, wd_l)
            _, pullback = jax.vjp(
                lambda gate_in, up_in: jax.nn.silu(gate_in) * up_in, gate_act, up_act
            )
            gate_grad, up_grad = pullback(hidden_grad)
            gate_grad = gate_grad.astype(jnp.bfloat16)
            up_grad = up_grad.astype(jnp.bfloat16)
            micro_grads[6] = left_product(normed2, gate_grad)
            micro_grads[7] = left_product(normed2, up_grad)
            normed2_grad = right_product(gate_grad, wg_l) + right_product(up_grad, wu_l)
            _, pullback = jax.vjp(rms_scale, middle, gain_two)
            middle_part, gain_two_part = pullback(normed2_grad)
            middle_grad = grad_out + middle_part
            micro_grads[5] = gain_two_part
            branch_in = middle_grad.astype(jnp.bfloat16)
            micro_grads[4] = left_product(mixed_out, branch_in)
            mixed_grad = right_product(branch_in, wo_l)
            _, pullback = jax.vjp(
                lambda query_in, key_in, value_in: attend(query_in, key_in, value_in, section_idx),
                query_f,
                key_all,
                values,
            )
            query_grad, key_grad, value_grad = pullback(
                mixed_grad.reshape(micro_rows, head_count, HEAD_DIM)
            )
            grad_kv = jnp.concatenate(
                [
                    key_grad.reshape(micro_rows, positions, model_width),
                    value_grad.reshape(micro_rows, positions, model_width),
                ],
                axis=-1,
            )
            own_grad = return_kv_grads(grad_kv, section_idx)
            query_low = query_grad.reshape(micro_rows, model_width).astype(jnp.bfloat16)
            key_low = own_grad[:, :model_width].astype(jnp.bfloat16)
            value_low = own_grad[:, model_width:].astype(jnp.bfloat16)
            micro_grads[1] = left_product(normed, query_low)
            micro_grads[2] = left_product(normed, key_low)
            micro_grads[3] = left_product(normed, value_low)
            normed_grad = (
                right_product(query_low, wq_l)
                + right_product(key_low, wk_l)
                + right_product(value_low, wv_l)
            )
            _, pullback = jax.vjp(rms_scale, frame_rows, gain_one)
            rows_part, gain_one_part = pullback(normed_grad)
            micro_grads[0] = gain_one_part
            upstream[micro_idx] = middle_grad + rows_part
            totals = [first + second for first, second in zip(totals, micro_grads)]
        layer_grads[layer_idx] = lax.psum_scatter(
            tuple((item[None] for item in totals)), "frames", scatter_dimension=1, tiled=True
        )
    input_grad = jnp.concatenate(upstream, axis=0)[:, None, :]
    stacked = tuple((jnp.stack([layer_grads[0][which]]) for which in range(9)))
    return (
        output,
        input_grad,
        stacked[0],
        stacked[1],
        stacked[2],
        stacked[3],
        stacked[4],
        stacked[5],
        stacked[6],
        stacked[7],
        stacked[8],
    )


def mega(Z, F, S, R, D, H, first, *refs):
    (
        x_ref, seg_ref, cot_ref, ga_ref, gb_ref,
        wq_ref, wk_ref, wv_ref, wo_ref, wg_ref, wu_ref, wd_ref,
        out_ref, ig_ref, gga_ref, ggb_ref, wdg_ref, wog_ref, cg_ref, gg_ref, ug_ref,
        NA, DI, N2, BR, WC, WO, WG, WU, WD, KV, QV, AT, MX,
        P1, P2, P3, P4, R1, R2, R3, R4, HID, GG, UG, KS, KR, OG, QG,
        CS, CR, CK, GS, GR, GK, US, UR, UK, OS, OR, DS, DR,
        GA, GB, PA, PB, QA, QB, ST, MID, GO, MG, ss, rs, ls,
    ) = refs
    C = D // Z
    QR = D // F
    HR = H // 2
    s = lax.axis_index("section")
    f = lax.axis_index("frames")
    z = f // 2
    x = f % 2
    fx = f + 1 - 2 * x
    mate = z + 1 - 2 * (z % 2)
    half = z // 2
    edge = z * (1 - half) + (Z - 1 - z) * half
    outer = edge == 0
    gate = edge == 1
    bf = jnp.bfloat16
    f32 = jnp.float32

    def order(i):
        near = i + edge * (1 - i // 2) * (1 - 2 * i)
        return half * (Z - 1) + (1 - 2 * half) * near

    def rows(i, n):
        if isinstance(i, int):
            return pl.ds(i * n, n)
        return pl.ds(pl.multiple_of(i * n, n), n)

    def remote(src, dst, sslot, rslot, dev):
        return pltpu.make_async_remote_copy(
            src_ref=src, dst_ref=dst, send_sem=ss.at[sslot], recv_sem=rs.at[rslot],
            device_id=dev, device_id_type=pl.DeviceIdType.MESH,
        )

    def arrive(dst, rslot):
        remote(dst, dst, 0, rslot, (s, fx)).wait_recv()

    def tdot(a, b):
        return lax.dot_general(a, b, (((0,), (0,)), ((), ())), preferred_element_type=f32)

    def dott(a, b):
        return lax.dot_general(a, b, (((1,), (1,)), ((), ())), preferred_element_type=f32)

    def dot(a, b):
        return jnp.dot(a, b, preferred_element_type=f32)

    def loop(n, body):
        def step(i, carry):
            body(i)
            return carry
        lax.fori_loop(0, n, step, 0)

    def ag_copy(buf, base, b, up):
        ref = buf.at[rows(b, R)]
        return remote(ref, ref, base + b + (0 if up else Z), base + b, (s, f + (2 if up else -2)))

    def ag_start(buf, base):
        @pl.when(z < Z - 1)
        def _():
            ag_copy(buf, base, z, True).start()

        @pl.when(z > 0)
        def _():
            ag_copy(buf, base, z, False).start()

    def ag_step(buf, base, b):
        @pl.when(b != z)
        def _():
            arrive(buf.at[rows(b, R)], base + b)

        @pl.when((b < z) & (z < Z - 1))
        def _():
            ag_copy(buf, base, b, True).start()

        @pl.when((b > z) & (z > 0))
        def _():
            ag_copy(buf, base, b, False).start()

    def ag_drain(buf, base):
        def body(b):
            @pl.when((b <= z) & (z < Z - 1))
            def _():
                ag_copy(buf, base, b, True).wait_send()

            @pl.when((b >= z) & (z > 0))
            def _():
                ag_copy(buf, base, b, False).wait_send()
        loop(Z, body)

    def rs_mate(P, Q, base):
        return remote(P.at[rows(mate, R)], Q.at[rows(0, R)], base, base, (s, 2 * mate + x))

    def rs_pre(P, Q, base, b):
        return remote(
            P.at[rows(b, R)], Q.at[rows(2 + b % 2, R)], base + 2 + b % 2, base + 2 + b % 2, (s, 2 * mate + x)
        )

    def rs_far(P, Q, base, b):
        return remote(P.at[rows(b, R)], Q.at[rows(1, R)], base + 4 + b % 2, base + 1, (s, 2 * b + x))

    def rs_send(P, Q, base, b):
        @pl.when(b == mate)
        def _():
            rs_mate(P, Q, base).start()

        @pl.when(outer & (b != mate) & (b != z))
        def _():
            rs_pre(P, Q, base, b).start()

    def rs_gate(P, Q, base):
        @pl.when(gate)
        def _():
            def body(i):
                b = order(i + 2)
                arrive(Q.at[rows(2 + b % 2, R)], base + 2 + b % 2)
                P[rows(b, R), :] = (
                    P[rows(b, R), :].astype(f32) + Q[rows(2 + b % 2, R), :].astype(f32)
                ).astype(bf)
                rs_far(P, Q, base, b).start()
            loop(2, body)

    def rs_wait(P, Q, base):
        arrive(Q.at[rows(0, R)], base)
        arrive(Q.at[rows(1, R)], base + 1)
        return (
            P[rows(z, R), :].astype(f32) + Q[rows(0, R), :].astype(f32) + Q[rows(1, R), :].astype(f32)
        )

    def rs_drain(P, Q, base):
        rs_mate(P, Q, base).wait_send()

        def body(i):
            b = order(i + 2)

            @pl.when(outer)
            def _():
                rs_pre(P, Q, base, b).wait_send()

            @pl.when(gate)
            def _():
                rs_far(P, Q, base, b).wait_send()
        loop(2, body)

    def col_copy(w, buf, base, a, width, k):
        to = (z + k) % Z
        cols = pl.ds(pl.multiple_of(to * width, width), width)
        return remote(
            w.at[:, cols], buf.at[rows(f, QR), pl.ds(a * width, width)],
            base + a * Z + k, base + a * Z + k, (s, 2 * to + x),
        )

    def own_copy(w, buf, slot, a, width):
        cols = pl.ds(pl.multiple_of(z * width, width), width)
        return pltpu.make_async_copy(w.at[:, cols], buf.at[rows(f, QR), pl.ds(a * width, width)], ls.at[slot])

    def side_copy(buf, base, line):
        ref = buf.at[rows(2 * line + x, QR)]
        return remote(ref, ref, base + line, base + line, (s, fx))

    def col_arrive(buf, base, count, width, k):
        line = (z + Z - k) % Z
        for a in range(count):
            arrive(buf.at[rows(2 * line + x, QR), pl.ds(a * width, width)], base + a * Z + k)
        return line

    def side_arrive(buf, base):
        loop(Z, lambda line: arrive(buf.at[rows(2 * line + 1 - x, QR)], base + line))

    def pair_copy(S_, Q_, base, line):
        return remote(S_.at[rows(line, QR)], Q_.at[rows(line, QR)], base + line, base + line, (s, fx))

    def home_copy(K_, o_ref, base, line):
        return remote(K_.at[rows(line, QR)], o_ref.at[z], base + line, base + z, (s, 2 * line + x))

    def grad_make(left, right, K_, S_, Q_, base):
        def body(line):
            both = tdot(left[:, pl.ds(pl.multiple_of(line * 2 * QR, 2 * QR), 2 * QR)], right[...]).astype(bf)
            K_[rows(line, QR), :] = jnp.where(x == 0, both[:QR], both[QR:])
            S_[rows(line, QR), :] = jnp.where(x == 0, both[QR:], both[:QR])
            pair_copy(S_, Q_, base, line).start()
        loop(Z, body)

    def grad_home(K_, Q_, o_ref, pbase, hbase, slot):
        def body(i):
            line = (z + 1 + i) % Z
            arrive(Q_.at[rows(line, QR)], pbase + line)
            K_[rows(line, QR), :] = (
                K_[rows(line, QR), :].astype(f32) + Q_[rows(line, QR), :].astype(f32)
            ).astype(bf)

            @pl.when(line != z)
            def _():
                home_copy(K_, o_ref, hbase, line).start()

            @pl.when(line == z)
            def _():
                pltpu.make_async_copy(K_.at[rows(line, QR)], o_ref.at[z], ls.at[slot]).start()
        loop(Z, body)

    def grad_drain(S_, K_, Q_, o_ref, pbase, hbase, slot):
        def body(line):
            pair_copy(S_, Q_, pbase, line).wait_send()

            @pl.when(line != z)
            def _():
                home_copy(K_, o_ref, hbase, line).wait_send()
                arrive(o_ref.at[line], hbase + line)
        loop(Z, body)
        pltpu.make_async_copy(K_.at[rows(z, QR)], o_ref.at[z], ls.at[slot]).wait()

    def gain_copy(src, buf, base, k, sliced):
        to = (f + k) % F
        return remote(src.at[to] if sliced else src, buf.at[f], base + k, base + k, (s, to))

    def gain_arrive(buf, base):
        for k in range(1, F):
            arrive(buf.at[(f + F - k) % F], base + k)

    def row_of(buf):
        return jnp.concatenate([buf[k] for k in range(F)], axis=-1)

    def kv_copy(b, t):
        ref = KV.at[s * Z + b]
        return remote(ref, ref, first["kv"] + t * Z + b, first["kv"] + s * Z + b, (t, f))

    def kg_copy(b, j):
        return remote(
            KS.at[j * Z + b], KR.at[s * Z + b], first["kg"] + j * Z + b, first["kg"] + s * Z + b, (j, f)
        )

    for j in range(1, S):
        @pl.when(j > s)
        def _(j=j):
            KV[pl.ds(j * Z, Z)] = jnp.zeros((Z, R, 2 * C), bf)

    barrier = pltpu.get_barrier_semaphore()
    for k in range(1, F):
        pl.semaphore_signal(
            barrier, inc=1, device_id=(s, (f + k) % F), device_id_type=pl.DeviceIdType.MESH
        )
    for k in range(1, S):
        pl.semaphore_signal(
            barrier, inc=1, device_id=((s + k) % S, f), device_id_type=pl.DeviceIdType.MESH
        )
    GA[f] = ga_ref[...]
    GB[f] = gb_ref[...]
    pl.semaphore_wait(barrier, F + S - 2)

    for k in range(1, F):
        gain_copy(ga_ref, GA, first["ga"], k, False).start()
    qkv = (wq_ref, wk_ref, wv_ref)
    for k in range(1, Z):
        for a in range(3):
            col_copy(qkv[a], WC, first["wc"], a, C, k).start()
    for a in range(3):
        own_copy(qkv[a], WC, a, a, C).start()
    for k in range(1, F):
        gain_copy(gb_ref, GB, first["gb"], k, False).start()
    ST[...] = x_ref[...].astype(f32)
    mask = (seg_ref[...] != 0).astype(f32)
    GO[...] = cot_ref[...].astype(f32) * mask
    DI[rows(z, R), :] = GO[...].astype(bf)
    for a in range(3):
        own_copy(qkv[a], WC, a, a, C).wait()
    side_copy(WC, first["wcx"], z).start()
    gain_arrive(GA, first["ga"])
    stream = ST[...]
    inverse = lax.rsqrt(jnp.mean(stream * stream, axis=-1, keepdims=True) + epsilon)
    NA[rows(z, R), :] = (stream * inverse * row_of(GA)).astype(bf)
    ag_start(NA, first["na"])
    for k in range(1, Z):
        line = col_arrive(WC, first["wc"], 3, C, k)
        side_copy(WC, first["wcx"], line).start()
    wo_own = pltpu.make_async_copy(wo_ref, WO.at[rows(x, QR)], ls.at[3])
    wo_own.start()
    wo_side = remote(wo_ref, WO.at[rows(x, QR)], first["wo"], first["wo"], (s, fx))
    wo_side.start()
    wd_own = pltpu.make_async_copy(wd_ref, WD.at[rows(x, HR)], ls.at[4])
    wd_own.start()
    own_copy(wg_ref, WG, 5, 0, H).start()
    own_copy(wu_ref, WU, 6, 0, H).start()
    side_arrive(WC, first["wcx"])

    def block_qkv(i):
        b = order(i)
        ag_step(NA, first["na"], b)
        both = dot(NA[rows(b, R), :], WC[...]).astype(bf)
        QV[rows(b, R), :] = both[:, :C]
        KV[s * Z + b] = both[:, C:]
        for t in range(1, S):
            @pl.when(t > s)
            def _(t=t):
                kv_copy(b, t).start()
    loop(Z, block_qkv)

    for k in range(1, Z):
        col_copy(wg_ref, WG, first["wg"], 0, H, k).start()
    own_copy(wg_ref, WG, 5, 0, H).wait()
    side_copy(WG, first["wgx"], z).start()
    for k in range(1, Z):
        col_copy(wu_ref, WU, first["wu"], 0, H, k).start()
    own_copy(wu_ref, WU, 6, 0, H).wait()
    side_copy(WU, first["wux"], z).start()
    wd_side = remote(wd_ref, WD.at[rows(x, HR)], first["wd"], first["wd"], (s, fx))
    wd_side.start()
    ag_start(DI, first["di"])
    wo_own.wait()
    arrive(WO.at[rows(1 - x, QR)], first["wo"])

    groups = lax.broadcasted_iota(jnp.int32, (C, C), 0) // HEAD_DIM
    ones = (groups == lax.broadcasted_iota(jnp.int32, (C, C), 1) // HEAD_DIM).astype(f32).astype(bf)

    def head_sum(product):
        high = product.astype(bf)
        rest = (product - high.astype(f32)).astype(bf)
        return dot(high, ones) + dot(rest, ones)

    def block_attend(i):
        b = order(i)
        ag_step(DI, first["di"], b)
        for j in range(S - 1):
            @pl.when(j < s)
            def _(j=j):
                arrive(KV.at[j * Z + b], first["kv"] + j * Z + b)
        query = QV[rows(b, R), :].astype(f32)
        scores = []
        for j in range(S):
            score = head_sum(query * KV[j * Z + b, :, :C].astype(f32)) * HEAD_DIM ** (-0.5)
            scores.append(jnp.where(j <= s, score, -1e30))
        largest = functools.reduce(jnp.maximum, scores)
        expo = [jnp.exp(score - largest) for score in scores]
        total = functools.reduce(lambda u, v: u + v, expo)
        mixed = jnp.zeros((R, C), f32)
        for j in range(S):
            attn = expo[j] / total
            AT[j * Z + b] = attn
            mixed = mixed + attn * KV[j * Z + b, :, C:].astype(f32)
        mixed = mixed.astype(bf)
        MX[rows(b, R), :] = mixed
        P1[rows(b, R), :] = dot(mixed, WO[...]).astype(bf)
        rs_send(P1, R1, first["r1"], b)
    loop(Z, block_attend)
    rs_gate(P1, R1, first["r1"])
    for k in range(1, Z):
        line = col_arrive(WG, first["wg"], 1, H, k)
        side_copy(WG, first["wgx"], line).start()
    for k in range(1, Z):
        line = col_arrive(WU, first["wu"], 1, H, k)
        side_copy(WU, first["wux"], line).start()
    middle = ST[...] + rs_wait(P1, R1, first["r1"])
    MID[...] = middle
    gain_arrive(GB, first["gb"])
    inverse = lax.rsqrt(jnp.mean(middle * middle, axis=-1, keepdims=True) + epsilon)
    N2[rows(z, R), :] = (middle * inverse * row_of(GB)).astype(bf)
    ag_start(N2, first["n2"])
    side_arrive(WG, first["wgx"])
    side_arrive(WU, first["wux"])
    wd_own.wait()
    arrive(WD.at[rows(1 - x, HR)], first["wd"])

    def block_ffn(i):
        b = order(i)
        ag_step(N2, first["n2"], b)
        normed2 = N2[rows(b, R), :]
        gate_act = dot(normed2, WG[...])
        sig = 1.0 / (1.0 + jnp.exp(-gate_act))
        silu = gate_act * sig
        up_act = dot(normed2, WU[...])
        HID[rows(b, R), :] = (silu * up_act).astype(bf)
        hidden_grad = dott(DI[rows(b, R), :], WD[...])
        gate_grad = (hidden_grad * up_act * (sig * (1.0 + gate_act * (1.0 - sig)))).astype(bf)
        up_grad = (hidden_grad * silu).astype(bf)
        GG[rows(b, R), :] = gate_grad
        UG[rows(b, R), :] = up_grad
        P2[rows(b, R), :] = (dott(gate_grad, WG[...]) + dott(up_grad, WU[...])).astype(bf)
        rs_send(P2, R2, first["r2"], b)
    loop(Z, block_ffn)
    rs_gate(P2, R2, first["r2"])

    grad_make(N2, GG, GK, GS, GR, first["gx"])
    grad_make(N2, UG, UK, US, UR, first["ux"])

    def block_down(i):
        b = order(i)
        P3[rows(b, R), :] = dot(HID[rows(b, R), :], WD[...]).astype(bf)
        rs_send(P3, R3, first["r3"], b)
    loop(Z, block_down)

    middle = MID[...]
    inverse = lax.rsqrt(jnp.mean(middle * middle, axis=-1, keepdims=True) + epsilon)
    unit = middle * inverse
    normed_grad = rs_wait(P2, R2, first["r2"])
    scaled = normed_grad * row_of(GB)
    middle_grad = GO[...] + (scaled - unit * jnp.mean(scaled * unit, axis=-1, keepdims=True)) * inverse
    MG[...] = middle_grad
    BR[rows(z, R), :] = middle_grad.astype(bf)
    ag_start(BR, first["br"])
    part = jnp.sum(normed_grad * unit, axis=0, keepdims=True)
    for k in range(F):
        PB[k] = part[:, k * QR : (k + 1) * QR]
    for k in range(1, F):
        gain_copy(PB, QB, first["qb"], k, True).start()
    rs_gate(P3, R3, first["r3"])
    pair = 2 * Z
    down_out = remote(DS, DR, first["dx"], first["dx"], (s, fx))

    def down_make(i):
        n = HR // 2
        mine = pl.ds(pl.multiple_of(x * HR + i * n, n), n)
        other = pl.ds(pl.multiple_of((1 - x) * HR + i * n, n), n)
        DS[rows(i, n), :] = tdot(HID[:, other], DI[...]).astype(bf)
        wdg_ref[rows(i, n), :] = tdot(HID[:, mine], DI[...])
    loop(2, down_make)
    down_out.start()
    grad_home(GK, GR, gg_ref, first["gx"], first["gh"], 7)

    def block_back(i):
        b = order(i)
        ag_step(BR, first["br"], b)
        mixed_grad = dott(BR[rows(b, R), :], WO[...])
        query = QV[rows(b, R), :].astype(f32)
        inner = []
        total = jnp.zeros((R, C), f32)
        for j in range(S):
            one = head_sum(mixed_grad * KV[j * Z + b, :, C:].astype(f32))
            inner.append(one)
            total = total + AT[j * Z + b] * one
        query_grad = jnp.zeros((R, C), f32)
        for j in range(S):
            attn = AT[j * Z + b]
            score_grad = attn * (inner[j] - total) * HEAD_DIM ** (-0.5)
            query_grad = query_grad + score_grad * KV[j * Z + b, :, :C].astype(f32)
            key_part = score_grad * query
            value_part = attn * mixed_grad

            @pl.when(j == s)
            def _(key_part=key_part, value_part=value_part):
                OG[b, :, :C] = key_part
                OG[b, :, C:] = value_part

            @pl.when(j < s)
            def _(j=j, key_part=key_part, value_part=value_part):
                KS[j * Z + b, :, :C] = key_part.astype(bf)
                KS[j * Z + b, :, C:] = value_part.astype(bf)
                kg_copy(b, j).start()
        QG[rows(b, R), :C] = query_grad.astype(bf)
    loop(Z, block_back)

    def block_normed(i):
        b = order(i)
        for j in range(1, S):
            @pl.when(j > s)
            def _(j=j):
                arrive(KR.at[j * Z + b], first["kg"] + j * Z + b)
                OG[b] = OG[b] + KR[j * Z + b].astype(f32)
        QG[rows(b, R), C:] = OG[b].astype(bf)
        P4[rows(b, R), :] = dott(QG[rows(b, R), :], WC[...]).astype(bf)
        rs_send(P4, R4, first["r4"], b)
    loop(Z, block_normed)
    grad_make(NA, QG, CK, CS, CR, first["cx"])
    rs_gate(P4, R4, first["r4"])
    grad_home(CK, CR, cg_ref, first["cx"], first["ch"], 9)
    grad_home(UK, UR, ug_ref, first["ux"], first["uh"], 8)

    both = tdot(MX[...], BR[...])
    wog_ref[...] = jnp.where(x == 0, both[:QR], both[QR:])
    OS[...] = jnp.where(x == 0, both[QR:], both[:QR]).astype(bf)
    out_out = remote(OS, OR, first["ox"], first["ox"], (s, fx))
    out_out.start()
    out_ref[...] = (MID[...] + rs_wait(P3, R3, first["r3"])).astype(bf)
    arrive(DR, first["dx"])
    wdg_ref[...] = wdg_ref[...] + DR[...].astype(f32)

    stream = ST[...]
    inverse = lax.rsqrt(jnp.mean(stream * stream, axis=-1, keepdims=True) + epsilon)
    unit = stream * inverse
    normed_grad = rs_wait(P4, R4, first["r4"])
    part = jnp.sum(normed_grad * unit, axis=0, keepdims=True)
    for k in range(F):
        PA[k] = part[:, k * QR : (k + 1) * QR]
    for k in range(1, F):
        gain_copy(PA, QA, first["qa"], k, True).start()
    scaled = normed_grad * row_of(GA)
    ig_ref[...] = MG[...] + (scaled - unit * jnp.mean(scaled * unit, axis=-1, keepdims=True)) * inverse
    QA[f] = PA[f]
    QB[f] = PB[f]
    arrive(OR, first["ox"])
    wog_ref[...] = wog_ref[...] + OR[...].astype(f32)
    gain_arrive(QB, first["qb"])
    gain_arrive(QA, first["qa"])
    gga_ref[...] = functools.reduce(lambda u, v: u + v, [QA[k] for k in range(F)])
    ggb_ref[...] = functools.reduce(lambda u, v: u + v, [QB[k] for k in range(F)])

    for k in range(1, F):
        gain_copy(ga_ref, GA, first["ga"], k, False).wait_send()
        gain_copy(gb_ref, GB, first["gb"], k, False).wait_send()
        gain_copy(PA, QA, first["qa"], k, True).wait_send()
        gain_copy(PB, QB, first["qb"], k, True).wait_send()
    for k in range(1, Z):
        for a in range(3):
            col_copy(qkv[a], WC, first["wc"], a, C, k).wait_send()
        col_copy(wg_ref, WG, first["wg"], 0, H, k).wait_send()
        col_copy(wu_ref, WU, first["wu"], 0, H, k).wait_send()

    def sides(line):
        side_copy(WC, first["wcx"], line).wait_send()
        side_copy(WG, first["wgx"], line).wait_send()
        side_copy(WU, first["wux"], line).wait_send()
    loop(Z, sides)
    wo_side.wait_send()
    wd_side.wait_send()
    down_out.wait_send()
    out_out.wait_send()
    ag_drain(NA, first["na"])
    ag_drain(DI, first["di"])
    ag_drain(N2, first["n2"])
    ag_drain(BR, first["br"])
    rs_drain(P1, R1, first["r1"])
    rs_drain(P2, R2, first["r2"])
    rs_drain(P3, R3, first["r3"])
    rs_drain(P4, R4, first["r4"])

    def across(b):
        for t in range(S):
            @pl.when(t > s)
            def _(t=t):
                kv_copy(b, t).wait_send()

            @pl.when(t < s)
            def _(t=t):
                kg_copy(b, t).wait_send()
    loop(Z, across)
    grad_drain(GS, GK, GR, gg_ref, first["gx"], first["gh"], 7)
    grad_drain(US, UK, UR, ug_ref, first["ux"], first["uh"], 8)
    grad_drain(CS, CK, CR, cg_ref, first["cx"], first["ch"], 9)


def line_plan(
    frames_in, segment_ids, cotangent, norm_attn, w_query, w_key, w_value, w_out, norm_ffn, w_gate, w_up, w_down
):
    R, _, D = frames_in.shape
    F = lax.axis_size("frames")
    S = lax.axis_size("section")
    Z = F // 2
    C = D // Z
    H = w_gate.shape[3] // Z
    QR = D // F
    HR = H // 2
    counts = dict(
        ga=F, gb=F, qa=F, qb=F, wc=3 * Z, wcx=Z, wg=Z, wgx=Z, wu=Z, wux=Z, wo=1, wd=1,
        na=2 * Z, di=2 * Z, n2=2 * Z, br=2 * Z, r1=6, r2=6, r3=6, r4=6,
        kv=S * Z, kg=S * Z, gx=Z, gh=Z, ux=Z, uh=Z, cx=Z, ch=Z, ox=1, dx=1,
    )
    first, slots = {}, 0
    for name, count in counts.items():
        first[name] = slots
        slots += count
    bf, f32 = jnp.bfloat16, jnp.float32
    V = pltpu.VMEM
    scratch = [
        V((Z * R, D), bf), V((Z * R, D), bf), V((Z * R, D), bf), V((Z * R, D), bf),
        V((D, 3 * C), bf), V((2 * QR, D), bf), V((D, H), bf), V((D, H), bf), V((2 * HR, D), bf),
        V((S * Z, R, 2 * C), bf), V((Z * R, C), bf), V((S * Z, R, C), f32), V((Z * R, C), bf),
        V((Z * R, D), bf), V((Z * R, D), bf), V((Z * R, D), bf), V((Z * R, D), bf),
        V((4 * R, D), bf), V((4 * R, D), bf), V((4 * R, D), bf), V((4 * R, D), bf),
        V((Z * R, H), bf), V((Z * R, H), bf), V((Z * R, H), bf),
        V((S * Z, R, 2 * C), bf), V((S * Z, R, 2 * C), bf), V((Z, R, 2 * C), f32), V((Z * R, 3 * C), bf),
        V((Z * QR, 3 * C), bf), V((Z * QR, 3 * C), bf), V((Z * QR, 3 * C), bf),
        V((Z * QR, H), bf), V((Z * QR, H), bf), V((Z * QR, H), bf),
        V((Z * QR, H), bf), V((Z * QR, H), bf), V((Z * QR, H), bf),
        V((QR, D), bf), V((QR, D), bf), V((HR, D), bf), V((HR, D), bf),
        V((F, 1, QR), f32), V((F, 1, QR), f32), V((F, 1, QR), f32), V((F, 1, QR), f32),
        V((F, 1, QR), f32), V((F, 1, QR), f32),
        V((R, D), f32), V((R, D), f32), V((R, D), f32), V((R, D), f32),
        pltpu.SemaphoreType.DMA((slots,)), pltpu.SemaphoreType.DMA((slots,)), pltpu.SemaphoreType.DMA((10,)),
    ]
    vmem = pl.BlockSpec(memory_space=pltpu.VMEM)
    anyw = pl.BlockSpec(memory_space=pl.ANY)
    shape = jax.ShapeDtypeStruct
    results = pl.pallas_call(
        functools.partial(mega, Z, F, S, R, D, H, first),
        out_shape=(
            shape((R, D), bf), shape((R, D), f32), shape((1, QR), f32), shape((1, QR), f32),
            shape((HR, D), f32), shape((QR, D), f32),
            shape((Z, QR, 3 * C), bf), shape((Z, QR, H), bf), shape((Z, QR, H), bf),
        ),
        in_specs=[vmem] * 5 + [anyw] * 7,
        out_specs=(vmem,) * 6 + (anyw,) * 3,
        scratch_shapes=scratch,
        compiler_params=pltpu.CompilerParams(
            collective_id=0, has_side_effects=True, vmem_limit_bytes=VMEM_LIMIT
        ),
        name="layer",
    )(
        frames_in[:, 0, :], segment_ids[:, None], cotangent[:, 0, :], norm_attn[0], norm_ffn[0],
        w_query[0, 0], w_key[0, 0], w_value[0, 0], w_out[0, 0], w_gate[0, 0], w_up[0, 0], w_down[0, 0],
    )
    output, input_grad, gain_one, gain_two, down, out, cols, gate, up = results
    cols = cols.reshape(Z, QR, 3, C).transpose(2, 1, 0, 3).reshape(3, QR, D).astype(f32)

    def joined(item):
        return item.transpose(1, 0, 2).reshape(1, 1, QR, Z * H).astype(f32)

    return (
        output[:, None, :], input_grad[:, None, :], gain_one[None],
        cols[0][None, None], cols[1][None, None], cols[2][None, None], out[None, None], gain_two[None],
        joined(gate), joined(up), down[None, None],
    )


def solution(mesh):
    placed = (
        P("frames", "section", None),
        P("frames"),
        P("frames", "section", None),
        P(None, "section", "frames"),
        P(None, "section", "frames", None),
        P(None, "section", "frames", None),
        P(None, "section", "frames", None),
        P(None, "section", "frames", None),
        P(None, "section", "frames"),
        P(None, "section", "frames", None),
        P(None, "section", "frames", None),
        P(None, "section", "frames", None),
    )
    lines = mesh.shape["frames"] == 8 and mesh.shape["section"] == 4

    def per_device(*arrays):
        width = arrays[0].shape[2]
        fits = lines and arrays[4].shape[0] == 1 and arrays[0].shape[1] == 1 and width % 1024 == 0
        return line_plan(*arrays) if fits else gather_plan(*arrays)

    return jax.shard_map(
        per_device,
        mesh=mesh,
        in_specs=placed,
        out_specs=(
            P("frames", "section", None),
            P("frames", "section", None),
            P(None, "section", "frames"),
            P(None, "section", "frames", None),
            P(None, "section", "frames", None),
            P(None, "section", "frames", None),
            P(None, "section", "frames", None),
            P(None, "section", "frames"),
            P(None, "section", "frames", None),
            P(None, "section", "frames", None),
            P(None, "section", "frames", None),
        ),
        check_vma=False,
    )
```

```python
import functools

import jax
import jax.numpy as jnp
from jax import lax
from jax.experimental import pallas as pl
from jax.experimental.pallas import tpu as pltpu
from jax.sharding import PartitionSpec as P

HEAD_DIM = 64
MICRO = 2
VMEM_LIMIT = 63 * 1024 * 1024


epsilon = 1e-05


def carried_in(shard, axis, combine, identity):
    devices, place = (lax.axis_size(axis), lax.axis_index(axis))
    everything = lax.all_gather(shard, axis)
    start = jnp.broadcast_to(jnp.asarray(identity, shard.dtype), shard.shape)

    def hop(k, before):
        reached = k < place
        new = combine(before, everything[k])
        return jnp.where(reached, new, before)

    return lax.fori_loop(0, devices, hop, start)


def carried_in_2(shard, axis, combine, identity):
    devices, place = (lax.axis_size(axis), lax.axis_index(axis))
    everything = lax.all_gather(shard.astype(jnp.bfloat16), axis)
    start = jnp.broadcast_to(jnp.asarray(identity, shard.dtype), shard.shape)

    def hop(k, before):
        at = devices - 1 - k
        reached = at > place
        new = combine(before, everything[at].astype(shard.dtype))
        return jnp.where(reached, new, before)

    return lax.fori_loop(0, devices, hop, start)


def rms_scale(values, gain):
    return values * lax.rsqrt(jnp.mean(values * values, axis=-1, keepdims=True) + epsilon) * gain


def project(left, weight):
    return jnp.dot(left, weight, preferred_element_type=jnp.float32)


def left_product(left, right):
    return lax.dot_general(
        left, right, (((0,), (0,)), ((), ())), preferred_element_type=jnp.float32
    )


def right_product(left, weight):
    return lax.dot_general(
        left, weight, (((1,), (1,)), ((), ())), preferred_element_type=jnp.float32
    )


def add_pair(first_part, second_part):
    return first_part + second_part


def attend(query_vec, key_all, values, section_idx):
    scores = jnp.einsum(
        "mhe,mphe->mhp", query_vec, key_all, precision=lax.Precision.HIGHEST
    ) * HEAD_DIM ** (-0.5)
    allowed = jnp.arange(key_all.shape[1]) <= section_idx
    scores = jnp.where(allowed, scores, -1e30)
    largest = jnp.max(scores, axis=-1, keepdims=True)
    expo_terms = jnp.exp(scores - largest)
    weights = expo_terms / jnp.sum(expo_terms, axis=-1, keepdims=True)
    return jnp.einsum("mhp,mphe->mhe", weights, values, precision=lax.Precision.HIGHEST)


def share_kv(own_kv, slot_mask):
    placed = jnp.where(slot_mask[None, :, None], own_kv[:, None, :], jnp.zeros((), jnp.bfloat16))
    earlier = carried_in(placed, "section", add_pair, jnp.zeros_like(placed))
    return earlier + placed


def return_kv_grads(grad_kv, section_idx):
    later_sum = carried_in_2(grad_kv, "section", add_pair, jnp.zeros_like(grad_kv))
    return lax.dynamic_index_in_dim(later_sum + grad_kv, section_idx, 1, keepdims=False)


def layer_rest(frame_rows, weights, query_vec, full_kv, section_idx):
    gain_one, wq_l, wk_l, wv_l, wo_l, gain_two, wg_l, wu_l, wd_l = weights
    packed_row_count = frame_rows.shape[0]
    model_width = frame_rows.shape[1]
    head_count = model_width // HEAD_DIM
    positions = full_kv.shape[1]
    key_all = (
        full_kv[:, :, :model_width]
        .astype(jnp.float32)
        .reshape(packed_row_count, positions, head_count, HEAD_DIM)
    )
    values = (
        full_kv[:, :, model_width:]
        .astype(jnp.float32)
        .reshape(packed_row_count, positions, head_count, HEAD_DIM)
    )
    query_f = query_vec.astype(jnp.float32).reshape(packed_row_count, head_count, HEAD_DIM)
    mixed_out = (
        attend(query_f, key_all, values, section_idx)
        .reshape(packed_row_count, model_width)
        .astype(jnp.bfloat16)
    )
    middle = frame_rows + project(mixed_out, wo_l)
    normed2 = rms_scale(middle, gain_two).astype(jnp.bfloat16)
    gate_act = project(normed2, wg_l)
    up_act = project(normed2, wu_l)
    hidden = (jax.nn.silu(gate_act) * up_act).astype(jnp.bfloat16)
    result = middle + project(hidden, wd_l)
    return (query_f, key_all, values, mixed_out, middle, normed2, gate_act, up_act, hidden, result)


def gather_plan(
    frames_in,
    segment_ids,
    cotangent,
    norm_attn,
    w_query,
    w_key,
    w_value,
    w_out,
    norm_ffn,
    w_gate,
    w_up,
    w_down,
):
    section_idx = lax.axis_index("section")
    frame_count = frames_in.shape[0]
    model_width = frames_in.shape[2]
    head_count = model_width // HEAD_DIM
    micro_rows = frame_count // MICRO
    positions = lax.axis_size("section") * frames_in.shape[1]
    layer_count = w_query.shape[0]
    slot_mask = jnp.arange(positions) == section_idx
    stream = frames_in[:, 0, :].astype(jnp.float32)
    layer_idx = 0
    pieces = (
        norm_attn[layer_idx],
        w_query[layer_idx],
        w_key[layer_idx],
        w_value[layer_idx],
        w_out[layer_idx],
        norm_ffn[layer_idx],
        w_gate[layer_idx],
        w_up[layer_idx],
        w_down[layer_idx],
    )
    gathered = (
        lax.all_gather(pieces[0].astype(jnp.bfloat16), "frames", axis=1, tiled=True).astype(
            jnp.float32
        ),
        lax.all_gather(pieces[1], "frames", axis=1, tiled=True),
        lax.all_gather(pieces[2], "frames", axis=1, tiled=True),
        lax.all_gather(pieces[3], "frames", axis=1, tiled=True),
        lax.all_gather(pieces[4], "frames", axis=1, tiled=True),
        lax.all_gather(pieces[5].astype(jnp.bfloat16), "frames", axis=1, tiled=True).astype(
            jnp.float32
        ),
        lax.all_gather(pieces[6], "frames", axis=1, tiled=True),
        lax.all_gather(pieces[7], "frames", axis=1, tiled=True),
        lax.all_gather(pieces[8], "frames", axis=1, tiled=True),
    )
    weights = tuple((gathered_item[0] for gathered_item in gathered))
    layer_inputs = []
    layer_kv = []
    results = []
    for micro_idx in range(MICRO):
        frame_rows = stream[micro_idx * micro_rows : (micro_idx + 1) * micro_rows]
        normed = rms_scale(frame_rows, weights[0]).astype(jnp.bfloat16)
        query_vec = project(normed, weights[1]).astype(jnp.bfloat16)
        own_kv = jnp.concatenate(
            [
                project(normed, weights[2]).astype(jnp.bfloat16),
                project(normed, weights[3]).astype(jnp.bfloat16),
            ],
            axis=-1,
        )
        full_kv = share_kv(own_kv, slot_mask)
        outcome = layer_rest(frame_rows, weights, query_vec, full_kv, section_idx)
        layer_inputs.append(frame_rows)
        layer_kv.append(full_kv)
        results.append(outcome[-1])
    kept_inputs = [layer_inputs]
    kept_kv = [layer_kv]
    stream = jnp.concatenate(results, axis=0)
    output = stream.astype(jnp.bfloat16)[:, None, :]
    frame_mask = (segment_ids != 0).astype(jnp.float32)[:, None]
    upstream_all = cotangent[:, 0, :].astype(jnp.float32) * frame_mask
    upstream = [
        upstream_all[micro_idx * micro_rows : (micro_idx + 1) * micro_rows]
        for micro_idx in range(MICRO)
    ]
    layer_grads = [None] * layer_count
    for layer_idx in reversed(range(layer_count)):
        pieces = (
            norm_attn[layer_idx],
            w_query[layer_idx],
            w_key[layer_idx],
            w_value[layer_idx],
            w_out[layer_idx],
            norm_ffn[layer_idx],
            w_gate[layer_idx],
            w_up[layer_idx],
            w_down[layer_idx],
        )
        gathered = (
            lax.all_gather(pieces[0].astype(jnp.bfloat16), "frames", axis=1, tiled=True).astype(
                jnp.float32
            ),
            lax.all_gather(pieces[1], "frames", axis=1, tiled=True),
            lax.all_gather(pieces[2], "frames", axis=1, tiled=True),
            lax.all_gather(pieces[3], "frames", axis=1, tiled=True),
            lax.all_gather(pieces[4], "frames", axis=1, tiled=True),
            lax.all_gather(pieces[5].astype(jnp.bfloat16), "frames", axis=1, tiled=True).astype(
                jnp.float32
            ),
            lax.all_gather(pieces[6], "frames", axis=1, tiled=True),
            lax.all_gather(pieces[7], "frames", axis=1, tiled=True),
            lax.all_gather(pieces[8], "frames", axis=1, tiled=True),
        )
        weights = tuple((gathered_item[0] for gathered_item in gathered))
        gain_one, wq_l, wk_l, wv_l, wo_l, gain_two, wg_l, wu_l, wd_l = weights
        totals = [jnp.zeros(item.shape, jnp.float32) for item in weights]
        for micro_idx in range(MICRO):
            micro_grads = [None] * 9
            frame_rows = kept_inputs[layer_idx][micro_idx]
            full_kv = kept_kv[layer_idx][micro_idx]
            grad_out = upstream[micro_idx]
            normed = rms_scale(frame_rows, gain_one).astype(jnp.bfloat16)
            query_vec = project(normed, wq_l).astype(jnp.bfloat16)
            (
                query_f,
                key_all,
                values,
                mixed_out,
                middle,
                normed2,
                gate_act,
                up_act,
                hidden,
                result,
            ) = layer_rest(frame_rows, weights, query_vec, full_kv, section_idx)
            down_in = grad_out.astype(jnp.bfloat16)
            micro_grads[8] = left_product(hidden, down_in)
            hidden_grad = right_product(down_in, wd_l)
            _, pullback = jax.vjp(
                lambda gate_in, up_in: jax.nn.silu(gate_in) * up_in, gate_act, up_act
            )
            gate_grad, up_grad = pullback(hidden_grad)
            gate_grad = gate_grad.astype(jnp.bfloat16)
            up_grad = up_grad.astype(jnp.bfloat16)
            micro_grads[6] = left_product(normed2, gate_grad)
            micro_grads[7] = left_product(normed2, up_grad)
            normed2_grad = right_product(gate_grad, wg_l) + right_product(up_grad, wu_l)
            _, pullback = jax.vjp(rms_scale, middle, gain_two)
            middle_part, gain_two_part = pullback(normed2_grad)
            middle_grad = grad_out + middle_part
            micro_grads[5] = gain_two_part
            branch_in = middle_grad.astype(jnp.bfloat16)
            micro_grads[4] = left_product(mixed_out, branch_in)
            mixed_grad = right_product(branch_in, wo_l)
            _, pullback = jax.vjp(
                lambda query_in, key_in, value_in: attend(query_in, key_in, value_in, section_idx),
                query_f,
                key_all,
                values,
            )
            query_grad, key_grad, value_grad = pullback(
                mixed_grad.reshape(micro_rows, head_count, HEAD_DIM)
            )
            grad_kv = jnp.concatenate(
                [
                    key_grad.reshape(micro_rows, positions, model_width),
                    value_grad.reshape(micro_rows, positions, model_width),
                ],
                axis=-1,
            )
            own_grad = return_kv_grads(grad_kv, section_idx)
            query_low = query_grad.reshape(micro_rows, model_width).astype(jnp.bfloat16)
            key_low = own_grad[:, :model_width].astype(jnp.bfloat16)
            value_low = own_grad[:, model_width:].astype(jnp.bfloat16)
            micro_grads[1] = left_product(normed, query_low)
            micro_grads[2] = left_product(normed, key_low)
            micro_grads[3] = left_product(normed, value_low)
            normed_grad = (
                right_product(query_low, wq_l)
                + right_product(key_low, wk_l)
                + right_product(value_low, wv_l)
            )
            _, pullback = jax.vjp(rms_scale, frame_rows, gain_one)
            rows_part, gain_one_part = pullback(normed_grad)
            micro_grads[0] = gain_one_part
            upstream[micro_idx] = middle_grad + rows_part
            totals = [first + second for first, second in zip(totals, micro_grads)]
        layer_grads[layer_idx] = lax.psum_scatter(
            tuple((item[None] for item in totals)), "frames", scatter_dimension=1, tiled=True
        )
    input_grad = jnp.concatenate(upstream, axis=0)[:, None, :]
    stacked = tuple((jnp.stack([layer_grads[0][which]]) for which in range(9)))
    return (
        output,
        input_grad,
        stacked[0],
        stacked[1],
        stacked[2],
        stacked[3],
        stacked[4],
        stacked[5],
        stacked[6],
        stacked[7],
        stacked[8],
    )


def mega(Z, F, S, R, D, H, first, *refs):
    (
        x_ref, seg_ref, cot_ref, ga_ref, gb_ref,
        wq_ref, wk_ref, wv_ref, wo_ref, wg_ref, wu_ref, wd_ref,
        out_ref, ig_ref, gga_ref, ggb_ref, wdg_ref, wog_ref, cg_ref, gg_ref, ug_ref,
        XA, NA, DI, N2, BR, WC, WO, WG, WU, WD, KV, QV, AT, MX,
        P1, P2, P3, P4, R1, R2, R3, R4, HID, GG, UG, GF, UF, KS, KR, OG, QG,
        CS, CR, CK, GS, GR, GK, US, UR, UK, OS, OR, DS, DR,
        GA, GB, PA, PB, QA, QB, ST, MID, GO, MG, ss, rs, ls,
    ) = refs
    C = D // Z
    QR = D // F
    HR = H // 2
    s = lax.axis_index("section")
    f = lax.axis_index("frames")
    z = f // 2
    x = f % 2
    fx = f + 1 - 2 * x
    mate = z + 1 - 2 * (z % 2)
    half = z // 2
    edge = z * (1 - half) + (Z - 1 - z) * half
    outer = edge == 0
    gate = edge == 1
    bf = jnp.bfloat16
    f32 = jnp.float32

    def order(i):
        near = i + edge * (1 - i // 2) * (1 - 2 * i)
        return half * (Z - 1) + (1 - 2 * half) * near

    def rows(i, n):
        if isinstance(i, int):
            return pl.ds(i * n, n)
        return pl.ds(pl.multiple_of(i * n, n), n)

    def remote(src, dst, sslot, rslot, dev):
        return pltpu.make_async_remote_copy(
            src_ref=src, dst_ref=dst, send_sem=ss.at[sslot], recv_sem=rs.at[rslot],
            device_id=dev, device_id_type=pl.DeviceIdType.MESH,
        )

    def arrive(dst, rslot):
        remote(dst, dst, 0, rslot, (s, fx)).wait_recv()

    def tdot(a, b):
        return lax.dot_general(a, b, (((0,), (0,)), ((), ())), preferred_element_type=f32)

    def dott(a, b):
        return lax.dot_general(a, b, (((1,), (1,)), ((), ())), preferred_element_type=f32)

    def dot(a, b):
        return jnp.dot(a, b, preferred_element_type=f32)

    def loop(n, body):
        def step(i, carry):
            body(i)
            return carry
        lax.fori_loop(0, n, step, 0)

    def ag_first(src, buf, base):
        ref = buf.at[rows(z, R)]

        @pl.when(z < Z - 1)
        def _():
            remote(src, ref, base + z, base + z, (s, f + 2)).start()

        @pl.when(z > 0)
        def _():
            remote(src, ref, base + Z + z, base + z, (s, f - 2)).start()

    def ag_copy(buf, base, b, up):
        ref = buf.at[rows(b, R)]
        return remote(ref, ref, base + b + (0 if up else Z), base + b, (s, f + (2 if up else -2)))

    def ag_start(buf, base):
        @pl.when(z < Z - 1)
        def _():
            ag_copy(buf, base, z, True).start()

        @pl.when(z > 0)
        def _():
            ag_copy(buf, base, z, False).start()

    def ag_step(buf, base, b):
        @pl.when(b != z)
        def _():
            arrive(buf.at[rows(b, R)], base + b)

        @pl.when((b < z) & (z < Z - 1))
        def _():
            ag_copy(buf, base, b, True).start()

        @pl.when((b > z) & (z > 0))
        def _():
            ag_copy(buf, base, b, False).start()

    def ag_drain(buf, base):
        def body(b):
            @pl.when((b <= z) & (z < Z - 1))
            def _():
                ag_copy(buf, base, b, True).wait_send()

            @pl.when((b >= z) & (z > 0))
            def _():
                ag_copy(buf, base, b, False).wait_send()
        loop(Z, body)

    def rs_mate(P, Q, base):
        return remote(P.at[rows(mate, R)], Q.at[rows(0, R)], base, base, (s, 2 * mate + x))

    def rs_pre(P, Q, base, b):
        return remote(
            P.at[rows(b, R)], Q.at[rows(2 + b % 2, R)], base + 2 + b % 2, base + 2 + b % 2, (s, 2 * mate + x)
        )

    def rs_far(P, Q, base, b):
        return remote(P.at[rows(b, R)], Q.at[rows(1, R)], base + 4 + b % 2, base + 1, (s, 2 * b + x))

    def rs_send(P, Q, base, b):
        @pl.when(b == mate)
        def _():
            rs_mate(P, Q, base).start()

        @pl.when(outer & (b != mate) & (b != z))
        def _():
            rs_pre(P, Q, base, b).start()

    def rs_gate(P, Q, base):
        @pl.when(gate)
        def _():
            def body(i):
                b = order(i + 2)
                arrive(Q.at[rows(2 + b % 2, R)], base + 2 + b % 2)
                P[rows(b, R), :] = (
                    P[rows(b, R), :].astype(f32) + Q[rows(2 + b % 2, R), :].astype(f32)
                ).astype(bf)
                rs_far(P, Q, base, b).start()
            loop(2, body)

    def rs_wait(P, Q, base):
        arrive(Q.at[rows(0, R)], base)
        arrive(Q.at[rows(1, R)], base + 1)
        return (
            P[rows(z, R), :].astype(f32) + Q[rows(0, R), :].astype(f32) + Q[rows(1, R), :].astype(f32)
        )

    def rs_drain(P, Q, base):
        rs_mate(P, Q, base).wait_send()

        def body(i):
            b = order(i + 2)

            @pl.when(outer)
            def _():
                rs_pre(P, Q, base, b).wait_send()

            @pl.when(gate)
            def _():
                rs_far(P, Q, base, b).wait_send()
        loop(2, body)

    def col_copy(w, buf, base, a, width, k):
        to = (z + k) % Z
        cols = pl.ds(pl.multiple_of(to * width, width), width)
        return remote(
            w.at[:, cols], buf.at[rows(f, QR), pl.ds(a * width, width)],
            base + a * Z + k, base + a * Z + k, (s, 2 * to + x),
        )

    def own_copy(w, buf, slot, a, width):
        cols = pl.ds(pl.multiple_of(z * width, width), width)
        return pltpu.make_async_copy(w.at[:, cols], buf.at[rows(f, QR), pl.ds(a * width, width)], ls.at[slot])

    def side_copy(buf, base, line):
        ref = buf.at[rows(2 * line + x, QR)]
        return remote(ref, ref, base + line, base + line, (s, fx))

    def col_arrive(buf, base, count, width, k):
        line = (z + Z - k) % Z
        for a in range(count):
            arrive(buf.at[rows(2 * line + x, QR), pl.ds(a * width, width)], base + a * Z + k)
        return line

    def side_arrive(buf, base):
        loop(Z, lambda line: arrive(buf.at[rows(2 * line + 1 - x, QR)], base + line))

    def pair_copy(S_, Q_, base, line):
        return remote(S_.at[rows(line, QR)], Q_.at[rows(line, QR)], base + line, base + line, (s, fx))

    def home_copy(K_, o_ref, base, line):
        return remote(K_.at[rows(line, QR)], o_ref.at[z], base + line, base + z, (s, 2 * line + x))

    def grad_make(left, right, K_, S_, Q_, base):
        def body(line):
            both = tdot(left[:, pl.ds(pl.multiple_of(line * 2 * QR, 2 * QR), 2 * QR)], right[...]).astype(bf)
            K_[rows(line, QR), :] = jnp.where(x == 0, both[:QR], both[QR:])
            S_[rows(line, QR), :] = jnp.where(x == 0, both[QR:], both[:QR])
            pair_copy(S_, Q_, base, line).start()
        loop(Z, body)

    def grad_home_step(K_, Q_, o_ref, pbase, hbase, slot, i):
        line = (z + 1 + i) % Z
        arrive(Q_.at[rows(line, QR)], pbase + line)
        K_[rows(line, QR), :] = (
            K_[rows(line, QR), :].astype(f32) + Q_[rows(line, QR), :].astype(f32)
        ).astype(bf)

        @pl.when(line != z)
        def _():
            home_copy(K_, o_ref, hbase, line).start()

        @pl.when(line == z)
        def _():
            pltpu.make_async_copy(K_.at[rows(line, QR)], o_ref.at[z], ls.at[slot]).start()

    def grad_home(*args):
        loop(Z, lambda i: grad_home_step(*args, i))

    def grad_drain(S_, K_, Q_, o_ref, pbase, hbase, slot):
        def body(line):
            pair_copy(S_, Q_, pbase, line).wait_send()

            @pl.when(line != z)
            def _():
                home_copy(K_, o_ref, hbase, line).wait_send()
                arrive(o_ref.at[line], hbase + line)
        loop(Z, body)
        pltpu.make_async_copy(K_.at[rows(z, QR)], o_ref.at[z], ls.at[slot]).wait()

    def gain_copy(src, buf, base, k, sliced):
        to = (f + k) % F
        return remote(src.at[to] if sliced else src, buf.at[f], base + k, base + k, (s, to))

    def gain_arrive(buf, base):
        for k in range(1, F):
            arrive(buf.at[(f + F - k) % F], base + k)

    def row_of(buf):
        return jnp.concatenate([buf[k] for k in range(F)], axis=-1)

    twin = s + 1 - 2 * (s % 2)
    first_of_chip = s % 2 == 0
    near_chip = s < 2

    def kv_copy(b, j, t, way):
        ref = KV.at[j * Z + b]
        return remote(ref, ref, first["kv"] + way * Z + b, first["kv"] + j * Z + b, (t, f))

    def kv_twin(b):
        return kv_copy(b, s, s + 1, 0)

    def kv_across(b):
        return kv_copy(b, s, s + 2, 1)

    def kv_onward(b):
        return kv_copy(b, s - 2, twin, 2)

    def kv_pass(b):
        @pl.when(s >= 2)
        def _():
            arrive(KV.at[(s - 2) * Z + b], first["kv"] + (s - 2) * Z + b)
            kv_onward(b).start()

    def kg_copy(b, j):
        return remote(
            KS.at[j * Z + b], KR.at[s * Z + b], first["kg"] + j * Z + b, first["kg"] + s * Z + b, (j, f)
        )

    def wd_copy(h):
        n = HR // 2
        return remote(
            wd_ref.at[rows(h, n)], WD.at[rows(2 * x + h, n)], first["wd"] + h, first["wd"] + h, (s, fx)
        )

    def wd_arrive():
        for h in range(2):
            arrive(WD.at[rows(2 * (1 - x) + h, HR // 2)], first["wd"] + h)

    for j in range(1, S):
        @pl.when(j > s)
        def _(j=j):
            KV[pl.ds(j * Z, Z)] = jnp.zeros((Z, R, 2 * C), bf)

    barrier = pltpu.get_barrier_semaphore()
    for k in range(1, F):
        pl.semaphore_signal(
            barrier, inc=1, device_id=(s, (f + k) % F), device_id_type=pl.DeviceIdType.MESH
        )
    for k in range(1, S):
        pl.semaphore_signal(
            barrier, inc=1, device_id=((s + k) % S, f), device_id_type=pl.DeviceIdType.MESH
        )
    GA[f] = ga_ref[...]
    GB[f] = gb_ref[...]
    pl.semaphore_wait(barrier, F + S - 2)

    own = pltpu.make_async_copy(x_ref, XA.at[rows(z, R)], ls.at[10])
    ag_first(x_ref, XA, first["na"])
    own.start()
    for k in range(1, F):
        gain_copy(ga_ref, GA, first["ga"], k, False).start()
    qkv = (wq_ref, wk_ref, wv_ref)
    wo_own = pltpu.make_async_copy(wo_ref, WO.at[rows(x, QR)], ls.at[3])
    wo_side = remote(wo_ref, WO.at[rows(x, QR)], first["wo"], first["wo"], (s, fx))
    wd_own = pltpu.make_async_copy(wd_ref, WD.at[rows(x, HR)], ls.at[4])
    for a in range(3):
        own_copy(qkv[a], WC, a, a, C).start()
    wo_own.start()
    wd_own.start()
    own_copy(wg_ref, WG, 5, 0, H).start()
    own_copy(wu_ref, WU, 6, 0, H).start()
    for k in range(1, F):
        gain_copy(gb_ref, GB, first["gb"], k, False).start()
    for a in range(3):
        own_copy(qkv[a], WC, a, a, C).wait()
    side_copy(WC, first["wcx"], z).start()
    for a in range(3):
        col_copy(qkv[a], WC, first["wc"], a, C, 3).start()
    for a in range(3):
        col_copy(qkv[a], WC, first["wc"], a, C, 2).start()
    for a in range(3):
        col_copy(qkv[a], WC, first["wc"], a, C, 1).start()
    ST[...] = x_ref[...].astype(f32)
    mask = (seg_ref[...] != 0).astype(f32)
    GO[...] = cot_ref[...].astype(f32) * mask
    DI[rows(z, R), :] = GO[...].astype(bf)
    own.wait()
    own_copy(wg_ref, WG, 5, 0, H).wait()
    own_copy(wu_ref, WU, 6, 0, H).wait()
    gain_arrive(GA, first["ga"])

    def wc_on(k):
        side_copy(WC, first["wcx"], col_arrive(WC, first["wc"], 3, C, k)).start()

    ag_step(XA, first["na"], order(1))
    wd_copy(0).start()
    ag_step(XA, first["na"], order(2))
    col_copy(wg_ref, WG, first["wg"], 0, H, 2).start()
    wc_on(2)
    wc_on(1)
    col_copy(wg_ref, WG, first["wg"], 0, H, 1).start()
    wc_on(3)
    col_copy(wg_ref, WG, first["wg"], 0, H, 3).start()
    side_arrive(WC, first["wcx"])
    wo_side.start()

    def block_qkv(i):
        b = order(i)

        @pl.when(i == 0)
        def _():
            wd_copy(1).start()

        @pl.when(i == 2)
        def _():
            col_copy(wu_ref, WU, first["wu"], 0, H, 1).start()

        @pl.when(i == 3)
        def _():
            col_copy(wu_ref, WU, first["wu"], 0, H, 2).start()

        @pl.when(i == 3)
        def _():
            side_copy(WG, first["wgx"], z).start()

        @pl.when(i == 3)
        def _():
            ag_step(XA, first["na"], order(3))
        block = XA[rows(b, R), :].astype(f32)
        scale = lax.rsqrt(jnp.mean(block * block, axis=-1, keepdims=True) + epsilon)
        NA[rows(b, R), :] = (block * scale * row_of(GA)).astype(bf)
        both = dot(NA[rows(b, R), :], WC[...]).astype(bf)
        QV[rows(b, R), :] = both[:, :C]
        KV[s * Z + b] = both[:, C:]

        @pl.when(near_chip)
        def _():
            kv_across(b).start()

        @pl.when(first_of_chip)
        def _():
            kv_twin(b).start()
    loop(Z, block_qkv)

    wo_own.wait()
    arrive(WO.at[rows(1 - x, QR)], first["wo"])

    groups = lax.broadcasted_iota(jnp.int32, (C, C), 0) // HEAD_DIM
    ones = (groups == lax.broadcasted_iota(jnp.int32, (C, C), 1) // HEAD_DIM).astype(f32).astype(bf)

    def head_sum(product):
        high = product.astype(bf)
        rest = (product - high.astype(f32)).astype(bf)
        return dot(high, ones) + dot(rest, ones)

    def block_attend(i):
        b = order(i)

        @pl.when(i < Z - 1)
        def _():
            kv_pass(order(i + 1))
        for j in range(S - 1):
            @pl.when((j < s) & (j != s - 2))
            def _(j=j):
                arrive(KV.at[j * Z + b], first["kv"] + j * Z + b)
        query = QV[rows(b, R), :].astype(f32)
        scores = []
        for j in range(S):
            score = head_sum(query * KV[j * Z + b, :, :C].astype(f32)) * HEAD_DIM ** (-0.5)
            scores.append(jnp.where(j <= s, score, -1e30))
        largest = functools.reduce(jnp.maximum, scores)
        expo = [jnp.exp(score - largest) for score in scores]
        total = functools.reduce(lambda u, v: u + v, expo)
        mixed = jnp.zeros((R, C), f32)
        for j in range(S):
            attn = expo[j] / total
            AT[j * Z + b] = attn
            mixed = mixed + attn * KV[j * Z + b, :, C:].astype(f32)
        mixed = mixed.astype(bf)
        MX[rows(b, R), :] = mixed
        P1[rows(b, R), :] = dot(mixed, WO[...]).astype(bf)
        rs_send(P1, R1, first["r1"], b)

        @pl.when(i == 1)
        def _():
            side_copy(WU, first["wux"], col_arrive(WU, first["wu"], 1, H, 1)).start()

        @pl.when(i == 2)
        def _():
            side_copy(WG, first["wgx"], col_arrive(WG, first["wg"], 1, H, 3)).start()

        @pl.when(i == 2)
        def _():
            side_copy(WG, first["wgx"], col_arrive(WG, first["wg"], 1, H, 1)).start()

        @pl.when(i == 3)
        def _():
            side_copy(WG, first["wgx"], col_arrive(WG, first["wg"], 1, H, 2)).start()

        @pl.when(i == 3)
        def _():
            side_copy(WU, first["wux"], col_arrive(WU, first["wu"], 1, H, 2)).start()

        @pl.when(i == 3)
        def _():
            side_copy(WU, first["wux"], z).start()
    kv_pass(order(0))
    loop(Z, block_attend)
    col_copy(wu_ref, WU, first["wu"], 0, H, 3).start()
    ag_start(DI, first["di"])
    rs_gate(P1, R1, first["r1"])
    side_copy(WU, first["wux"], col_arrive(WU, first["wu"], 1, H, 3)).start()
    middle = ST[...] + rs_wait(P1, R1, first["r1"])
    MID[...] = middle
    gain_arrive(GB, first["gb"])
    inverse = lax.rsqrt(jnp.mean(middle * middle, axis=-1, keepdims=True) + epsilon)
    N2[rows(z, R), :] = (middle * inverse * row_of(GB)).astype(bf)
    ag_start(N2, first["n2"])
    ag_step(DI, first["di"], order(1))
    side_arrive(WG, first["wgx"])
    side_arrive(WU, first["wux"])
    wd_own.wait()
    wd_arrive()

    def block_ffn(i):
        b = order(i)
        ag_step(N2, first["n2"], b)
        normed2 = N2[rows(b, R), :]
        gate_act = dot(normed2, WG[...])
        up_act = dot(normed2, WU[...])
        GF[rows(b, R), :] = gate_act
        UF[rows(b, R), :] = up_act
        HID[rows(b, R), :] = (gate_act / (1.0 + jnp.exp(-gate_act)) * up_act).astype(bf)

        @pl.when(i == 0)
        def _():
            ag_step(DI, first["di"], order(2))
    loop(Z, block_ffn)

    def block_down(i):
        b = order(i)
        P3[rows(b, R), :] = dot(HID[rows(b, R), :], WD[...]).astype(bf)
        rs_send(P3, R3, first["r3"], b)

    down_out = remote(DS, DR, first["dx"], first["dx"], (s, fx))

    def down_make(i):
        n = HR // 2
        mine = pl.ds(pl.multiple_of(x * HR + i * n, n), n)
        other = pl.ds(pl.multiple_of((1 - x) * HR + i * n, n), n)
        DS[rows(i, n), :] = tdot(HID[:, other], DI[...]).astype(bf)
        wdg_ref[rows(i, n), :] = tdot(HID[:, mine], DI[...])

    def block_ffn_back(i):
        b = order(i)
        gate_act = GF[rows(b, R), :]
        up_act = UF[rows(b, R), :]
        sig = 1.0 / (1.0 + jnp.exp(-gate_act))
        silu = gate_act * sig
        hidden_grad = dott(DI[rows(b, R), :], WD[...])
        gate_grad = (hidden_grad * up_act * (sig * (1.0 + gate_act * (1.0 - sig)))).astype(bf)
        up_grad = (hidden_grad * silu).astype(bf)
        GG[rows(b, R), :] = gate_grad
        UG[rows(b, R), :] = up_grad
        P2[rows(b, R), :] = (dott(gate_grad, WG[...]) + dott(up_grad, WU[...])).astype(bf)
        rs_send(P2, R2, first["r2"], b)

        @pl.when(i == 2)
        def _():
            ag_step(DI, first["di"], order(3))
    loop(Z, block_ffn_back)
    grad_make(N2, GG, GK, GS, GR, first["gx"])
    grad_make(N2, UG, UK, US, UR, first["ux"])
    rs_gate(P2, R2, first["r2"])

    middle = MID[...]
    inverse = lax.rsqrt(jnp.mean(middle * middle, axis=-1, keepdims=True) + epsilon)
    unit = middle * inverse
    normed_grad = rs_wait(P2, R2, first["r2"])
    scaled = normed_grad * row_of(GB)
    middle_grad = GO[...] + (scaled - unit * jnp.mean(scaled * unit, axis=-1, keepdims=True)) * inverse
    MG[...] = middle_grad
    BR[rows(z, R), :] = middle_grad.astype(bf)
    ag_start(BR, first["br"])
    loop(2, down_make)
    down_out.start()
    part = jnp.sum(normed_grad * unit, axis=0, keepdims=True)
    for k in range(F):
        PB[k] = part[:, k * QR : (k + 1) * QR]
    for k in range(1, F):
        gain_copy(PB, QB, first["qb"], k, True).start()
    block_down(0)
    block_down(1)
    block_down(2)
    block_down(3)

    def out_make():
        both = tdot(MX[...], BR[...])
        wog_ref[...] = jnp.where(x == 0, both[:QR], both[QR:])
        OS[...] = jnp.where(x == 0, both[QR:], both[:QR]).astype(bf)
        out_out.start()

    out_out = remote(OS, OR, first["ox"], first["ox"], (s, fx))

    def block_back(i):
        b = order(i)
        ag_step(BR, first["br"], b)

        @pl.when(i == 0)
        def _():
            grad_home_step(GK, GR, gg_ref, first["gx"], first["gh"], 7, 2)

        @pl.when(i == 0)
        def _():
            grad_home_step(GK, GR, gg_ref, first["gx"], first["gh"], 7, 0)

        @pl.when(i == 2)
        def _():
            grad_home_step(UK, UR, ug_ref, first["ux"], first["uh"], 8, 0)

        @pl.when(i == 2)
        def _():
            grad_home_step(GK, GR, gg_ref, first["gx"], first["gh"], 7, 1)

        @pl.when(i == 2)
        def _():
            grad_home_step(UK, UR, ug_ref, first["ux"], first["uh"], 8, 2)

        @pl.when(i == 3)
        def _():
            rs_gate(P3, R3, first["r3"])

        @pl.when(i == 3)
        def _():
            grad_home_step(UK, UR, ug_ref, first["ux"], first["uh"], 8, 3)
        mixed_grad = dott(BR[rows(b, R), :], WO[...])
        query = QV[rows(b, R), :].astype(f32)
        inner = []
        total = jnp.zeros((R, C), f32)
        for j in range(S):
            one = head_sum(mixed_grad * KV[j * Z + b, :, C:].astype(f32))
            inner.append(one)
            total = total + AT[j * Z + b] * one
        query_grad = jnp.zeros((R, C), f32)
        for j in range(S):
            attn = AT[j * Z + b]
            score_grad = attn * (inner[j] - total) * HEAD_DIM ** (-0.5)
            query_grad = query_grad + score_grad * KV[j * Z + b, :, :C].astype(f32)
            key_part = score_grad * query
            value_part = attn * mixed_grad

            @pl.when(j == s)
            def _(key_part=key_part, value_part=value_part):
                OG[b, :, :C] = key_part
                OG[b, :, C:] = value_part

            @pl.when(j < s)
            def _(j=j, key_part=key_part, value_part=value_part):
                KS[j * Z + b, :, :C] = key_part.astype(bf)
                KS[j * Z + b, :, C:] = value_part.astype(bf)
                kg_copy(b, j).start()
        QG[rows(b, R), :C] = query_grad.astype(bf)
    loop(Z, block_back)
    grad_home_step(UK, UR, ug_ref, first["ux"], first["uh"], 8, 1)

    def block_normed(i):
        b = order(i)
        for j in range(1, S):
            @pl.when(j > s)
            def _(j=j):
                arrive(KR.at[j * Z + b], first["kg"] + j * Z + b)
                OG[b] = OG[b] + KR[j * Z + b].astype(f32)
        QG[rows(b, R), C:] = OG[b].astype(bf)
        P4[rows(b, R), :] = dott(QG[rows(b, R), :], WC[...]).astype(bf)
        rs_send(P4, R4, first["r4"], b)
    loop(Z, block_normed)
    grad_home_step(GK, GR, gg_ref, first["gx"], first["gh"], 7, 3)
    grad_make(NA, QG, CK, CS, CR, first["cx"])
    grad_home_step(CK, CR, cg_ref, first["cx"], first["ch"], 9, 0)
    grad_home_step(CK, CR, cg_ref, first["cx"], first["ch"], 9, 2)
    rs_gate(P4, R4, first["r4"])
    grad_home_step(CK, CR, cg_ref, first["cx"], first["ch"], 9, 1)
    grad_home_step(CK, CR, cg_ref, first["cx"], first["ch"], 9, 3)

    out_make()

    stream = ST[...]
    inverse = lax.rsqrt(jnp.mean(stream * stream, axis=-1, keepdims=True) + epsilon)
    unit = stream * inverse
    normed_grad = rs_wait(P4, R4, first["r4"])
    part = jnp.sum(normed_grad * unit, axis=0, keepdims=True)
    for k in range(F):
        PA[k] = part[:, k * QR : (k + 1) * QR]
    for k in range(1, F):
        gain_copy(PA, QA, first["qa"], k, True).start()
    scaled = normed_grad * row_of(GA)
    ig_ref[...] = MG[...] + (scaled - unit * jnp.mean(scaled * unit, axis=-1, keepdims=True)) * inverse
    QA[f] = PA[f]
    QB[f] = PB[f]
    out_ref[...] = (MID[...] + rs_wait(P3, R3, first["r3"])).astype(bf)
    arrive(DR, first["dx"])
    wdg_ref[...] = wdg_ref[...] + DR[...].astype(f32)

    arrive(OR, first["ox"])
    wog_ref[...] = wog_ref[...] + OR[...].astype(f32)
    gain_arrive(QB, first["qb"])
    gain_arrive(QA, first["qa"])
    gga_ref[...] = functools.reduce(lambda u, v: u + v, [QA[k] for k in range(F)])
    ggb_ref[...] = functools.reduce(lambda u, v: u + v, [QB[k] for k in range(F)])

    for k in range(1, F):
        gain_copy(ga_ref, GA, first["ga"], k, False).wait_send()
        gain_copy(gb_ref, GB, first["gb"], k, False).wait_send()
        gain_copy(PA, QA, first["qa"], k, True).wait_send()
        gain_copy(PB, QB, first["qb"], k, True).wait_send()
    for k in range(1, Z):
        for a in range(3):
            col_copy(qkv[a], WC, first["wc"], a, C, k).wait_send()
        col_copy(wg_ref, WG, first["wg"], 0, H, k).wait_send()
        col_copy(wu_ref, WU, first["wu"], 0, H, k).wait_send()

    def sides(line):
        side_copy(WC, first["wcx"], line).wait_send()
        side_copy(WG, first["wgx"], line).wait_send()
        side_copy(WU, first["wux"], line).wait_send()
    loop(Z, sides)
    wo_side.wait_send()
    wd_copy(0).wait_send()
    wd_copy(1).wait_send()
    down_out.wait_send()
    out_out.wait_send()
    ag_drain(XA, first["na"])
    ag_drain(DI, first["di"])
    ag_drain(N2, first["n2"])
    ag_drain(BR, first["br"])
    rs_drain(P1, R1, first["r1"])
    rs_drain(P2, R2, first["r2"])
    rs_drain(P3, R3, first["r3"])
    rs_drain(P4, R4, first["r4"])

    def across(b):
        @pl.when(near_chip)
        def _():
            kv_across(b).wait_send()

        @pl.when(s >= 2)
        def _():
            kv_onward(b).wait_send()

        @pl.when(first_of_chip)
        def _():
            kv_twin(b).wait_send()

        for t in range(S):
            @pl.when(t < s)
            def _(t=t):
                kg_copy(b, t).wait_send()
    loop(Z, across)
    grad_drain(GS, GK, GR, gg_ref, first["gx"], first["gh"], 7)
    grad_drain(US, UK, UR, ug_ref, first["ux"], first["uh"], 8)
    grad_drain(CS, CK, CR, cg_ref, first["cx"], first["ch"], 9)


def finish(
    Z, QR, C, H, output, input_grad, gain_one, gain_two, down, out, cols, gate, up,
    o_in, o_q, o_k, o_v, o_gate, o_up, o_out, o_down, o_wo, o_ga, o_gb,
    iw, qf, kf, vf, gf, uf, os,
):
    stores = []

    def store(src, dst):
        stores.append(pltpu.make_async_copy(src, dst, os.at[len(stores)]))
        stores[-1].start()

    for src, dst in ((down, o_down), (out, o_wo), (output, o_out), (gain_one, o_ga), (gain_two, o_gb)):
        store(src, dst)
    for part, (full, target) in enumerate(((qf, o_q), (kf, o_k), (vf, o_v))):
        for line in range(Z):
            full[:, line * C : (line + 1) * C] = cols[line, :, part * C : (part + 1) * C].astype(jnp.float32)
        store(full, target)
    for low, full, target in ((gate, gf, o_gate), (up, uf, o_up)):
        for line in range(Z):
            cols_of = pl.ds(line * H, H)
            full[:, cols_of] = low[line].astype(jnp.float32)
            store(full.at[:, cols_of], target.at[:, cols_of])
    iw[...] = input_grad[...].reshape(iw.shape)
    store(iw, o_in)
    for item in stores:
        item.wait()


def line_plan(
    frames_in, segment_ids, cotangent, norm_attn, w_query, w_key, w_value, w_out, norm_ffn, w_gate, w_up, w_down
):
    R, _, D = frames_in.shape
    F = lax.axis_size("frames")
    S = lax.axis_size("section")
    Z = F // 2
    C = D // Z
    H = w_gate.shape[3] // Z
    QR = D // F
    HR = H // 2
    counts = dict(
        ga=F, gb=F, qa=F, qb=F, wc=3 * Z, wcx=Z, wg=Z, wgx=Z, wu=Z, wux=Z, wo=1, wd=2,
        na=2 * Z, di=2 * Z, n2=2 * Z, br=2 * Z, r1=6, r2=6, r3=6, r4=6,
        kv=S * Z, kg=S * Z, gx=Z, gh=Z, ux=Z, uh=Z, cx=Z, ch=Z, ox=1, dx=1,
    )
    first, slots = {}, 0
    for name, count in counts.items():
        first[name] = slots
        slots += count
    bf, f32 = jnp.bfloat16, jnp.float32
    V = pltpu.VMEM
    scratch = [
        V((Z * R, D), bf), V((Z * R, D), bf), V((Z * R, D), bf), V((Z * R, D), bf), V((Z * R, D), bf),
        V((D, 3 * C), bf), V((2 * QR, D), bf), V((D, H), bf), V((D, H), bf), V((2 * HR, D), bf),
        V((S * Z, R, 2 * C), bf), V((Z * R, C), bf), V((S * Z, R, C), f32), V((Z * R, C), bf),
        V((Z * R, D), bf), V((Z * R, D), bf), V((Z * R, D), bf), V((Z * R, D), bf),
        V((4 * R, D), bf), V((4 * R, D), bf), V((4 * R, D), bf), V((4 * R, D), bf),
        V((Z * R, H), bf), V((Z * R, H), bf), V((Z * R, H), bf),
        V((Z * R, H), f32), V((Z * R, H), f32),
        V((S * Z, R, 2 * C), bf), V((S * Z, R, 2 * C), bf), V((Z, R, 2 * C), f32), V((Z * R, 3 * C), bf),
        V((Z * QR, 3 * C), bf), V((Z * QR, 3 * C), bf), V((Z * QR, 3 * C), bf),
        V((Z * QR, H), bf), V((Z * QR, H), bf), V((Z * QR, H), bf),
        V((Z * QR, H), bf), V((Z * QR, H), bf), V((Z * QR, H), bf),
        V((QR, D), bf), V((QR, D), bf), V((HR, D), bf), V((HR, D), bf),
        V((F, 1, QR), f32), V((F, 1, QR), f32), V((F, 1, QR), f32), V((F, 1, QR), f32),
        V((F, 1, QR), f32), V((F, 1, QR), f32),
        V((R, D), f32), V((R, D), f32), V((R, D), f32), V((R, D), f32),
        pltpu.SemaphoreType.DMA((slots,)), pltpu.SemaphoreType.DMA((slots,)), pltpu.SemaphoreType.DMA((11,)),
    ]
    vmem = pl.BlockSpec(memory_space=pltpu.VMEM)
    anyw = pl.BlockSpec(memory_space=pl.ANY)
    shape = jax.ShapeDtypeStruct
    results = pl.pallas_call(
        functools.partial(mega, Z, F, S, R, D, H, first),
        out_shape=(
            shape((R, D), bf), shape((R, D), f32), shape((1, QR), f32), shape((1, QR), f32),
            shape((HR, D), f32), shape((QR, D), f32),
            shape((Z, QR, 3 * C), bf), shape((Z, QR, H), bf), shape((Z, QR, H), bf),
        ),
        in_specs=[vmem] * 5 + [anyw] * 7,
        out_specs=(vmem,) * 6 + (anyw,) * 3,
        scratch_shapes=scratch,
        compiler_params=pltpu.CompilerParams(
            collective_id=0, has_side_effects=True, vmem_limit_bytes=VMEM_LIMIT
        ),
        name="layer",
    )(
        frames_in[:, 0, :], segment_ids[:, None], cotangent[:, 0, :], norm_attn[0], norm_ffn[0],
        w_query[0, 0], w_key[0, 0], w_value[0, 0], w_out[0, 0], w_gate[0, 0], w_up[0, 0], w_down[0, 0],
    )
    output, input_grad, gain_one, gain_two, down, out, cols, gate, up = results
    done = pl.pallas_call(
        functools.partial(finish, Z, QR, C, H),
        out_shape=(
            shape((R, 1, D), f32), shape((QR, D), f32), shape((QR, D), f32), shape((QR, D), f32),
            shape((QR, Z * H), f32), shape((QR, Z * H), f32), shape((R, D), bf), shape((HR, D), f32),
            shape((QR, D), f32), shape((1, QR), f32), shape((1, QR), f32),
        ),
        in_specs=[vmem] * 9,
        out_specs=(anyw,) * 11,
        scratch_shapes=[
            V((R, 1, D), f32), V((QR, D), f32), V((QR, D), f32), V((QR, D), f32), V((QR, Z * H), f32), V((QR, Z * H), f32),
            pltpu.SemaphoreType.DMA((9 + 2 * Z,)),
        ],
        compiler_params=pltpu.CompilerParams(vmem_limit_bytes=VMEM_LIMIT),
        name="finish",
    )(output, input_grad, gain_one, gain_two, down, out, cols, gate, up)
    input_grad, query, key, value, gate, up, output, down, out, gain_one, gain_two = done
    return (
        output[:, None, :], input_grad, gain_one[None],
        query[None, None], key[None, None], value[None, None], out[None, None], gain_two[None],
        gate[None, None], up[None, None], down[None, None],
    )


def solution(mesh):
    placed = (
        P("frames", "section", None),
        P("frames"),
        P("frames", "section", None),
        P(None, "section", "frames"),
        P(None, "section", "frames", None),
        P(None, "section", "frames", None),
        P(None, "section", "frames", None),
        P(None, "section", "frames", None),
        P(None, "section", "frames"),
        P(None, "section", "frames", None),
        P(None, "section", "frames", None),
        P(None, "section", "frames", None),
    )
    lines = mesh.shape["frames"] == 8 and mesh.shape["section"] == 4

    def per_device(*arrays):
        width = arrays[0].shape[2]
        fits = lines and arrays[4].shape[0] == 1 and arrays[0].shape[1] == 1 and width % 1024 == 0
        return line_plan(*arrays) if fits else gather_plan(*arrays)

    return jax.shard_map(
        per_device,
        mesh=mesh,
        in_specs=placed,
        out_specs=(
            P("frames", "section", None),
            P("frames", "section", None),
            P(None, "section", "frames"),
            P(None, "section", "frames", None),
            P(None, "section", "frames", None),
            P(None, "section", "frames", None),
            P(None, "section", "frames", None),
            P(None, "section", "frames"),
            P(None, "section", "frames", None),
            P(None, "section", "frames", None),
            P(None, "section", "frames", None),
        ),
        check_vma=False,
    )
```

```python
import functools

import jax
import jax.numpy as jnp
from jax import lax
from jax.experimental import pallas as pl
from jax.experimental.pallas import tpu as pltpu
from jax.sharding import PartitionSpec as P

HEAD_DIM = 64
MICRO = 2
VMEM_LIMIT = 63 * 1024 * 1024


epsilon = 1e-05


def carried_in(shard, axis, combine, identity):
    devices, place = (lax.axis_size(axis), lax.axis_index(axis))
    everything = lax.all_gather(shard, axis)
    start = jnp.broadcast_to(jnp.asarray(identity, shard.dtype), shard.shape)

    def hop(k, before):
        reached = k < place
        new = combine(before, everything[k])
        return jnp.where(reached, new, before)

    return lax.fori_loop(0, devices, hop, start)


def carried_in_2(shard, axis, combine, identity):
    devices, place = (lax.axis_size(axis), lax.axis_index(axis))
    everything = lax.all_gather(shard.astype(jnp.bfloat16), axis)
    start = jnp.broadcast_to(jnp.asarray(identity, shard.dtype), shard.shape)

    def hop(k, before):
        at = devices - 1 - k
        reached = at > place
        new = combine(before, everything[at].astype(shard.dtype))
        return jnp.where(reached, new, before)

    return lax.fori_loop(0, devices, hop, start)


def rms_scale(values, gain):
    return values * lax.rsqrt(jnp.mean(values * values, axis=-1, keepdims=True) + epsilon) * gain


def project(left, weight):
    return jnp.dot(left, weight, preferred_element_type=jnp.float32)


def left_product(left, right):
    return lax.dot_general(
        left, right, (((0,), (0,)), ((), ())), preferred_element_type=jnp.float32
    )


def right_product(left, weight):
    return lax.dot_general(
        left, weight, (((1,), (1,)), ((), ())), preferred_element_type=jnp.float32
    )


def add_pair(first_part, second_part):
    return first_part + second_part


def attend(query_vec, key_all, values, section_idx):
    scores = jnp.einsum(
        "mhe,mphe->mhp", query_vec, key_all, precision=lax.Precision.HIGHEST
    ) * HEAD_DIM ** (-0.5)
    allowed = jnp.arange(key_all.shape[1]) <= section_idx
    scores = jnp.where(allowed, scores, -1e30)
    largest = jnp.max(scores, axis=-1, keepdims=True)
    expo_terms = jnp.exp(scores - largest)
    weights = expo_terms / jnp.sum(expo_terms, axis=-1, keepdims=True)
    return jnp.einsum("mhp,mphe->mhe", weights, values, precision=lax.Precision.HIGHEST)


def share_kv(own_kv, slot_mask):
    placed = jnp.where(slot_mask[None, :, None], own_kv[:, None, :], jnp.zeros((), jnp.bfloat16))
    earlier = carried_in(placed, "section", add_pair, jnp.zeros_like(placed))
    return earlier + placed


def return_kv_grads(grad_kv, section_idx):
    later_sum = carried_in_2(grad_kv, "section", add_pair, jnp.zeros_like(grad_kv))
    return lax.dynamic_index_in_dim(later_sum + grad_kv, section_idx, 1, keepdims=False)


def layer_rest(frame_rows, weights, query_vec, full_kv, section_idx):
    gain_one, wq_l, wk_l, wv_l, wo_l, gain_two, wg_l, wu_l, wd_l = weights
    packed_row_count = frame_rows.shape[0]
    model_width = frame_rows.shape[1]
    head_count = model_width // HEAD_DIM
    positions = full_kv.shape[1]
    key_all = (
        full_kv[:, :, :model_width]
        .astype(jnp.float32)
        .reshape(packed_row_count, positions, head_count, HEAD_DIM)
    )
    values = (
        full_kv[:, :, model_width:]
        .astype(jnp.float32)
        .reshape(packed_row_count, positions, head_count, HEAD_DIM)
    )
    query_f = query_vec.astype(jnp.float32).reshape(packed_row_count, head_count, HEAD_DIM)
    mixed_out = (
        attend(query_f, key_all, values, section_idx)
        .reshape(packed_row_count, model_width)
        .astype(jnp.bfloat16)
    )
    middle = frame_rows + project(mixed_out, wo_l)
    normed2 = rms_scale(middle, gain_two).astype(jnp.bfloat16)
    gate_act = project(normed2, wg_l)
    up_act = project(normed2, wu_l)
    hidden = (jax.nn.silu(gate_act) * up_act).astype(jnp.bfloat16)
    result = middle + project(hidden, wd_l)
    return (query_f, key_all, values, mixed_out, middle, normed2, gate_act, up_act, hidden, result)


def gather_plan(
    frames_in,
    segment_ids,
    cotangent,
    norm_attn,
    w_query,
    w_key,
    w_value,
    w_out,
    norm_ffn,
    w_gate,
    w_up,
    w_down,
):
    section_idx = lax.axis_index("section")
    frame_count = frames_in.shape[0]
    model_width = frames_in.shape[2]
    head_count = model_width // HEAD_DIM
    micro_rows = frame_count // MICRO
    positions = lax.axis_size("section") * frames_in.shape[1]
    layer_count = w_query.shape[0]
    slot_mask = jnp.arange(positions) == section_idx
    stream = frames_in[:, 0, :].astype(jnp.float32)
    layer_idx = 0
    pieces = (
        norm_attn[layer_idx],
        w_query[layer_idx],
        w_key[layer_idx],
        w_value[layer_idx],
        w_out[layer_idx],
        norm_ffn[layer_idx],
        w_gate[layer_idx],
        w_up[layer_idx],
        w_down[layer_idx],
    )
    gathered = (
        lax.all_gather(pieces[0].astype(jnp.bfloat16), "frames", axis=1, tiled=True).astype(
            jnp.float32
        ),
        lax.all_gather(pieces[1], "frames", axis=1, tiled=True),
        lax.all_gather(pieces[2], "frames", axis=1, tiled=True),
        lax.all_gather(pieces[3], "frames", axis=1, tiled=True),
        lax.all_gather(pieces[4], "frames", axis=1, tiled=True),
        lax.all_gather(pieces[5].astype(jnp.bfloat16), "frames", axis=1, tiled=True).astype(
            jnp.float32
        ),
        lax.all_gather(pieces[6], "frames", axis=1, tiled=True),
        lax.all_gather(pieces[7], "frames", axis=1, tiled=True),
        lax.all_gather(pieces[8], "frames", axis=1, tiled=True),
    )
    weights = tuple((gathered_item[0] for gathered_item in gathered))
    layer_inputs = []
    layer_kv = []
    results = []
    for micro_idx in range(MICRO):
        frame_rows = stream[micro_idx * micro_rows : (micro_idx + 1) * micro_rows]
        normed = rms_scale(frame_rows, weights[0]).astype(jnp.bfloat16)
        query_vec = project(normed, weights[1]).astype(jnp.bfloat16)
        own_kv = jnp.concatenate(
            [
                project(normed, weights[2]).astype(jnp.bfloat16),
                project(normed, weights[3]).astype(jnp.bfloat16),
            ],
            axis=-1,
        )
        full_kv = share_kv(own_kv, slot_mask)
        outcome = layer_rest(frame_rows, weights, query_vec, full_kv, section_idx)
        layer_inputs.append(frame_rows)
        layer_kv.append(full_kv)
        results.append(outcome[-1])
    kept_inputs = [layer_inputs]
    kept_kv = [layer_kv]
    stream = jnp.concatenate(results, axis=0)
    output = stream.astype(jnp.bfloat16)[:, None, :]
    frame_mask = (segment_ids != 0).astype(jnp.float32)[:, None]
    upstream_all = cotangent[:, 0, :].astype(jnp.float32) * frame_mask
    upstream = [
        upstream_all[micro_idx * micro_rows : (micro_idx + 1) * micro_rows]
        for micro_idx in range(MICRO)
    ]
    layer_grads = [None] * layer_count
    for layer_idx in reversed(range(layer_count)):
        pieces = (
            norm_attn[layer_idx],
            w_query[layer_idx],
            w_key[layer_idx],
            w_value[layer_idx],
            w_out[layer_idx],
            norm_ffn[layer_idx],
            w_gate[layer_idx],
            w_up[layer_idx],
            w_down[layer_idx],
        )
        gathered = (
            lax.all_gather(pieces[0].astype(jnp.bfloat16), "frames", axis=1, tiled=True).astype(
                jnp.float32
            ),
            lax.all_gather(pieces[1], "frames", axis=1, tiled=True),
            lax.all_gather(pieces[2], "frames", axis=1, tiled=True),
            lax.all_gather(pieces[3], "frames", axis=1, tiled=True),
            lax.all_gather(pieces[4], "frames", axis=1, tiled=True),
            lax.all_gather(pieces[5].astype(jnp.bfloat16), "frames", axis=1, tiled=True).astype(
                jnp.float32
            ),
            lax.all_gather(pieces[6], "frames", axis=1, tiled=True),
            lax.all_gather(pieces[7], "frames", axis=1, tiled=True),
            lax.all_gather(pieces[8], "frames", axis=1, tiled=True),
        )
        weights = tuple((gathered_item[0] for gathered_item in gathered))
        gain_one, wq_l, wk_l, wv_l, wo_l, gain_two, wg_l, wu_l, wd_l = weights
        totals = [jnp.zeros(item.shape, jnp.float32) for item in weights]
        for micro_idx in range(MICRO):
            micro_grads = [None] * 9
            frame_rows = kept_inputs[layer_idx][micro_idx]
            full_kv = kept_kv[layer_idx][micro_idx]
            grad_out = upstream[micro_idx]
            normed = rms_scale(frame_rows, gain_one).astype(jnp.bfloat16)
            query_vec = project(normed, wq_l).astype(jnp.bfloat16)
            (
                query_f,
                key_all,
                values,
                mixed_out,
                middle,
                normed2,
                gate_act,
                up_act,
                hidden,
                result,
            ) = layer_rest(frame_rows, weights, query_vec, full_kv, section_idx)
            down_in = grad_out.astype(jnp.bfloat16)
            micro_grads[8] = left_product(hidden, down_in)
            hidden_grad = right_product(down_in, wd_l)
            _, pullback = jax.vjp(
                lambda gate_in, up_in: jax.nn.silu(gate_in) * up_in, gate_act, up_act
            )
            gate_grad, up_grad = pullback(hidden_grad)
            gate_grad = gate_grad.astype(jnp.bfloat16)
            up_grad = up_grad.astype(jnp.bfloat16)
            micro_grads[6] = left_product(normed2, gate_grad)
            micro_grads[7] = left_product(normed2, up_grad)
            normed2_grad = right_product(gate_grad, wg_l) + right_product(up_grad, wu_l)
            _, pullback = jax.vjp(rms_scale, middle, gain_two)
            middle_part, gain_two_part = pullback(normed2_grad)
            middle_grad = grad_out + middle_part
            micro_grads[5] = gain_two_part
            branch_in = middle_grad.astype(jnp.bfloat16)
            micro_grads[4] = left_product(mixed_out, branch_in)
            mixed_grad = right_product(branch_in, wo_l)
            _, pullback = jax.vjp(
                lambda query_in, key_in, value_in: attend(query_in, key_in, value_in, section_idx),
                query_f,
                key_all,
                values,
            )
            query_grad, key_grad, value_grad = pullback(
                mixed_grad.reshape(micro_rows, head_count, HEAD_DIM)
            )
            grad_kv = jnp.concatenate(
                [
                    key_grad.reshape(micro_rows, positions, model_width),
                    value_grad.reshape(micro_rows, positions, model_width),
                ],
                axis=-1,
            )
            own_grad = return_kv_grads(grad_kv, section_idx)
            query_low = query_grad.reshape(micro_rows, model_width).astype(jnp.bfloat16)
            key_low = own_grad[:, :model_width].astype(jnp.bfloat16)
            value_low = own_grad[:, model_width:].astype(jnp.bfloat16)
            micro_grads[1] = left_product(normed, query_low)
            micro_grads[2] = left_product(normed, key_low)
            micro_grads[3] = left_product(normed, value_low)
            normed_grad = (
                right_product(query_low, wq_l)
                + right_product(key_low, wk_l)
                + right_product(value_low, wv_l)
            )
            _, pullback = jax.vjp(rms_scale, frame_rows, gain_one)
            rows_part, gain_one_part = pullback(normed_grad)
            micro_grads[0] = gain_one_part
            upstream[micro_idx] = middle_grad + rows_part
            totals = [first + second for first, second in zip(totals, micro_grads)]
        layer_grads[layer_idx] = lax.psum_scatter(
            tuple((item[None] for item in totals)), "frames", scatter_dimension=1, tiled=True
        )
    input_grad = jnp.concatenate(upstream, axis=0)[:, None, :]
    stacked = tuple((jnp.stack([layer_grads[0][which]]) for which in range(9)))
    return (
        output,
        input_grad,
        stacked[0],
        stacked[1],
        stacked[2],
        stacked[3],
        stacked[4],
        stacked[5],
        stacked[6],
        stacked[7],
        stacked[8],
    )


def mega(Z, F, S, R, D, H, first, *refs):
    (
        x_ref, seg_ref, cot_ref, ga_ref, gb_ref,
        wq_ref, wk_ref, wv_ref, wo_ref, wg_ref, wu_ref, wd_ref,
        out_ref, ig_ref, gga_ref, ggb_ref, wdg_ref, wog_ref, cg_ref, gg_ref, ug_ref,
        XA, NA, DI, N2, BR, WC, WO, WG, WU, WD, KV, QV, AT, MX,
        P1, P2, P3, P4, R1, R2, R3, R4, HID, GG, UG, GF, UF, KS, KR, OG, QG,
        CS, CR, CK, GS, GR, GK, US, UR, UK, OS, OR, DS, DR,
        GA, GB, PA, PB, QA, QB, AC, ST, MID, GO, MG, OUT, DF, OF, ss, rs, ls,
    ) = refs
    C = D // Z
    QR = D // F
    HR = H // 2
    U = R // 2
    HB = Z * U
    s = lax.axis_index("section")
    f = lax.axis_index("frames")
    z = f // 2
    x = f % 2
    fx = f + 1 - 2 * x
    mate = z + 1 - 2 * (z % 2)
    half = z // 2
    edge = z * (1 - half) + (Z - 1 - z) * half
    outer = edge == 0
    gate = edge == 1
    bf = jnp.bfloat16
    f32 = jnp.float32

    def order(i):
        near = i + edge * (1 - i // 2) * (1 - 2 * i)
        return half * (Z - 1) + (1 - 2 * half) * near

    def rows(i, n):
        if isinstance(i, int):
            return pl.ds(i * n, n)
        return pl.ds(pl.multiple_of(i * n, n), n)

    def remote(src, dst, sslot, rslot, dev):
        return pltpu.make_async_remote_copy(
            src_ref=src, dst_ref=dst, send_sem=ss.at[sslot], recv_sem=rs.at[rslot],
            device_id=dev, device_id_type=pl.DeviceIdType.MESH,
        )

    def arrive(dst, rslot):
        remote(dst, dst, 0, rslot, (s, fx)).wait_recv()

    def tdot(a, b):
        return lax.dot_general(a, b, (((0,), (0,)), ((), ())), preferred_element_type=f32)

    def dott(a, b):
        return lax.dot_general(a, b, (((1,), (1,)), ((), ())), preferred_element_type=f32)

    def dot(a, b):
        return jnp.dot(a, b, preferred_element_type=f32)

    def loop(n, body):
        def step(i, carry):
            body(i)
            return carry
        lax.fori_loop(0, n, step, 0)

    def unit(h, b):
        return pl.ds(pl.multiple_of(h * HB + b * U, U), U)

    def part(h, k):
        return pl.ds((4 * h + k) * U, U) if isinstance(k, int) else pl.ds(pl.multiple_of((4 * h + k) * U, U), U)

    def own_rows(h):
        return pl.ds(h * U, U)

    def ag_copy(buf, base, h, b, up, src=None):
        ref = buf.at[unit(h, b)]
        base = base + 2 * Z * h
        return remote(
            ref if src is None else src, ref, base + b + (0 if up else Z), base + b, (s, f + (2 if up else -2))
        )

    def ag_start(buf, base, h, src=None):
        @pl.when(z < Z - 1)
        def _():
            ag_copy(buf, base, h, z, True, src).start()

        @pl.when(z > 0)
        def _():
            ag_copy(buf, base, h, z, False, src).start()

    def ag_step(buf, base, h, b):
        @pl.when(b != z)
        def _():
            arrive(buf.at[unit(h, b)], base + 2 * Z * h + b)

        @pl.when((b < z) & (z < Z - 1))
        def _():
            ag_copy(buf, base, h, b, True).start()

        @pl.when((b > z) & (z > 0))
        def _():
            ag_copy(buf, base, h, b, False).start()

    def ag_drain(buf, base):
        def body(b):
            for h in range(2):
                @pl.when((b <= z) & (z < Z - 1))
                def _(h=h):
                    ag_copy(buf, base, h, b, True).wait_send()

                @pl.when((b >= z) & (z > 0))
                def _(h=h):
                    ag_copy(buf, base, h, b, False).wait_send()
        loop(Z, body)

    def rs_mate(P, Q, base, h):
        return remote(P.at[unit(h, mate)], Q.at[part(h, 0)], base + 6 * h, base + 6 * h, (s, 2 * mate + x))

    def rs_pre(P, Q, base, h, b):
        slot = base + 6 * h + 2 + b % 2
        return remote(P.at[unit(h, b)], Q.at[part(h, 2 + b % 2)], slot, slot, (s, 2 * mate + x))

    def rs_far(P, Q, base, h, b):
        return remote(
            P.at[unit(h, b)], Q.at[part(h, 1)], base + 6 * h + 4 + b % 2, base + 6 * h + 1, (s, 2 * b + x)
        )

    def rs_send(P, Q, base, h):
        def body(i):
            b = order(Z - 1 - i)

            @pl.when(outer & (i < 2))
            def _():
                rs_pre(P, Q, base, h, b).start()

            @pl.when(b == mate)
            def _():
                rs_mate(P, Q, base, h).start()
        loop(Z - 1, body)

    def rs_gate(P, Q, base, h):
        @pl.when(gate)
        def _():
            def body(i):
                b = order(Z - 1 - i)
                arrive(Q.at[part(h, 2 + b % 2)], base + 6 * h + 2 + b % 2)
                P[unit(h, b), :] = (
                    P[unit(h, b), :].astype(f32) + Q[part(h, 2 + b % 2), :].astype(f32)
                ).astype(bf)
                rs_far(P, Q, base, h, b).start()
            loop(2, body)

    def rs_wait(P, Q, base, h):
        arrive(Q.at[part(h, 0)], base + 6 * h)
        arrive(Q.at[part(h, 1)], base + 6 * h + 1)
        return (
            P[unit(h, z), :].astype(f32) + Q[part(h, 0), :].astype(f32) + Q[part(h, 1), :].astype(f32)
        )

    def rs_drain(P, Q, base):
        for h in range(2):
            rs_mate(P, Q, base, h).wait_send()

            def body(i, h=h):
                b = order(Z - 1 - i)

                @pl.when(outer)
                def _():
                    rs_pre(P, Q, base, h, b).wait_send()

                @pl.when(gate)
                def _():
                    rs_far(P, Q, base, h, b).wait_send()
            loop(2, body)

    def col_copy(w, buf, base, a, width, k):
        to = (z + k) % Z
        cols = pl.ds(pl.multiple_of(to * width, width), width)
        return remote(
            w.at[:, cols], buf.at[rows(f, QR), pl.ds(a * width, width)],
            base + a * Z + k, base + a * Z + k, (s, 2 * to + x),
        )

    def own_copy(w, buf, slot, a, width):
        cols = pl.ds(pl.multiple_of(z * width, width), width)
        return pltpu.make_async_copy(w.at[:, cols], buf.at[rows(f, QR), pl.ds(a * width, width)], ls.at[slot])

    def side_copy(buf, base, line):
        ref = buf.at[rows(2 * line + x, QR)]
        return remote(ref, ref, base + line, base + line, (s, fx))

    def col_arrive(buf, base, count, width, k):
        line = (z + Z - k) % Z
        for a in range(count):
            arrive(buf.at[rows(2 * line + x, QR), pl.ds(a * width, width)], base + a * Z + k)
        return line

    def side_arrive(buf, base):
        loop(Z, lambda line: arrive(buf.at[rows(2 * line + 1 - x, QR)], base + line))

    def pair_copy(S_, Q_, base, line):
        return remote(S_.at[rows(line, QR)], Q_.at[rows(line, QR)], base + line, base + line, (s, fx))

    def home_copy(K_, o_ref, base, line):
        return remote(K_.at[rows(line, QR)], o_ref.at[z], base + line, base + z, (s, 2 * line + x))

    def grad_make(left, right, K_, S_, Q_, base):
        def body(line):
            both = tdot(left[:, pl.ds(pl.multiple_of(line * 2 * QR, 2 * QR), 2 * QR)], right[...]).astype(bf)
            K_[rows(line, QR), :] = jnp.where(x == 0, both[:QR], both[QR:])
            S_[rows(line, QR), :] = jnp.where(x == 0, both[QR:], both[:QR])
            pair_copy(S_, Q_, base, line).start()
        loop(Z, body)

    def grad_home_step(K_, Q_, o_ref, pbase, hbase, slot, i):
        line = (z + 1 + i) % Z
        arrive(Q_.at[rows(line, QR)], pbase + line)
        K_[rows(line, QR), :] = (
            K_[rows(line, QR), :].astype(f32) + Q_[rows(line, QR), :].astype(f32)
        ).astype(bf)

        @pl.when(line != z)
        def _():
            home_copy(K_, o_ref, hbase, line).start()

        @pl.when(line == z)
        def _():
            pltpu.make_async_copy(K_.at[rows(line, QR)], o_ref.at[z], ls.at[slot]).start()

    def grad_home(*args):
        loop(Z, lambda i: grad_home_step(*args, i))

    def grad_drain(S_, K_, Q_, o_ref, pbase, hbase, slot):
        def body(line):
            pair_copy(S_, Q_, pbase, line).wait_send()

            @pl.when(line != z)
            def _():
                home_copy(K_, o_ref, hbase, line).wait_send()
                arrive(o_ref.at[line], hbase + line)
        loop(Z, body)
        pltpu.make_async_copy(K_.at[rows(z, QR)], o_ref.at[z], ls.at[slot]).wait()

    def gain_copy(src, buf, base, k, sliced):
        to = (f + k) % F
        return remote(src.at[to] if sliced else src, buf.at[f], base + k, base + k, (s, to))

    def gain_arrive(buf, base):
        for k in range(1, F):
            arrive(buf.at[(f + F - k) % F], base + k)

    def row_of(buf):
        return jnp.concatenate([buf[k] for k in range(F)], axis=-1)

    twin = s + 1 - 2 * (s % 2)
    first_of_chip = s % 2 == 0
    near_chip = s < 2

    def kv_copy(h, j, t, way):
        ref = KV.at[j * 2 + h]
        return remote(ref, ref, first["kv"] + way * 2 + h, first["kv"] + j * 2 + h, (t, f))

    def kv_twin(h):
        return kv_copy(h, s, s + 1, 0)

    def kv_across(h):
        return kv_copy(h, s, s + 2, 1)

    def kv_onward(h):
        return kv_copy(h, s - 2, twin, 2)

    def kv_pass(h):
        @pl.when(s >= 2)
        def _():
            arrive(KV.at[(s - 2) * 2 + h], first["kv"] + (s - 2) * 2 + h)
            kv_onward(h).start()

    def kg_copy(h, j):
        return remote(
            KS.at[j * 2 + h], KR.at[s * 2 + h], first["kg"] + j * 2 + h, first["kg"] + s * 2 + h, (j, f)
        )

    def wd_copy(h):
        n = HR // 2
        return remote(
            wd_ref.at[rows(h, n)], WD.at[rows(2 * x + h, n)], first["wd"] + h, first["wd"] + h, (s, fx)
        )

    def wd_arrive():
        for h in range(2):
            arrive(WD.at[rows(2 * (1 - x) + h, HR // 2)], first["wd"] + h)

    barrier = pltpu.get_barrier_semaphore()
    for k in range(1, F):
        pl.semaphore_signal(
            barrier, inc=1, device_id=(s, (f + k) % F), device_id_type=pl.DeviceIdType.MESH
        )
    for k in range(1, S):
        pl.semaphore_signal(
            barrier, inc=1, device_id=((s + k) % S, f), device_id_type=pl.DeviceIdType.MESH
        )
    qkv = (wq_ref, wk_ref, wv_ref)
    own_x = [
        pltpu.make_async_copy(x_ref.at[own_rows(h)], XA.at[unit(h, z)], ls.at[10 + h]) for h in range(2)
    ]
    own_c = [
        pltpu.make_async_copy(cot_ref.at[own_rows(h)], DI.at[unit(h, z)], ls.at[12 + h]) for h in range(2)
    ]
    wo_own = pltpu.make_async_copy(wo_ref, WO.at[rows(x, QR)], ls.at[3])
    wo_side = remote(wo_ref, WO.at[rows(x, QR)], first["wo"], first["wo"], (s, fx))
    wd_own = pltpu.make_async_copy(wd_ref, WD.at[rows(x, HR)], ls.at[4])
    down_out = remote(DS, DR, first["dx"], first["dx"], (s, fx))
    out_out = remote(OS, OR, first["ox"], first["ox"], (s, fx))
    for a in range(3):
        own_copy(qkv[a], WC, a, a, C).start()
    for item in own_x + own_c:
        item.start()
    wo_own.start()
    wd_own.start()
    own_copy(wg_ref, WG, 5, 0, H).start()
    own_copy(wu_ref, WU, 6, 0, H).start()
    GA[f] = ga_ref[...]
    GB[f] = gb_ref[...]
    for j in range(1, S):
        @pl.when(j > s)
        def _(j=j):
            KV[pl.ds(j * 2, 2)] = jnp.zeros((2, HB, 2 * C), bf)
    groups = lax.broadcasted_iota(jnp.int32, (C, C), 0) // HEAD_DIM
    ones = (groups == lax.broadcasted_iota(jnp.int32, (C, C), 1) // HEAD_DIM).astype(f32).astype(bf)
    same = lax.broadcasted_iota(jnp.int32, (R, R), 0) == lax.broadcasted_iota(jnp.int32, (R, R), 1)
    kept = jnp.where(same, (seg_ref[...] != 0).astype(f32), 0.0)
    mask = jnp.sum(kept, axis=1, keepdims=True)
    pl.semaphore_wait(barrier, F + S - 2)

    for h in range(2):
        ag_start(XA, first["na"], h, x_ref.at[own_rows(h)])
    for k in range(1, F):
        gain_copy(ga_ref, GA, first["ga"], k, False).start()

    def local_ready():
        for a in range(3):
            own_copy(qkv[a], WC, a, a, C).wait()
        side_copy(WC, first["wcx"], z).start()
        for k in range(1, F):
            gain_copy(gb_ref, GB, first["gb"], k, False).start()
        for item in own_x + own_c:
            item.wait()
        for h in range(2):
            ST[own_rows(h), :] = XA[unit(h, z), :].astype(f32)
            GO[own_rows(h), :] = DI[unit(h, z), :].astype(f32) * mask[h * U : (h + 1) * U]
            DI[unit(h, z), :] = GO[own_rows(h), :].astype(bf)
        own_copy(wg_ref, WG, 5, 0, H).wait()
        own_copy(wu_ref, WU, 6, 0, H).wait()
        wd_own.wait()
        wo_own.wait()

    def wc_on(k):
        side_copy(WC, first["wcx"], col_arrive(WC, first["wc"], 3, C, k)).start()

    def head_sum(product):
        high = product.astype(bf)
        rest = (product - high.astype(f32)).astype(bf)
        return dot(high, ones) + dot(rest, ones)

    def chunk_of(h, c):
        return pl.ds(pl.multiple_of(h * HB + c * R, R), R)

    def make_qkv(h):
        def chunk(c):
            at, inner = chunk_of(h, c), rows(c, R)
            block = XA[at, :].astype(f32)
            scale = lax.rsqrt(jnp.mean(block * block, axis=-1, keepdims=True) + epsilon)
            normed = (block * scale * row_of(GA)).astype(bf)
            NA[at, :] = normed
            both = dot(normed, WC[...]).astype(bf)
            QV[at, :] = both[:, :C]
            KV[s * 2 + h, inner, :] = both[:, C:]
        loop(HB // R, chunk)

        @pl.when(near_chip)
        def _():
            kv_across(h).start()

        @pl.when(first_of_chip)
        def _():
            kv_twin(h).start()

    def attend_half(h):
        for j in range(S - 1):
            @pl.when((j < s) & (j != s - 2))
            def _(j=j):
                arrive(KV.at[j * 2 + h], first["kv"] + j * 2 + h)

        def chunk(c):
            at, inner = chunk_of(h, c), rows(c, R)
            query = QV[at, :].astype(f32)
            scores = []
            for j in range(S):
                score = head_sum(query * KV[j * 2 + h, inner, :C].astype(f32)) * HEAD_DIM ** (-0.5)
                scores.append(jnp.where(j <= s, score, -1e30))
            largest = functools.reduce(jnp.maximum, scores)
            expo = [jnp.exp(score - largest) for score in scores]
            total = functools.reduce(lambda u, v: u + v, expo)
            mixed = jnp.zeros((R, C), f32)
            for j in range(S):
                attn = expo[j] / total
                AT[j * 2 + h, inner, :] = attn
                mixed = mixed + attn * KV[j * 2 + h, inner, C:].astype(f32)
            mixed = mixed.astype(bf)
            MX[at, :] = mixed
            P1[at, :] = dot(mixed, WO[...]).astype(bf)
        loop(HB // R, chunk)
        rs_send(P1, R1, first["r1"], h)

    def middle_half(h):
        middle = ST[own_rows(h), :] + rs_wait(P1, R1, first["r1"], h)
        MID[own_rows(h), :] = middle
        inverse = lax.rsqrt(jnp.mean(middle * middle, axis=-1, keepdims=True) + epsilon)
        N2[unit(h, z), :] = (middle * inverse * row_of(GB)).astype(bf)
        ag_start(N2, first["n2"], h)

    def weights_ready():
        side_arrive(WG, first["wgx"])
        side_arrive(WU, first["wux"])

    def ffn_front(h):
        def chunk(c):
            at = chunk_of(h, c)
            normed2 = N2[at, :]
            gate_act = dot(normed2, WG[...])
            sig = 1.0 / (1.0 + jnp.exp(-gate_act))
            silu = gate_act * sig
            up_act = dot(normed2, WU[...])
            HID[at, :] = (silu * up_act).astype(bf)
            GF[at, :] = up_act * (sig * (1.0 + gate_act * (1.0 - sig)))
            UF[at, :] = silu
        loop(HB // R, chunk)

    def ffn_back(h):
        def chunk(c):
            at = chunk_of(h, c)
            hidden_grad = dott(DI[at, :], WD[...])
            gate_grad = (hidden_grad * GF[at, :]).astype(bf)
            up_grad = (hidden_grad * UF[at, :]).astype(bf)
            GG[at, :] = gate_grad
            UG[at, :] = up_grad
            P2[at, :] = (dott(gate_grad, WG[...]) + dott(up_grad, WU[...])).astype(bf)
        loop(HB // R, chunk)
        rs_send(P2, R2, first["r2"], h)

    def down_half(h):
        P3[rows(h, HB), :] = dot(HID[rows(h, HB), :], WD[...]).astype(bf)
        rs_send(P3, R3, first["r3"], h)

    def down_make(i):
        n = HR // 2
        mine = pl.ds(pl.multiple_of(x * HR + i * n, n), n)
        other = pl.ds(pl.multiple_of((1 - x) * HR + i * n, n), n)
        DS[rows(i, n), :] = tdot(HID[:, other], DI[...]).astype(bf)
        DF[rows(i, n), :] = tdot(HID[:, mine], DI[...])

    def out_make():
        both = tdot(MX[...], BR[...])
        OF[...] = jnp.where(x == 0, both[:QR], both[QR:])
        OS[...] = jnp.where(x == 0, both[QR:], both[:QR]).astype(bf)
        out_out.start()

    def split_gain(buf, sums, fresh):
        for k in range(F):
            piece = sums[:, k * QR : (k + 1) * QR]
            buf[k] = piece if fresh else buf[k] + piece

    def middle_grad_half(h):
        middle = MID[own_rows(h), :]
        inverse = lax.rsqrt(jnp.mean(middle * middle, axis=-1, keepdims=True) + epsilon)
        unit_rows = middle * inverse
        normed_grad = rs_wait(P2, R2, first["r2"], h)
        scaled = normed_grad * row_of(GB)
        middle_grad = GO[own_rows(h), :] + (
            scaled - unit_rows * jnp.mean(scaled * unit_rows, axis=-1, keepdims=True)
        ) * inverse
        MG[own_rows(h), :] = middle_grad
        BR[unit(h, z), :] = middle_grad.astype(bf)
        ag_start(BR, first["br"], h)
        split_gain(PB, jnp.sum(normed_grad * unit_rows, axis=0, keepdims=True), h == 0)
        if h == 1:
            for k in range(1, F):
                gain_copy(PB, QB, first["qb"], k, True).start()

    def back_half(h):
        def chunk(c):
            at, inner = chunk_of(h, c), rows(c, R)
            mixed_grad = dott(BR[at, :], WO[...])
            query = QV[at, :].astype(f32)
            inside = []
            total = jnp.zeros((R, C), f32)
            for j in range(S):
                one = head_sum(mixed_grad * KV[j * 2 + h, inner, C:].astype(f32))
                inside.append(one)
                total = total + AT[j * 2 + h, inner, :] * one
            query_grad = jnp.zeros((R, C), f32)
            for j in range(S):
                attn = AT[j * 2 + h, inner, :]
                score_grad = attn * (inside[j] - total) * HEAD_DIM ** (-0.5)
                query_grad = query_grad + score_grad * KV[j * 2 + h, inner, :C].astype(f32)
                key_part = score_grad * query
                value_part = attn * mixed_grad

                @pl.when(j == s)
                def _(key_part=key_part, value_part=value_part):
                    OG[h, inner, :C] = key_part
                    OG[h, inner, C:] = value_part

                @pl.when(j < s)
                def _(j=j, key_part=key_part, value_part=value_part):
                    KS[j * 2 + h, inner, :C] = key_part.astype(bf)
                    KS[j * 2 + h, inner, C:] = value_part.astype(bf)
            QG[at, :C] = query_grad.astype(bf)
        loop(HB // R, chunk)
        for j in range(S - 1):
            @pl.when(j < s)
            def _(j=j):
                kg_copy(h, j).start()

    def normed_half(h):
        for j in range(1, S):
            @pl.when(j > s)
            def _(j=j):
                arrive(KR.at[j * 2 + h], first["kg"] + j * 2 + h)
                OG[h] = OG[h] + KR[j * 2 + h].astype(f32)
        if h == 0:
            AC[...] = jnp.zeros((1, D), f32)

        def chunk(c):
            at = chunk_of(h, c)
            QG[at, C:] = OG[h, rows(c, R), :].astype(bf)
            normed_grad = dott(QG[at, :], WC[...])
            P4[at, :] = normed_grad.astype(bf)
            block = XA[at, :].astype(f32)
            scale = lax.rsqrt(jnp.mean(block * block, axis=-1, keepdims=True) + epsilon)
            AC[...] = AC[...] + jnp.sum(normed_grad * (block * scale), axis=0, keepdims=True)
        loop(HB // R, chunk)
        rs_send(P4, R4, first["r4"], h)
        if h == 1:
            for k in range(F):
                PA[k] = AC[:, k * QR : (k + 1) * QR]
            for k in range(1, F):
                gain_copy(PA, QA, first["qa"], k, True).start()

    def input_half(h):
        stream = ST[own_rows(h), :]
        inverse = lax.rsqrt(jnp.mean(stream * stream, axis=-1, keepdims=True) + epsilon)
        unit_rows = stream * inverse
        normed_grad = rs_wait(P4, R4, first["r4"], h)
        scaled = normed_grad * row_of(GA)
        ST[own_rows(h), :] = MG[own_rows(h), :] + (
            scaled - unit_rows * jnp.mean(scaled * unit_rows, axis=-1, keepdims=True)
        ) * inverse
        in_copy[h].start()

    def output_half(h):
        OUT[own_rows(h), :] = (MID[own_rows(h), :] + rs_wait(P3, R3, first["r3"], h)).astype(bf)

    out_copy = pltpu.make_async_copy(OUT, out_ref, ls.at[14])
    down_copy = pltpu.make_async_copy(DF, wdg_ref, ls.at[15])
    wo_copy = pltpu.make_async_copy(OF, wog_ref, ls.at[16])
    in_copy = [
        pltpu.make_async_copy(ST.at[own_rows(h)], ig_ref.at[own_rows(h)], ls.at[17 + h]) for h in range(2)
    ]

    def down_done():
        arrive(DR, first["dx"])
        DF[...] = DF[...] + DR[...].astype(f32)
        down_copy.start()

    def out_done():
        arrive(OR, first["ox"])
        OF[...] = OF[...] + OR[...].astype(f32)
        wo_copy.start()

    def gain_done(P_, Q_, base, target):
        Q_[f] = P_[f]
        gain_arrive(Q_, base)
        target[...] = functools.reduce(lambda u, v: u + v, [Q_[k] for k in range(F)])

    wd_copy(1).start()
    wo_side.start()
    for a in range(3):
        col_copy(qkv[a], WC, first["wc"], a, C, 1).start()
    local_ready()
    side_copy(WU, first["wux"], z).start()
    ag_step(XA, first["na"], 0, order(1))
    ag_step(XA, first["na"], 0, order(2))
    wd_copy(0).start()
    gain_arrive(GA, first["ga"])
    col_copy(wg_ref, WG, first["wg"], 0, H, 2).start()
    ag_step(XA, first["na"], 1, order(1))
    ag_step(XA, first["na"], 0, order(3))
    for a in range(3):
        col_copy(qkv[a], WC, first["wc"], a, C, 2).start()
    wc_on(1)
    arrive(WO.at[rows(1 - x, QR)], first["wo"])
    for a in range(3):
        col_copy(qkv[a], WC, first["wc"], a, C, 3).start()
    col_copy(wg_ref, WG, first["wg"], 0, H, 1).start()
    ag_step(XA, first["na"], 1, order(2))
    wc_on(2)
    wd_arrive()
    col_copy(wg_ref, WG, first["wg"], 0, H, 3).start()
    wc_on(3)
    ag_step(XA, first["na"], 1, order(3))
    col_copy(wu_ref, WU, first["wu"], 0, H, 1).start()
    col_copy(wu_ref, WU, first["wu"], 0, H, 3).start()
    side_copy(WG, first["wgx"], col_arrive(WG, first["wg"], 1, H, 1)).start()
    side_copy(WG, first["wgx"], col_arrive(WG, first["wg"], 1, H, 2)).start()
    side_arrive(WC, first["wcx"])
    make_qkv(0)
    col_copy(wu_ref, WU, first["wu"], 0, H, 2).start()
    make_qkv(1)
    kv_pass(0)
    attend_half(0)
    side_copy(WU, first["wux"], col_arrive(WU, first["wu"], 1, H, 1)).start()
    kv_pass(1)
    ag_start(DI, first["di"], 1)
    side_copy(WU, first["wux"], col_arrive(WU, first["wu"], 1, H, 2)).start()
    attend_half(1)
    side_copy(WG, first["wgx"], z).start()
    ag_start(DI, first["di"], 0)
    rs_gate(P1, R1, first["r1"], 0)
    rs_gate(P1, R1, first["r1"], 1)
    gain_arrive(GB, first["gb"])
    side_copy(WU, first["wux"], col_arrive(WU, first["wu"], 1, H, 3)).start()
    middle_half(0)
    middle_half(1)
    side_copy(WG, first["wgx"], col_arrive(WG, first["wg"], 1, H, 3)).start()
    ag_step(N2, first["n2"], 0, order(1))
    ag_step(N2, first["n2"], 0, order(2))
    ag_step(DI, first["di"], 0, order(1))
    ag_step(N2, first["n2"], 1, order(1))
    ag_step(DI, first["di"], 1, order(1))
    ag_step(DI, first["di"], 0, order(2))
    ag_step(DI, first["di"], 1, order(2))
    weights_ready()
    ag_step(N2, first["n2"], 0, order(3))
    ag_step(N2, first["n2"], 1, order(2))
    ffn_front(0)
    ag_step(DI, first["di"], 0, order(3))
    ffn_back(0)
    ag_step(DI, first["di"], 1, order(3))
    ag_step(N2, first["n2"], 1, order(3))
    ffn_front(1)
    ffn_back(1)
    grad_make(N2, GG, GK, GS, GR, first["gx"])
    rs_gate(P2, R2, first["r2"], 0)
    rs_gate(P2, R2, first["r2"], 1)
    middle_grad_half(0)
    down_half(1)
    down_half(0)
    middle_grad_half(1)
    ag_step(BR, first["br"], 0, order(1))
    grad_make(N2, UG, UK, US, UR, first["ux"])
    grad_home_step(GK, GR, gg_ref, first["gx"], first["gh"], 7, 1)
    grad_home_step(GK, GR, gg_ref, first["gx"], first["gh"], 7, 2)
    ag_step(BR, first["br"], 0, order(2))
    ag_step(BR, first["br"], 0, order(3))
    back_half(0)
    loop(2, down_make)
    down_out.start()
    ag_step(BR, first["br"], 1, order(1))
    ag_step(BR, first["br"], 1, order(2))
    grad_home_step(UK, UR, ug_ref, first["ux"], first["uh"], 8, 1)
    ag_step(BR, first["br"], 1, order(3))
    grad_home_step(UK, UR, ug_ref, first["ux"], first["uh"], 8, 0)
    grad_home_step(UK, UR, ug_ref, first["ux"], first["uh"], 8, 2)
    back_half(1)
    normed_half(0)
    grad_home_step(GK, GR, gg_ref, first["gx"], first["gh"], 7, 3)
    rs_gate(P3, R3, first["r3"], 0)
    rs_gate(P3, R3, first["r3"], 1)
    normed_half(1)
    grad_make(NA, QG, CK, CS, CR, first["cx"])
    grad_home_step(GK, GR, gg_ref, first["gx"], first["gh"], 7, 0)
    rs_gate(P4, R4, first["r4"], 0)
    gain_done(PB, QB, first["qb"], ggb_ref)
    grad_home_step(UK, UR, ug_ref, first["ux"], first["uh"], 8, 3)
    grad_home_step(CK, CR, cg_ref, first["cx"], first["ch"], 9, 2)
    out_make()
    grad_home_step(CK, CR, cg_ref, first["cx"], first["ch"], 9, 0)
    rs_gate(P4, R4, first["r4"], 1)
    out_done()
    grad_home_step(CK, CR, cg_ref, first["cx"], first["ch"], 9, 1)
    grad_home_step(CK, CR, cg_ref, first["cx"], first["ch"], 9, 3)
    output_half(0)
    down_done()
    input_half(0)
    output_half(1)
    input_half(1)
    out_copy.start()
    gain_done(PA, QA, first["qa"], gga_ref)

    for k in range(1, F):
        gain_copy(ga_ref, GA, first["ga"], k, False).wait_send()
        gain_copy(gb_ref, GB, first["gb"], k, False).wait_send()
        gain_copy(PA, QA, first["qa"], k, True).wait_send()
        gain_copy(PB, QB, first["qb"], k, True).wait_send()
    for k in range(1, Z):
        for a in range(3):
            col_copy(qkv[a], WC, first["wc"], a, C, k).wait_send()
        col_copy(wg_ref, WG, first["wg"], 0, H, k).wait_send()
        col_copy(wu_ref, WU, first["wu"], 0, H, k).wait_send()

    def sides(line):
        side_copy(WC, first["wcx"], line).wait_send()
        side_copy(WG, first["wgx"], line).wait_send()
        side_copy(WU, first["wux"], line).wait_send()
    loop(Z, sides)
    wo_side.wait_send()
    wd_copy(0).wait_send()
    wd_copy(1).wait_send()
    down_out.wait_send()
    out_out.wait_send()
    ag_drain(XA, first["na"])
    ag_drain(DI, first["di"])
    ag_drain(N2, first["n2"])
    ag_drain(BR, first["br"])
    rs_drain(P1, R1, first["r1"])
    rs_drain(P2, R2, first["r2"])
    rs_drain(P3, R3, first["r3"])
    rs_drain(P4, R4, first["r4"])

    def across(h):
        @pl.when(near_chip)
        def _():
            kv_across(h).wait_send()

        @pl.when(s >= 2)
        def _():
            kv_onward(h).wait_send()

        @pl.when(first_of_chip)
        def _():
            kv_twin(h).wait_send()

        for t in range(S):
            @pl.when(t < s)
            def _(t=t):
                kg_copy(h, t).wait_send()
    loop(2, across)
    grad_drain(GS, GK, GR, gg_ref, first["gx"], first["gh"], 7)
    grad_drain(US, UK, UR, ug_ref, first["ux"], first["uh"], 8)
    grad_drain(CS, CK, CR, cg_ref, first["cx"], first["ch"], 9)
    for item in (out_copy, down_copy, wo_copy, *in_copy):
        item.wait()


def finish(
    Z, QR, C, H, output, input_grad, gain_one, gain_two, down, out, cols, gate, up,
    o_in, o_q, o_k, o_v, o_gate, o_up, o_out, o_down, o_wo, o_ga, o_gb,
    gv, uv, cv, iv, dv, wv, ov, av, bv, iw, qf, kf, vf, gf, uf, ls, os,
):
    loads = [
        pltpu.make_async_copy(src, dst, ls.at[k])
        for k, (src, dst) in enumerate(
            (
                (gate, gv), (up, uv), (cols, cv), (input_grad, iv), (down, dv),
                (out, wv), (output, ov), (gain_one, av), (gain_two, bv),
            )
        )
    ]
    for item in loads:
        item.start()
    stores = []

    def store(src, dst):
        stores.append(pltpu.make_async_copy(src, dst, os.at[len(stores)]))
        stores[-1].start()

    for k, (low, full, target) in enumerate(((gv, gf, o_gate), (uv, uf, o_up))):
        loads[k].wait()
        for line in range(Z):
            cols_of = pl.ds(line * H, H)
            full[:, cols_of] = low[line].astype(jnp.float32)
            store(full.at[:, cols_of], target.at[:, cols_of])
    loads[2].wait()
    for part, (full, target) in enumerate(((qf, o_q), (kf, o_k), (vf, o_v))):
        for line in range(Z):
            full[:, line * C : (line + 1) * C] = cv[line, :, part * C : (part + 1) * C].astype(jnp.float32)
        store(full, target)
    loads[3].wait()
    iw[...] = iv[...].reshape(iw.shape)
    store(iw, o_in)
    for k, (src, dst) in enumerate(((dv, o_down), (wv, o_wo), (ov, o_out), (av, o_ga), (bv, o_gb))):
        loads[4 + k].wait()
        store(src, dst)
    for item in stores:
        item.wait()


def line_plan(
    frames_in, segment_ids, cotangent, norm_attn, w_query, w_key, w_value, w_out, norm_ffn, w_gate, w_up, w_down
):
    R, _, D = frames_in.shape
    F = lax.axis_size("frames")
    S = lax.axis_size("section")
    Z = F // 2
    C = D // Z
    H = w_gate.shape[3] // Z
    QR = D // F
    HR = H // 2
    HB = Z * R // 2
    counts = dict(
        ga=F, gb=F, qa=F, qb=F, wc=3 * Z, wcx=Z, wg=Z, wgx=Z, wu=Z, wux=Z, wo=1, wd=2,
        na=4 * Z, di=4 * Z, n2=4 * Z, br=4 * Z, r1=12, r2=12, r3=12, r4=12,
        kv=2 * S, kg=2 * S, gx=Z, gh=Z, ux=Z, uh=Z, cx=Z, ch=Z, ox=1, dx=1,
    )
    first, slots = {}, 0
    for name, count in counts.items():
        first[name] = slots
        slots += count
    bf, f32 = jnp.bfloat16, jnp.float32
    V = pltpu.VMEM
    scratch = [
        V((Z * R, D), bf), V((Z * R, D), bf), V((Z * R, D), bf), V((Z * R, D), bf), V((Z * R, D), bf),
        V((D, 3 * C), bf), V((2 * QR, D), bf), V((D, H), bf), V((D, H), bf), V((2 * HR, D), bf),
        V((2 * S, HB, 2 * C), bf), V((Z * R, C), bf), V((2 * S, HB, C), f32), V((Z * R, C), bf),
        V((Z * R, D), bf), V((Z * R, D), bf), V((Z * R, D), bf), V((Z * R, D), bf),
        V((4 * R, D), bf), V((4 * R, D), bf), V((4 * R, D), bf), V((4 * R, D), bf),
        V((Z * R, H), bf), V((Z * R, H), bf), V((Z * R, H), bf),
        V((Z * R, H), f32), V((Z * R, H), f32),
        V((2 * S, HB, 2 * C), bf), V((2 * S, HB, 2 * C), bf), V((2, HB, 2 * C), f32), V((Z * R, 3 * C), bf),
        V((Z * QR, 3 * C), bf), V((Z * QR, 3 * C), bf), V((Z * QR, 3 * C), bf),
        V((Z * QR, H), bf), V((Z * QR, H), bf), V((Z * QR, H), bf),
        V((Z * QR, H), bf), V((Z * QR, H), bf), V((Z * QR, H), bf),
        V((QR, D), bf), V((QR, D), bf), V((HR, D), bf), V((HR, D), bf),
        V((F, 1, QR), f32), V((F, 1, QR), f32), V((F, 1, QR), f32), V((F, 1, QR), f32),
        V((F, 1, QR), f32), V((F, 1, QR), f32), V((1, D), f32),
        V((R, D), f32), V((R, D), f32), V((R, D), f32), V((R, D), f32),
        V((R, D), bf), V((HR, D), f32), V((QR, D), f32),
        pltpu.SemaphoreType.DMA((slots,)), pltpu.SemaphoreType.DMA((slots,)), pltpu.SemaphoreType.DMA((19,)),
    ]
    vmem = pl.BlockSpec(memory_space=pltpu.VMEM)
    anyw = pl.BlockSpec(memory_space=pl.ANY)
    shape = jax.ShapeDtypeStruct
    results = pl.pallas_call(
        functools.partial(mega, Z, F, S, R, D, H, first),
        out_shape=(
            shape((R, D), bf), shape((R, D), f32), shape((1, QR), f32), shape((1, QR), f32),
            shape((HR, D), f32), shape((QR, D), f32),
            shape((Z, QR, 3 * C), bf), shape((Z, QR, H), bf), shape((Z, QR, H), bf),
        ),
        in_specs=[anyw, vmem, anyw, vmem, vmem] + [anyw] * 7,
        out_specs=(anyw, anyw, vmem, vmem) + (anyw,) * 5,
        scratch_shapes=scratch,
        compiler_params=pltpu.CompilerParams(
            collective_id=0, has_side_effects=True, vmem_limit_bytes=VMEM_LIMIT
        ),
        name="layer",
    )(
        frames_in[:, 0, :], segment_ids[None, :], cotangent[:, 0, :], norm_attn[0], norm_ffn[0],
        w_query[0, 0], w_key[0, 0], w_value[0, 0], w_out[0, 0], w_gate[0, 0], w_up[0, 0], w_down[0, 0],
    )
    output, input_grad, gain_one, gain_two, down, out, cols, gate, up = results
    done = pl.pallas_call(
        functools.partial(finish, Z, QR, C, H),
        out_shape=(
            shape((R, 1, D), f32), shape((QR, D), f32), shape((QR, D), f32), shape((QR, D), f32),
            shape((QR, Z * H), f32), shape((QR, Z * H), f32), shape((R, D), bf), shape((HR, D), f32),
            shape((QR, D), f32), shape((1, QR), f32), shape((1, QR), f32),
        ),
        in_specs=[anyw] * 9,
        out_specs=(anyw,) * 11,
        scratch_shapes=[
            V((Z, QR, H), bf), V((Z, QR, H), bf), V((Z, QR, 3 * C), bf), V((R, D), f32), V((HR, D), f32),
            V((QR, D), f32), V((R, D), bf), V((1, QR), f32), V((1, QR), f32),
            V((R, 1, D), f32), V((QR, D), f32), V((QR, D), f32), V((QR, D), f32), V((QR, Z * H), f32), V((QR, Z * H), f32),
            pltpu.SemaphoreType.DMA((9,)), pltpu.SemaphoreType.DMA((9 + 2 * Z,)),
        ],
        compiler_params=pltpu.CompilerParams(vmem_limit_bytes=VMEM_LIMIT),
        name="finish",
    )(output, input_grad, gain_one, gain_two, down, out, cols, gate, up)
    input_grad, query, key, value, gate, up, output, down, out, gain_one, gain_two = done
    return (
        output[:, None, :], input_grad, gain_one[None],
        query[None, None], key[None, None], value[None, None], out[None, None], gain_two[None],
        gate[None, None], up[None, None], down[None, None],
    )


def solution(mesh):
    placed = (
        P("frames", "section", None),
        P("frames"),
        P("frames", "section", None),
        P(None, "section", "frames"),
        P(None, "section", "frames", None),
        P(None, "section", "frames", None),
        P(None, "section", "frames", None),
        P(None, "section", "frames", None),
        P(None, "section", "frames"),
        P(None, "section", "frames", None),
        P(None, "section", "frames", None),
        P(None, "section", "frames", None),
    )
    lines = mesh.shape["frames"] == 8 and mesh.shape["section"] == 4

    def per_device(*arrays):
        width = arrays[0].shape[2]
        fits = lines and arrays[4].shape[0] == 1 and arrays[0].shape[1] == 1 and width % 1024 == 0
        return line_plan(*arrays) if fits else gather_plan(*arrays)

    return jax.shard_map(
        per_device,
        mesh=mesh,
        in_specs=placed,
        out_specs=(
            P("frames", "section", None),
            P("frames", "section", None),
            P(None, "section", "frames"),
            P(None, "section", "frames", None),
            P(None, "section", "frames", None),
            P(None, "section", "frames", None),
            P(None, "section", "frames", None),
            P(None, "section", "frames"),
            P(None, "section", "frames", None),
            P(None, "section", "frames", None),
            P(None, "section", "frames", None),
        ),
        check_vma=False,
    )
```

```python
import functools

import jax
import jax.numpy as jnp
from jax import lax
from jax.experimental import pallas as pl
from jax.experimental.pallas import tpu as pltpu
from jax.sharding import PartitionSpec as P

HEAD_DIM = 64
MICRO = 2
VMEM_LIMIT = 63 * 1024 * 1024


epsilon = 1e-05


def carried_in(shard, axis, combine, identity):
    devices, place = (lax.axis_size(axis), lax.axis_index(axis))
    everything = lax.all_gather(shard, axis)
    start = jnp.broadcast_to(jnp.asarray(identity, shard.dtype), shard.shape)

    def hop(k, before):
        reached = k < place
        new = combine(before, everything[k])
        return jnp.where(reached, new, before)

    return lax.fori_loop(0, devices, hop, start)


def carried_in_2(shard, axis, combine, identity):
    devices, place = (lax.axis_size(axis), lax.axis_index(axis))
    everything = lax.all_gather(shard.astype(jnp.bfloat16), axis)
    start = jnp.broadcast_to(jnp.asarray(identity, shard.dtype), shard.shape)

    def hop(k, before):
        at = devices - 1 - k
        reached = at > place
        new = combine(before, everything[at].astype(shard.dtype))
        return jnp.where(reached, new, before)

    return lax.fori_loop(0, devices, hop, start)


def rms_scale(values, gain):
    return values * lax.rsqrt(jnp.mean(values * values, axis=-1, keepdims=True) + epsilon) * gain


def project(left, weight):
    return jnp.dot(left, weight, preferred_element_type=jnp.float32)


def left_product(left, right):
    return lax.dot_general(
        left, right, (((0,), (0,)), ((), ())), preferred_element_type=jnp.float32
    )


def right_product(left, weight):
    return lax.dot_general(
        left, weight, (((1,), (1,)), ((), ())), preferred_element_type=jnp.float32
    )


def add_pair(first_part, second_part):
    return first_part + second_part


def attend(query_vec, key_all, values, section_idx):
    scores = jnp.einsum(
        "mhe,mphe->mhp", query_vec, key_all, precision=lax.Precision.HIGHEST
    ) * HEAD_DIM ** (-0.5)
    allowed = jnp.arange(key_all.shape[1]) <= section_idx
    scores = jnp.where(allowed, scores, -1e30)
    largest = jnp.max(scores, axis=-1, keepdims=True)
    expo_terms = jnp.exp(scores - largest)
    weights = expo_terms / jnp.sum(expo_terms, axis=-1, keepdims=True)
    return jnp.einsum("mhp,mphe->mhe", weights, values, precision=lax.Precision.HIGHEST)


def share_kv(own_kv, slot_mask):
    placed = jnp.where(slot_mask[None, :, None], own_kv[:, None, :], jnp.zeros((), jnp.bfloat16))
    earlier = carried_in(placed, "section", add_pair, jnp.zeros_like(placed))
    return earlier + placed


def return_kv_grads(grad_kv, section_idx):
    later_sum = carried_in_2(grad_kv, "section", add_pair, jnp.zeros_like(grad_kv))
    return lax.dynamic_index_in_dim(later_sum + grad_kv, section_idx, 1, keepdims=False)


def layer_rest(frame_rows, weights, query_vec, full_kv, section_idx):
    gain_one, wq_l, wk_l, wv_l, wo_l, gain_two, wg_l, wu_l, wd_l = weights
    packed_row_count = frame_rows.shape[0]
    model_width = frame_rows.shape[1]
    head_count = model_width // HEAD_DIM
    positions = full_kv.shape[1]
    key_all = (
        full_kv[:, :, :model_width]
        .astype(jnp.float32)
        .reshape(packed_row_count, positions, head_count, HEAD_DIM)
    )
    values = (
        full_kv[:, :, model_width:]
        .astype(jnp.float32)
        .reshape(packed_row_count, positions, head_count, HEAD_DIM)
    )
    query_f = query_vec.astype(jnp.float32).reshape(packed_row_count, head_count, HEAD_DIM)
    mixed_out = (
        attend(query_f, key_all, values, section_idx)
        .reshape(packed_row_count, model_width)
        .astype(jnp.bfloat16)
    )
    middle = frame_rows + project(mixed_out, wo_l)
    normed2 = rms_scale(middle, gain_two).astype(jnp.bfloat16)
    gate_act = project(normed2, wg_l)
    up_act = project(normed2, wu_l)
    hidden = (jax.nn.silu(gate_act) * up_act).astype(jnp.bfloat16)
    result = middle + project(hidden, wd_l)
    return (query_f, key_all, values, mixed_out, middle, normed2, gate_act, up_act, hidden, result)


def gather_plan(
    frames_in,
    segment_ids,
    cotangent,
    norm_attn,
    w_query,
    w_key,
    w_value,
    w_out,
    norm_ffn,
    w_gate,
    w_up,
    w_down,
):
    section_idx = lax.axis_index("section")
    frame_count = frames_in.shape[0]
    model_width = frames_in.shape[2]
    head_count = model_width // HEAD_DIM
    micro_rows = frame_count // MICRO
    positions = lax.axis_size("section") * frames_in.shape[1]
    layer_count = w_query.shape[0]
    slot_mask = jnp.arange(positions) == section_idx
    stream = frames_in[:, 0, :].astype(jnp.float32)
    layer_idx = 0
    pieces = (
        norm_attn[layer_idx],
        w_query[layer_idx],
        w_key[layer_idx],
        w_value[layer_idx],
        w_out[layer_idx],
        norm_ffn[layer_idx],
        w_gate[layer_idx],
        w_up[layer_idx],
        w_down[layer_idx],
    )
    gathered = (
        lax.all_gather(pieces[0].astype(jnp.bfloat16), "frames", axis=1, tiled=True).astype(
            jnp.float32
        ),
        lax.all_gather(pieces[1], "frames", axis=1, tiled=True),
        lax.all_gather(pieces[2], "frames", axis=1, tiled=True),
        lax.all_gather(pieces[3], "frames", axis=1, tiled=True),
        lax.all_gather(pieces[4], "frames", axis=1, tiled=True),
        lax.all_gather(pieces[5].astype(jnp.bfloat16), "frames", axis=1, tiled=True).astype(
            jnp.float32
        ),
        lax.all_gather(pieces[6], "frames", axis=1, tiled=True),
        lax.all_gather(pieces[7], "frames", axis=1, tiled=True),
        lax.all_gather(pieces[8], "frames", axis=1, tiled=True),
    )
    weights = tuple((gathered_item[0] for gathered_item in gathered))
    layer_inputs = []
    layer_kv = []
    results = []
    for micro_idx in range(MICRO):
        frame_rows = stream[micro_idx * micro_rows : (micro_idx + 1) * micro_rows]
        normed = rms_scale(frame_rows, weights[0]).astype(jnp.bfloat16)
        query_vec = project(normed, weights[1]).astype(jnp.bfloat16)
        own_kv = jnp.concatenate(
            [
                project(normed, weights[2]).astype(jnp.bfloat16),
                project(normed, weights[3]).astype(jnp.bfloat16),
            ],
            axis=-1,
        )
        full_kv = share_kv(own_kv, slot_mask)
        outcome = layer_rest(frame_rows, weights, query_vec, full_kv, section_idx)
        layer_inputs.append(frame_rows)
        layer_kv.append(full_kv)
        results.append(outcome[-1])
    kept_inputs = [layer_inputs]
    kept_kv = [layer_kv]
    stream = jnp.concatenate(results, axis=0)
    output = stream.astype(jnp.bfloat16)[:, None, :]
    frame_mask = (segment_ids != 0).astype(jnp.float32)[:, None]
    upstream_all = cotangent[:, 0, :].astype(jnp.float32) * frame_mask
    upstream = [
        upstream_all[micro_idx * micro_rows : (micro_idx + 1) * micro_rows]
        for micro_idx in range(MICRO)
    ]
    layer_grads = [None] * layer_count
    for layer_idx in reversed(range(layer_count)):
        pieces = (
            norm_attn[layer_idx],
            w_query[layer_idx],
            w_key[layer_idx],
            w_value[layer_idx],
            w_out[layer_idx],
            norm_ffn[layer_idx],
            w_gate[layer_idx],
            w_up[layer_idx],
            w_down[layer_idx],
        )
        gathered = (
            lax.all_gather(pieces[0].astype(jnp.bfloat16), "frames", axis=1, tiled=True).astype(
                jnp.float32
            ),
            lax.all_gather(pieces[1], "frames", axis=1, tiled=True),
            lax.all_gather(pieces[2], "frames", axis=1, tiled=True),
            lax.all_gather(pieces[3], "frames", axis=1, tiled=True),
            lax.all_gather(pieces[4], "frames", axis=1, tiled=True),
            lax.all_gather(pieces[5].astype(jnp.bfloat16), "frames", axis=1, tiled=True).astype(
                jnp.float32
            ),
            lax.all_gather(pieces[6], "frames", axis=1, tiled=True),
            lax.all_gather(pieces[7], "frames", axis=1, tiled=True),
            lax.all_gather(pieces[8], "frames", axis=1, tiled=True),
        )
        weights = tuple((gathered_item[0] for gathered_item in gathered))
        gain_one, wq_l, wk_l, wv_l, wo_l, gain_two, wg_l, wu_l, wd_l = weights
        totals = [jnp.zeros(item.shape, jnp.float32) for item in weights]
        for micro_idx in range(MICRO):
            micro_grads = [None] * 9
            frame_rows = kept_inputs[layer_idx][micro_idx]
            full_kv = kept_kv[layer_idx][micro_idx]
            grad_out = upstream[micro_idx]
            normed = rms_scale(frame_rows, gain_one).astype(jnp.bfloat16)
            query_vec = project(normed, wq_l).astype(jnp.bfloat16)
            (
                query_f,
                key_all,
                values,
                mixed_out,
                middle,
                normed2,
                gate_act,
                up_act,
                hidden,
                result,
            ) = layer_rest(frame_rows, weights, query_vec, full_kv, section_idx)
            down_in = grad_out.astype(jnp.bfloat16)
            micro_grads[8] = left_product(hidden, down_in)
            hidden_grad = right_product(down_in, wd_l)
            _, pullback = jax.vjp(
                lambda gate_in, up_in: jax.nn.silu(gate_in) * up_in, gate_act, up_act
            )
            gate_grad, up_grad = pullback(hidden_grad)
            gate_grad = gate_grad.astype(jnp.bfloat16)
            up_grad = up_grad.astype(jnp.bfloat16)
            micro_grads[6] = left_product(normed2, gate_grad)
            micro_grads[7] = left_product(normed2, up_grad)
            normed2_grad = right_product(gate_grad, wg_l) + right_product(up_grad, wu_l)
            _, pullback = jax.vjp(rms_scale, middle, gain_two)
            middle_part, gain_two_part = pullback(normed2_grad)
            middle_grad = grad_out + middle_part
            micro_grads[5] = gain_two_part
            branch_in = middle_grad.astype(jnp.bfloat16)
            micro_grads[4] = left_product(mixed_out, branch_in)
            mixed_grad = right_product(branch_in, wo_l)
            _, pullback = jax.vjp(
                lambda query_in, key_in, value_in: attend(query_in, key_in, value_in, section_idx),
                query_f,
                key_all,
                values,
            )
            query_grad, key_grad, value_grad = pullback(
                mixed_grad.reshape(micro_rows, head_count, HEAD_DIM)
            )
            grad_kv = jnp.concatenate(
                [
                    key_grad.reshape(micro_rows, positions, model_width),
                    value_grad.reshape(micro_rows, positions, model_width),
                ],
                axis=-1,
            )
            own_grad = return_kv_grads(grad_kv, section_idx)
            query_low = query_grad.reshape(micro_rows, model_width).astype(jnp.bfloat16)
            key_low = own_grad[:, :model_width].astype(jnp.bfloat16)
            value_low = own_grad[:, model_width:].astype(jnp.bfloat16)
            micro_grads[1] = left_product(normed, query_low)
            micro_grads[2] = left_product(normed, key_low)
            micro_grads[3] = left_product(normed, value_low)
            normed_grad = (
                right_product(query_low, wq_l)
                + right_product(key_low, wk_l)
                + right_product(value_low, wv_l)
            )
            _, pullback = jax.vjp(rms_scale, frame_rows, gain_one)
            rows_part, gain_one_part = pullback(normed_grad)
            micro_grads[0] = gain_one_part
            upstream[micro_idx] = middle_grad + rows_part
            totals = [first + second for first, second in zip(totals, micro_grads)]
        layer_grads[layer_idx] = lax.psum_scatter(
            tuple((item[None] for item in totals)), "frames", scatter_dimension=1, tiled=True
        )
    input_grad = jnp.concatenate(upstream, axis=0)[:, None, :]
    stacked = tuple((jnp.stack([layer_grads[0][which]]) for which in range(9)))
    return (
        output,
        input_grad,
        stacked[0],
        stacked[1],
        stacked[2],
        stacked[3],
        stacked[4],
        stacked[5],
        stacked[6],
        stacked[7],
        stacked[8],
    )


def mega(Z, F, S, R, D, H, first, *refs):
    (
        x_ref, seg_ref, cot_ref, ga_ref, gb_ref,
        wq_ref, wk_ref, wv_ref, wo_ref, wg_ref, wu_ref, wd_ref,
        out_ref, ig_ref, gga_ref, ggb_ref, wdg_ref, wog_ref, cg_ref, gg_ref, ug_ref,
        XA, NA, DI, N2, BR, WC, WO, WG, WU, WD, KV, QV, AT, MX,
        P1, P2, P3, P4, R1, R2, R3, R4, HID, GG, UG, GF, UF, PF, KS, KR, OG, QG,
        CS, CR, CK, GS, GR, GK, US, UR, UK, OS, OR, DS, DR,
        GA, GB, PA, PB, QA, QB, AC, ST, MID, GO, MG, OUT, DF, OF, ss, rs, ls,
    ) = refs
    C = D // Z
    QR = D // F
    HR = H // 2
    U = R // 2
    HB = Z * U
    s = lax.axis_index("section")
    f = lax.axis_index("frames")
    z = f // 2
    x = f % 2
    fx = f + 1 - 2 * x
    mate = z + 1 - 2 * (z % 2)
    half = z // 2
    edge = z * (1 - half) + (Z - 1 - z) * half
    outer = edge == 0
    gate = edge == 1
    bf = jnp.bfloat16
    f32 = jnp.float32

    def order(i):
        near = i + edge * (1 - i // 2) * (1 - 2 * i)
        return half * (Z - 1) + (1 - 2 * half) * near

    def rows(i, n):
        if isinstance(i, int):
            return pl.ds(i * n, n)
        return pl.ds(pl.multiple_of(i * n, n), n)

    def remote(src, dst, sslot, rslot, dev):
        return pltpu.make_async_remote_copy(
            src_ref=src, dst_ref=dst, send_sem=ss.at[sslot], recv_sem=rs.at[rslot],
            device_id=dev, device_id_type=pl.DeviceIdType.MESH,
        )

    def arrive(dst, rslot):
        remote(dst, dst, 0, rslot, (s, fx)).wait_recv()

    def tdot(a, b):
        return lax.dot_general(a, b, (((0,), (0,)), ((), ())), preferred_element_type=f32)

    def dott(a, b):
        return lax.dot_general(a, b, (((1,), (1,)), ((), ())), preferred_element_type=f32)

    def dot(a, b):
        return jnp.dot(a, b, preferred_element_type=f32)

    def loop(n, body):
        def step(i, carry):
            body(i)
            return carry
        lax.fori_loop(0, n, step, 0)

    def unit(h, b):
        return pl.ds(pl.multiple_of(h * HB + b * U, U), U)

    def part(h, k):
        return pl.ds((4 * h + k) * U, U) if isinstance(k, int) else pl.ds(pl.multiple_of((4 * h + k) * U, U), U)

    def own_rows(h):
        return pl.ds(h * U, U)

    def ag_copy(buf, base, h, b, up, src=None):
        ref = buf.at[unit(h, b)]
        base = base + 2 * Z * h
        return remote(
            ref if src is None else src, ref, base + b + (0 if up else Z), base + b, (s, f + (2 if up else -2))
        )

    def ag_start(buf, base, h, src=None):
        @pl.when(z < Z - 1)
        def _():
            ag_copy(buf, base, h, z, True, src).start()

        @pl.when(z > 0)
        def _():
            ag_copy(buf, base, h, z, False, src).start()

    def ag_step(buf, base, h, b):
        @pl.when(b != z)
        def _():
            arrive(buf.at[unit(h, b)], base + 2 * Z * h + b)

        @pl.when((b < z) & (z < Z - 1))
        def _():
            ag_copy(buf, base, h, b, True).start()

        @pl.when((b > z) & (z > 0))
        def _():
            ag_copy(buf, base, h, b, False).start()

    def ag_drain(buf, base):
        def body(b):
            for h in range(2):
                @pl.when((b <= z) & (z < Z - 1))
                def _(h=h):
                    ag_copy(buf, base, h, b, True).wait_send()

                @pl.when((b >= z) & (z > 0))
                def _(h=h):
                    ag_copy(buf, base, h, b, False).wait_send()
        loop(Z, body)

    def rs_mate(P, Q, base, h):
        return remote(P.at[unit(h, mate)], Q.at[part(h, 0)], base + 6 * h, base + 6 * h, (s, 2 * mate + x))

    def rs_pre(P, Q, base, h, b):
        slot = base + 6 * h + 2 + b % 2
        return remote(P.at[unit(h, b)], Q.at[part(h, 2 + b % 2)], slot, slot, (s, 2 * mate + x))

    def rs_far(P, Q, base, h, b):
        return remote(
            P.at[unit(h, b)], Q.at[part(h, 1)], base + 6 * h + 4 + b % 2, base + 6 * h + 1, (s, 2 * b + x)
        )

    def rs_send(P, Q, base, h):
        def body(i):
            b = order(Z - 1 - i)

            @pl.when(outer & (i < 2))
            def _():
                rs_pre(P, Q, base, h, b).start()

            @pl.when(b == mate)
            def _():
                rs_mate(P, Q, base, h).start()
        loop(Z - 1, body)

    def rs_gate(P, Q, base, h):
        @pl.when(gate)
        def _():
            def body(i):
                b = order(Z - 1 - i)
                arrive(Q.at[part(h, 2 + b % 2)], base + 6 * h + 2 + b % 2)
                P[unit(h, b), :] = (
                    P[unit(h, b), :].astype(f32) + Q[part(h, 2 + b % 2), :].astype(f32)
                ).astype(bf)
                rs_far(P, Q, base, h, b).start()
            loop(2, body)

    def rs_wait(P, Q, base, h):
        arrive(Q.at[part(h, 0)], base + 6 * h)
        arrive(Q.at[part(h, 1)], base + 6 * h + 1)
        return (
            P[unit(h, z), :].astype(f32) + Q[part(h, 0), :].astype(f32) + Q[part(h, 1), :].astype(f32)
        )

    def rs_drain(P, Q, base):
        for h in range(2):
            rs_mate(P, Q, base, h).wait_send()

            def body(i, h=h):
                b = order(Z - 1 - i)

                @pl.when(outer)
                def _():
                    rs_pre(P, Q, base, h, b).wait_send()

                @pl.when(gate)
                def _():
                    rs_far(P, Q, base, h, b).wait_send()
            loop(2, body)

    def col_copy(w, buf, base, a, width, k):
        to = (z + k) % Z
        cols = pl.ds(pl.multiple_of(to * width, width), width)
        return remote(
            w.at[:, cols], buf.at[rows(f, QR), pl.ds(a * width, width)],
            base + a * Z + k, base + a * Z + k, (s, 2 * to + x),
        )

    def ff_copy(w, buf, base, c, k):
        to = (z + k) % Z
        cols = pl.ds(pl.multiple_of(to * H + c * HR, HR), HR)
        slot = base + c * Z + k
        return remote(w.at[:, cols], buf.at[rows(f, QR), pl.ds(c * HR, HR)], slot, slot, (s, 2 * to + x))

    def ff_side(buf, base, c, line):
        ref = buf.at[rows(2 * line + x, QR), pl.ds(c * HR, HR)]
        return remote(ref, ref, base + c * Z + line, base + c * Z + line, (s, fx))

    def ff_on(buf, base, xbase, c, k):
        line = (z + Z - k) % Z
        arrive(buf.at[rows(2 * line + x, QR), pl.ds(c * HR, HR)], base + c * Z + k)
        ff_side(buf, xbase, c, line).start()

    def own_copy(w, buf, slot, a, width):
        cols = pl.ds(pl.multiple_of(z * width, width), width)
        return pltpu.make_async_copy(w.at[:, cols], buf.at[rows(f, QR), pl.ds(a * width, width)], ls.at[slot])

    def side_copy(buf, base, line):
        ref = buf.at[rows(2 * line + x, QR)]
        return remote(ref, ref, base + line, base + line, (s, fx))

    def col_arrive(buf, base, count, width, k):
        line = (z + Z - k) % Z
        for a in range(count):
            arrive(buf.at[rows(2 * line + x, QR), pl.ds(a * width, width)], base + a * Z + k)
        return line

    def side_arrive(buf, base):
        loop(Z, lambda line: arrive(buf.at[rows(2 * line + 1 - x, QR)], base + line))

    def pair_copy(S_, Q_, base, line):
        return remote(S_.at[rows(line, QR)], Q_.at[rows(line, QR)], base + line, base + line, (s, fx))

    def home_copy(K_, o_ref, base, line):
        return remote(K_.at[rows(line, QR)], o_ref.at[z], base + line, base + z, (s, 2 * line + x))

    def grad_make(left, right, K_, S_, Q_, base):
        def body(line):
            both = tdot(left[:, pl.ds(pl.multiple_of(line * 2 * QR, 2 * QR), 2 * QR)], right[...]).astype(bf)
            K_[rows(line, QR), :] = jnp.where(x == 0, both[:QR], both[QR:])
            S_[rows(line, QR), :] = jnp.where(x == 0, both[QR:], both[:QR])
            pair_copy(S_, Q_, base, line).start()
        loop(Z, body)

    def grad_home_step(K_, Q_, o_ref, pbase, hbase, slot, i):
        line = (z + 1 + i) % Z
        arrive(Q_.at[rows(line, QR)], pbase + line)
        K_[rows(line, QR), :] = (
            K_[rows(line, QR), :].astype(f32) + Q_[rows(line, QR), :].astype(f32)
        ).astype(bf)

        @pl.when(line != z)
        def _():
            home_copy(K_, o_ref, hbase, line).start()

        @pl.when(line == z)
        def _():
            pltpu.make_async_copy(K_.at[rows(line, QR)], o_ref.at[z], ls.at[slot]).start()

    def grad_home(*args):
        loop(Z, lambda i: grad_home_step(*args, i))

    def grad_drain(S_, K_, Q_, o_ref, pbase, hbase, slot):
        def body(line):
            pair_copy(S_, Q_, pbase, line).wait_send()

            @pl.when(line != z)
            def _():
                home_copy(K_, o_ref, hbase, line).wait_send()
                arrive(o_ref.at[line], hbase + line)
        loop(Z, body)
        pltpu.make_async_copy(K_.at[rows(z, QR)], o_ref.at[z], ls.at[slot]).wait()

    def gain_copy(src, buf, base, k, sliced):
        to = (f + k) % F
        return remote(src.at[to] if sliced else src, buf.at[f], base + k, base + k, (s, to))

    def gain_arrive(buf, base):
        for k in range(1, F):
            arrive(buf.at[(f + F - k) % F], base + k)

    def row_of(buf):
        return jnp.concatenate([buf[k] for k in range(F)], axis=-1)

    twin = s + 1 - 2 * (s % 2)
    first_of_chip = s % 2 == 0
    near_chip = s < 2

    def kv_copy(h, j, t, way):
        ref = KV.at[j * 2 + h]
        return remote(ref, ref, first["kv"] + way * 2 + h, first["kv"] + j * 2 + h, (t, f))

    def kv_twin(h):
        return kv_copy(h, s, s + 1, 0)

    def kv_across(h):
        return kv_copy(h, s, s + 2, 1)

    def kv_onward(h):
        return kv_copy(h, s - 2, twin, 2)

    def kv_pass(h):
        @pl.when(s >= 2)
        def _():
            arrive(KV.at[(s - 2) * 2 + h], first["kv"] + (s - 2) * 2 + h)
            kv_onward(h).start()

    def kg_copy(h, j):
        return remote(
            KS.at[j * 2 + h], KR.at[s * 2 + h], first["kg"] + j * 2 + h, first["kg"] + s * 2 + h, (j, f)
        )

    def wd_copy(h):
        n = HR // 2
        return remote(
            wd_ref.at[rows(h, n)], WD.at[rows(2 * x + h, n)], first["wd"] + h, first["wd"] + h, (s, fx)
        )

    def wd_arrive():
        for h in range(2):
            arrive(WD.at[rows(2 * (1 - x) + h, HR // 2)], first["wd"] + h)

    barrier = pltpu.get_barrier_semaphore()
    for k in range(1, F):
        pl.semaphore_signal(
            barrier, inc=1, device_id=(s, (f + k) % F), device_id_type=pl.DeviceIdType.MESH
        )
    for k in range(1, S):
        pl.semaphore_signal(
            barrier, inc=1, device_id=((s + k) % S, f), device_id_type=pl.DeviceIdType.MESH
        )
    qkv = (wq_ref, wk_ref, wv_ref)
    own_x = [
        pltpu.make_async_copy(x_ref.at[own_rows(h)], XA.at[unit(h, z)], ls.at[10 + h]) for h in range(2)
    ]
    own_c = [
        pltpu.make_async_copy(cot_ref.at[own_rows(h)], DI.at[unit(h, z)], ls.at[12 + h]) for h in range(2)
    ]
    wo_own = pltpu.make_async_copy(wo_ref, WO.at[rows(x, QR)], ls.at[3])
    wo_side = remote(wo_ref, WO.at[rows(x, QR)], first["wo"], first["wo"], (s, fx))
    wd_own = pltpu.make_async_copy(wd_ref, WD.at[rows(x, HR)], ls.at[4])
    down_out = remote(DS, DR, first["dx"], first["dx"], (s, fx))
    out_out = remote(OS, OR, first["ox"], first["ox"], (s, fx))
    for a in range(3):
        own_copy(qkv[a], WC, a, a, C).start()
    for item in own_x + own_c:
        item.start()
    wo_own.start()
    wd_own.start()
    own_copy(wg_ref, WG, 5, 0, H).start()
    own_copy(wu_ref, WU, 6, 0, H).start()
    GA[f] = ga_ref[...]
    GB[f] = gb_ref[...]
    for j in range(1, S):
        @pl.when(j > s)
        def _(j=j):
            KV[pl.ds(j * 2, 2)] = jnp.zeros((2, HB, 2 * C), bf)
    groups = lax.broadcasted_iota(jnp.int32, (C, C), 0) // HEAD_DIM
    ones = (groups == lax.broadcasted_iota(jnp.int32, (C, C), 1) // HEAD_DIM).astype(f32).astype(bf)
    same = lax.broadcasted_iota(jnp.int32, (R, R), 0) == lax.broadcasted_iota(jnp.int32, (R, R), 1)
    kept = jnp.where(same, (seg_ref[...] != 0).astype(f32), 0.0)
    mask = jnp.sum(kept, axis=1, keepdims=True)
    pl.semaphore_wait(barrier, F + S - 2)

    for h in range(2):
        ag_start(XA, first["na"], h, x_ref.at[own_rows(h)])
    for k in range(1, F):
        gain_copy(ga_ref, GA, first["ga"], k, False).start()

    def local_ready():
        for a in range(3):
            own_copy(qkv[a], WC, a, a, C).wait()
        side_copy(WC, first["wcx"], z).start()
        for k in range(1, F):
            gain_copy(gb_ref, GB, first["gb"], k, False).start()
        for item in own_x + own_c:
            item.wait()
        for h in range(2):
            ST[own_rows(h), :] = XA[unit(h, z), :].astype(f32)
            GO[own_rows(h), :] = DI[unit(h, z), :].astype(f32) * mask[h * U : (h + 1) * U]
            DI[unit(h, z), :] = GO[own_rows(h), :].astype(bf)
        own_copy(wg_ref, WG, 5, 0, H).wait()
        own_copy(wu_ref, WU, 6, 0, H).wait()
        wd_own.wait()
        wo_own.wait()

    def wc_on(k):
        side_copy(WC, first["wcx"], col_arrive(WC, first["wc"], 3, C, k)).start()

    def head_sum(product):
        high = product.astype(bf)
        rest = (product - high.astype(f32)).astype(bf)
        return dot(high, ones) + dot(rest, ones)

    def chunk_of(h, c):
        return pl.ds(pl.multiple_of(h * HB + c * R, R), R)

    def make_qkv(h):
        def chunk(c):
            at, inner = chunk_of(h, c), rows(c, R)
            block = XA[at, :].astype(f32)
            scale = lax.rsqrt(jnp.mean(block * block, axis=-1, keepdims=True) + epsilon)
            normed = (block * scale * row_of(GA)).astype(bf)
            NA[at, :] = normed
            both = dot(normed, WC[...]).astype(bf)
            QV[at, :] = both[:, :C]
            KV[s * 2 + h, inner, :] = both[:, C:]
        loop(HB // R, chunk)

        @pl.when(near_chip)
        def _():
            kv_across(h).start()

        @pl.when(first_of_chip)
        def _():
            kv_twin(h).start()

    def attend_half(h):
        for j in range(S - 1):
            @pl.when((j < s) & (j != s - 2))
            def _(j=j):
                arrive(KV.at[j * 2 + h], first["kv"] + j * 2 + h)

        def chunk(c):
            at, inner = chunk_of(h, c), rows(c, R)
            query = QV[at, :].astype(f32)
            scores = []
            for j in range(S):
                score = head_sum(query * KV[j * 2 + h, inner, :C].astype(f32)) * HEAD_DIM ** (-0.5)
                scores.append(jnp.where(j <= s, score, -1e30))
            largest = functools.reduce(jnp.maximum, scores)
            expo = [jnp.exp(score - largest) for score in scores]
            total = functools.reduce(lambda u, v: u + v, expo)
            mixed = jnp.zeros((R, C), f32)
            for j in range(S):
                attn = expo[j] / total
                AT[j * 2 + h, inner, :] = attn
                mixed = mixed + attn * KV[j * 2 + h, inner, C:].astype(f32)
            mixed = mixed.astype(bf)
            MX[at, :] = mixed
            P1[at, :] = dot(mixed, WO[...]).astype(bf)
        loop(HB // R, chunk)
        rs_send(P1, R1, first["r1"], h)

    def middle_half(h):
        middle = ST[own_rows(h), :] + rs_wait(P1, R1, first["r1"], h)
        MID[own_rows(h), :] = middle
        inverse = lax.rsqrt(jnp.mean(middle * middle, axis=-1, keepdims=True) + epsilon)
        N2[unit(h, z), :] = (middle * inverse * row_of(GB)).astype(bf)
        ag_start(N2, first["n2"], h)

    def weights_ready(c):
        for buf, base in ((WG, first["wgx"]), (WU, first["wux"])):
            def body(line, buf=buf, base=base):
                arrive(buf.at[rows(2 * line + 1 - x, QR), pl.ds(c * HR, HR)], base + c * Z + line)
            loop(Z, body)

    def ffn_front(h, c):
        at, cols = rows(h, HB), pl.ds(c * HR, HR)
        normed2 = N2[at, :]
        gate_act = dot(normed2, WG[:, cols])
        sig = 1.0 / (1.0 + jnp.exp(-gate_act))
        silu = gate_act * sig
        up_act = dot(normed2, WU[:, cols])
        HID[at, cols] = (silu * up_act).astype(bf)
        GF[at, cols] = up_act * (sig * (1.0 + gate_act * (1.0 - sig)))
        UF[at, cols] = silu

    def ffn_back(h, c):
        at, cols = rows(h, HB), pl.ds(c * HR, HR)
        hidden_grad = dott(DI[at, :], WD[rows(c, HR), :])
        gate_grad = (hidden_grad * GF[at, cols]).astype(bf)
        up_grad = (hidden_grad * UF[at, cols]).astype(bf)
        GG[at, cols] = gate_grad
        UG[at, cols] = up_grad
        both = dott(gate_grad, WG[:, cols]) + dott(up_grad, WU[:, cols])
        if c == 0:
            PF[at, :] = both
        else:
            P2[at, :] = (PF[at, :] + both).astype(bf)
            rs_send(P2, R2, first["r2"], h)

    def down_half(h):
        P3[rows(h, HB), :] = dot(HID[rows(h, HB), :], WD[...]).astype(bf)
        rs_send(P3, R3, first["r3"], h)

    def down_make(i):
        n = HR // 2
        mine = pl.ds(pl.multiple_of(x * HR + i * n, n), n)
        other = pl.ds(pl.multiple_of((1 - x) * HR + i * n, n), n)
        DS[rows(i, n), :] = tdot(HID[:, other], DI[...]).astype(bf)
        DF[rows(i, n), :] = tdot(HID[:, mine], DI[...])

    def out_make():
        both = tdot(MX[...], BR[...])
        OF[...] = jnp.where(x == 0, both[:QR], both[QR:])
        OS[...] = jnp.where(x == 0, both[QR:], both[:QR]).astype(bf)
        out_out.start()

    def split_gain(buf, sums, fresh):
        for k in range(F):
            piece = sums[:, k * QR : (k + 1) * QR]
            buf[k] = piece if fresh else buf[k] + piece

    def middle_grad_half(h):
        middle = MID[own_rows(h), :]
        inverse = lax.rsqrt(jnp.mean(middle * middle, axis=-1, keepdims=True) + epsilon)
        unit_rows = middle * inverse
        normed_grad = rs_wait(P2, R2, first["r2"], h)
        scaled = normed_grad * row_of(GB)
        middle_grad = GO[own_rows(h), :] + (
            scaled - unit_rows * jnp.mean(scaled * unit_rows, axis=-1, keepdims=True)
        ) * inverse
        MG[own_rows(h), :] = middle_grad
        BR[unit(h, z), :] = middle_grad.astype(bf)
        ag_start(BR, first["br"], h)
        split_gain(PB, jnp.sum(normed_grad * unit_rows, axis=0, keepdims=True), h == 0)
        if h == 1:
            for k in range(1, F):
                gain_copy(PB, QB, first["qb"], k, True).start()

    def back_half(h):
        def chunk(c):
            at, inner = chunk_of(h, c), rows(c, R)
            mixed_grad = dott(BR[at, :], WO[...])
            query = QV[at, :].astype(f32)
            inside = []
            total = jnp.zeros((R, C), f32)
            for j in range(S):
                one = head_sum(mixed_grad * KV[j * 2 + h, inner, C:].astype(f32))
                inside.append(one)
                total = total + AT[j * 2 + h, inner, :] * one
            query_grad = jnp.zeros((R, C), f32)
            for j in range(S):
                attn = AT[j * 2 + h, inner, :]
                score_grad = attn * (inside[j] - total) * HEAD_DIM ** (-0.5)
                query_grad = query_grad + score_grad * KV[j * 2 + h, inner, :C].astype(f32)
                key_part = score_grad * query
                value_part = attn * mixed_grad

                @pl.when(j == s)
                def _(key_part=key_part, value_part=value_part):
                    OG[h, inner, :C] = key_part
                    OG[h, inner, C:] = value_part

                @pl.when(j < s)
                def _(j=j, key_part=key_part, value_part=value_part):
                    KS[j * 2 + h, inner, :C] = key_part.astype(bf)
                    KS[j * 2 + h, inner, C:] = value_part.astype(bf)
            QG[at, :C] = query_grad.astype(bf)
        loop(HB // R, chunk)
        for j in range(S - 1):
            @pl.when(j < s)
            def _(j=j):
                kg_copy(h, j).start()

    def normed_half(h):
        for j in range(1, S):
            @pl.when(j > s)
            def _(j=j):
                arrive(KR.at[j * 2 + h], first["kg"] + j * 2 + h)
                OG[h] = OG[h] + KR[j * 2 + h].astype(f32)
        if h == 0:
            AC[...] = jnp.zeros((1, D), f32)

        def chunk(c):
            at = chunk_of(h, c)
            QG[at, C:] = OG[h, rows(c, R), :].astype(bf)
            normed_grad = dott(QG[at, :], WC[...])
            P4[at, :] = normed_grad.astype(bf)
            block = XA[at, :].astype(f32)
            scale = lax.rsqrt(jnp.mean(block * block, axis=-1, keepdims=True) + epsilon)
            AC[...] = AC[...] + jnp.sum(normed_grad * (block * scale), axis=0, keepdims=True)
        loop(HB // R, chunk)
        rs_send(P4, R4, first["r4"], h)
        if h == 1:
            for k in range(F):
                PA[k] = AC[:, k * QR : (k + 1) * QR]
            for k in range(1, F):
                gain_copy(PA, QA, first["qa"], k, True).start()

    def input_half(h):
        stream = ST[own_rows(h), :]
        inverse = lax.rsqrt(jnp.mean(stream * stream, axis=-1, keepdims=True) + epsilon)
        unit_rows = stream * inverse
        normed_grad = rs_wait(P4, R4, first["r4"], h)
        scaled = normed_grad * row_of(GA)
        ST[own_rows(h), :] = MG[own_rows(h), :] + (
            scaled - unit_rows * jnp.mean(scaled * unit_rows, axis=-1, keepdims=True)
        ) * inverse
        in_copy[h].start()

    def output_half(h):
        OUT[own_rows(h), :] = (MID[own_rows(h), :] + rs_wait(P3, R3, first["r3"], h)).astype(bf)

    out_copy = pltpu.make_async_copy(OUT, out_ref, ls.at[14])
    down_copy = pltpu.make_async_copy(DF, wdg_ref, ls.at[15])
    wo_copy = pltpu.make_async_copy(OF, wog_ref, ls.at[16])
    in_copy = [
        pltpu.make_async_copy(ST.at[own_rows(h)], ig_ref.at[own_rows(h)], ls.at[17 + h]) for h in range(2)
    ]

    def down_done():
        arrive(DR, first["dx"])
        DF[...] = DF[...] + DR[...].astype(f32)
        down_copy.start()

    def out_done():
        arrive(OR, first["ox"])
        OF[...] = OF[...] + OR[...].astype(f32)
        wo_copy.start()

    def gain_done(P_, Q_, base, target):
        Q_[f] = P_[f]
        gain_arrive(Q_, base)
        target[...] = functools.reduce(lambda u, v: u + v, [Q_[k] for k in range(F)])

    wd_copy(1).start()
    for a in range(3):
        col_copy(qkv[a], WC, first["wc"], a, C, 1).start()
    gain_arrive(GA, first["ga"])
    wo_side.start()
    local_ready()
    ag_step(XA, first["na"], 0, order(1))
    ff_copy(wg_ref, WG, first["wg"], 0, 2).start()
    ag_step(XA, first["na"], 0, order(2))
    ag_step(XA, first["na"], 1, order(1))
    wc_on(1)
    wd_copy(0).start()
    ag_step(XA, first["na"], 0, order(3))
    for a in range(3):
        col_copy(qkv[a], WC, first["wc"], a, C, 2).start()
    arrive(WO.at[rows(1 - x, QR)], first["wo"])
    for a in range(3):
        col_copy(qkv[a], WC, first["wc"], a, C, 3).start()
    ag_step(XA, first["na"], 1, order(2))
    ff_copy(wg_ref, WG, first["wg"], 0, 1).start()
    wc_on(2)
    ff_copy(wg_ref, WG, first["wg"], 0, 3).start()
    wc_on(3)
    ag_step(XA, first["na"], 1, order(3))
    ff_copy(wu_ref, WU, first["wu"], 0, 3).start()
    ff_copy(wu_ref, WU, first["wu"], 0, 1).start()
    side_arrive(WC, first["wcx"])
    make_qkv(0)
    wd_arrive()
    ff_on(WG, first["wg"], first["wgx"], 0, 1)
    ff_copy(wg_ref, WG, first["wg"], 1, 3).start()
    ff_on(WG, first["wg"], first["wgx"], 0, 2)
    make_qkv(1)
    ff_copy(wu_ref, WU, first["wu"], 0, 2).start()
    gain_arrive(GB, first["gb"])
    kv_pass(0)
    ff_copy(wu_ref, WU, first["wu"], 1, 2).start()
    ff_side(WG, first["wgx"], 1, z).start()
    ff_copy(wu_ref, WU, first["wu"], 1, 3).start()
    ff_side(WG, first["wgx"], 0, z).start()
    ag_start(DI, first["di"], 1)
    ff_on(WG, first["wg"], first["wgx"], 0, 3)
    kv_pass(1)
    attend_half(0)
    ff_on(WU, first["wu"], first["wux"], 0, 1)
    attend_half(1)
    ff_on(WU, first["wu"], first["wux"], 0, 2)
    ag_start(DI, first["di"], 0)
    ff_on(WU, first["wu"], first["wux"], 0, 3)
    rs_gate(P1, R1, first["r1"], 0)
    rs_gate(P1, R1, first["r1"], 1)
    middle_half(0)
    ff_copy(wg_ref, WG, first["wg"], 1, 1).start()
    ff_on(WU, first["wu"], first["wux"], 1, 2)
    middle_half(1)
    ff_copy(wg_ref, WG, first["wg"], 1, 2).start()
    ff_side(WU, first["wux"], 0, z).start()
    ff_copy(wu_ref, WU, first["wu"], 1, 1).start()
    ag_step(N2, first["n2"], 0, order(1))
    ff_side(WU, first["wux"], 1, z).start()
    ff_on(WG, first["wg"], first["wgx"], 1, 3)
    ag_step(N2, first["n2"], 0, order(2))
    ag_step(DI, first["di"], 0, order(1))
    ff_on(WU, first["wu"], first["wux"], 1, 3)
    ag_step(N2, first["n2"], 1, order(1))
    ff_on(WG, first["wg"], first["wgx"], 1, 2)
    ag_step(DI, first["di"], 0, order(2))
    ff_on(WG, first["wg"], first["wgx"], 1, 1)
    weights_ready(0)
    ag_step(DI, first["di"], 1, order(1))
    ag_step(N2, first["n2"], 1, order(2))
    ag_step(DI, first["di"], 1, order(2))
    ff_on(WU, first["wu"], first["wux"], 1, 1)
    ag_step(N2, first["n2"], 0, order(3))
    ffn_front(0, 0)
    ag_step(DI, first["di"], 0, order(3))
    ffn_back(0, 0)
    ag_step(N2, first["n2"], 1, order(3))
    ffn_front(1, 0)
    weights_ready(1)
    ffn_front(0, 1)
    ag_step(DI, first["di"], 1, order(3))
    ffn_back(0, 1)
    ffn_back(1, 0)
    ffn_front(1, 1)
    ffn_back(1, 1)
    grad_make(N2, GG, GK, GS, GR, first["gx"])
    rs_gate(P2, R2, first["r2"], 0)
    rs_gate(P2, R2, first["r2"], 1)
    middle_grad_half(0)
    down_half(1)
    middle_grad_half(1)
    ag_step(BR, first["br"], 0, order(1))
    ag_step(BR, first["br"], 0, order(2))
    grad_home_step(GK, GR, gg_ref, first["gx"], first["gh"], 7, 2)
    grad_make(N2, UG, UK, US, UR, first["ux"])
    grad_home_step(GK, GR, gg_ref, first["gx"], first["gh"], 7, 1)
    ag_step(BR, first["br"], 0, order(3))
    down_half(0)
    ag_step(BR, first["br"], 1, order(1))
    back_half(0)
    loop(2, down_make)
    down_out.start()
    ag_step(BR, first["br"], 1, order(2))
    grad_home_step(UK, UR, ug_ref, first["ux"], first["uh"], 8, 1)
    ag_step(BR, first["br"], 1, order(3))
    grad_home_step(UK, UR, ug_ref, first["ux"], first["uh"], 8, 2)
    out_make()
    grad_home_step(UK, UR, ug_ref, first["ux"], first["uh"], 8, 0)
    back_half(1)
    grad_home_step(GK, GR, gg_ref, first["gx"], first["gh"], 7, 3)
    normed_half(0)
    rs_gate(P3, R3, first["r3"], 0)
    normed_half(1)
    grad_make(NA, QG, CK, CS, CR, first["cx"])
    grad_home_step(GK, GR, gg_ref, first["gx"], first["gh"], 7, 0)
    rs_gate(P3, R3, first["r3"], 1)
    rs_gate(P4, R4, first["r4"], 0)
    grad_home_step(CK, CR, cg_ref, first["cx"], first["ch"], 9, 2)
    grad_home_step(CK, CR, cg_ref, first["cx"], first["ch"], 9, 0)
    gain_done(PB, QB, first["qb"], ggb_ref)
    grad_home_step(UK, UR, ug_ref, first["ux"], first["uh"], 8, 3)
    rs_gate(P4, R4, first["r4"], 1)
    output_half(1)
    out_done()
    input_half(0)
    grad_home_step(CK, CR, cg_ref, first["cx"], first["ch"], 9, 1)
    grad_home_step(CK, CR, cg_ref, first["cx"], first["ch"], 9, 3)
    down_done()
    input_half(1)
    output_half(0)
    out_copy.start()
    gain_done(PA, QA, first["qa"], gga_ref)

    for k in range(1, F):
        gain_copy(ga_ref, GA, first["ga"], k, False).wait_send()
        gain_copy(gb_ref, GB, first["gb"], k, False).wait_send()
        gain_copy(PA, QA, first["qa"], k, True).wait_send()
        gain_copy(PB, QB, first["qb"], k, True).wait_send()
    for k in range(1, Z):
        for a in range(3):
            col_copy(qkv[a], WC, first["wc"], a, C, k).wait_send()
        for c in range(2):
            ff_copy(wg_ref, WG, first["wg"], c, k).wait_send()
            ff_copy(wu_ref, WU, first["wu"], c, k).wait_send()

    def sides(line):
        side_copy(WC, first["wcx"], line).wait_send()
        for c in range(2):
            ff_side(WG, first["wgx"], c, line).wait_send()
            ff_side(WU, first["wux"], c, line).wait_send()
    loop(Z, sides)
    wo_side.wait_send()
    wd_copy(0).wait_send()
    wd_copy(1).wait_send()
    down_out.wait_send()
    out_out.wait_send()
    ag_drain(XA, first["na"])
    ag_drain(DI, first["di"])
    ag_drain(N2, first["n2"])
    ag_drain(BR, first["br"])
    rs_drain(P1, R1, first["r1"])
    rs_drain(P2, R2, first["r2"])
    rs_drain(P3, R3, first["r3"])
    rs_drain(P4, R4, first["r4"])

    def across(h):
        @pl.when(near_chip)
        def _():
            kv_across(h).wait_send()

        @pl.when(s >= 2)
        def _():
            kv_onward(h).wait_send()

        @pl.when(first_of_chip)
        def _():
            kv_twin(h).wait_send()

        for t in range(S):
            @pl.when(t < s)
            def _(t=t):
                kg_copy(h, t).wait_send()
    loop(2, across)
    grad_drain(GS, GK, GR, gg_ref, first["gx"], first["gh"], 7)
    grad_drain(US, UK, UR, ug_ref, first["ux"], first["uh"], 8)
    grad_drain(CS, CK, CR, cg_ref, first["cx"], first["ch"], 9)
    for item in (out_copy, down_copy, wo_copy, *in_copy):
        item.wait()


def finish(
    Z, QR, C, H, output, input_grad, gain_one, gain_two, down, out, cols, gate, up,
    o_in, o_q, o_k, o_v, o_gate, o_up, o_out, o_down, o_wo, o_ga, o_gb,
    gv, uv, cv, iv, dv, wv, ov, av, bv, iw, qf, kf, vf, gf, uf, ls, os,
):
    loads = [
        pltpu.make_async_copy(src, dst, ls.at[k])
        for k, (src, dst) in enumerate(
            (
                (gate, gv), (up, uv), (cols, cv), (input_grad, iv), (down, dv),
                (out, wv), (output, ov), (gain_one, av), (gain_two, bv),
            )
        )
    ]
    for item in loads:
        item.start()
    stores = []

    def store(src, dst):
        stores.append(pltpu.make_async_copy(src, dst, os.at[len(stores)]))
        stores[-1].start()

    for k, (low, full, target) in enumerate(((gv, gf, o_gate), (uv, uf, o_up))):
        loads[k].wait()
        for line in range(Z):
            cols_of = pl.ds(line * H, H)
            full[:, cols_of] = low[line].astype(jnp.float32)
            store(full.at[:, cols_of], target.at[:, cols_of])
    loads[2].wait()
    for part, (full, target) in enumerate(((qf, o_q), (kf, o_k), (vf, o_v))):
        for line in range(Z):
            full[:, line * C : (line + 1) * C] = cv[line, :, part * C : (part + 1) * C].astype(jnp.float32)
        store(full, target)
    loads[3].wait()
    iw[...] = iv[...].reshape(iw.shape)
    store(iw, o_in)
    for k, (src, dst) in enumerate(((dv, o_down), (wv, o_wo), (ov, o_out), (av, o_ga), (bv, o_gb))):
        loads[4 + k].wait()
        store(src, dst)
    for item in stores:
        item.wait()


def line_plan(
    frames_in, segment_ids, cotangent, norm_attn, w_query, w_key, w_value, w_out, norm_ffn, w_gate, w_up, w_down
):
    R, _, D = frames_in.shape
    F = lax.axis_size("frames")
    S = lax.axis_size("section")
    Z = F // 2
    C = D // Z
    H = w_gate.shape[3] // Z
    QR = D // F
    HR = H // 2
    HB = Z * R // 2
    counts = dict(
        ga=F, gb=F, qa=F, qb=F, wc=3 * Z, wcx=Z, wg=2 * Z, wgx=2 * Z, wu=2 * Z, wux=2 * Z, wo=1, wd=2,
        na=4 * Z, di=4 * Z, n2=4 * Z, br=4 * Z, r1=12, r2=12, r3=12, r4=12,
        kv=2 * S, kg=2 * S, gx=Z, gh=Z, ux=Z, uh=Z, cx=Z, ch=Z, ox=1, dx=1,
    )
    first, slots = {}, 0
    for name, count in counts.items():
        first[name] = slots
        slots += count
    bf, f32 = jnp.bfloat16, jnp.float32
    V = pltpu.VMEM
    scratch = [
        V((Z * R, D), bf), V((Z * R, D), bf), V((Z * R, D), bf), V((Z * R, D), bf), V((Z * R, D), bf),
        V((D, 3 * C), bf), V((2 * QR, D), bf), V((D, H), bf), V((D, H), bf), V((2 * HR, D), bf),
        V((2 * S, HB, 2 * C), bf), V((Z * R, C), bf), V((2 * S, HB, C), f32), V((Z * R, C), bf),
        V((Z * R, D), bf), V((Z * R, D), bf), V((Z * R, D), bf), V((Z * R, D), bf),
        V((4 * R, D), bf), V((4 * R, D), bf), V((4 * R, D), bf), V((4 * R, D), bf),
        V((Z * R, H), bf), V((Z * R, H), bf), V((Z * R, H), bf),
        V((Z * R, H), f32), V((Z * R, H), f32), V((Z * R, D), f32),
        V((2 * S, HB, 2 * C), bf), V((2 * S, HB, 2 * C), bf), V((2, HB, 2 * C), f32), V((Z * R, 3 * C), bf),
        V((Z * QR, 3 * C), bf), V((Z * QR, 3 * C), bf), V((Z * QR, 3 * C), bf),
        V((Z * QR, H), bf), V((Z * QR, H), bf), V((Z * QR, H), bf),
        V((Z * QR, H), bf), V((Z * QR, H), bf), V((Z * QR, H), bf),
        V((QR, D), bf), V((QR, D), bf), V((HR, D), bf), V((HR, D), bf),
        V((F, 1, QR), f32), V((F, 1, QR), f32), V((F, 1, QR), f32), V((F, 1, QR), f32),
        V((F, 1, QR), f32), V((F, 1, QR), f32), V((1, D), f32),
        V((R, D), f32), V((R, D), f32), V((R, D), f32), V((R, D), f32),
        V((R, D), bf), V((HR, D), f32), V((QR, D), f32),
        pltpu.SemaphoreType.DMA((slots,)), pltpu.SemaphoreType.DMA((slots,)), pltpu.SemaphoreType.DMA((19,)),
    ]
    vmem = pl.BlockSpec(memory_space=pltpu.VMEM)
    anyw = pl.BlockSpec(memory_space=pl.ANY)
    shape = jax.ShapeDtypeStruct
    results = pl.pallas_call(
        functools.partial(mega, Z, F, S, R, D, H, first),
        out_shape=(
            shape((R, D), bf), shape((R, D), f32), shape((1, QR), f32), shape((1, QR), f32),
            shape((HR, D), f32), shape((QR, D), f32),
            shape((Z, QR, 3 * C), bf), shape((Z, QR, H), bf), shape((Z, QR, H), bf),
        ),
        in_specs=[anyw, vmem, anyw, vmem, vmem] + [anyw] * 7,
        out_specs=(anyw, anyw, vmem, vmem) + (anyw,) * 5,
        scratch_shapes=scratch,
        compiler_params=pltpu.CompilerParams(
            collective_id=0, has_side_effects=True, vmem_limit_bytes=VMEM_LIMIT
        ),
        name="layer",
    )(
        frames_in[:, 0, :], segment_ids[None, :], cotangent[:, 0, :], norm_attn[0], norm_ffn[0],
        w_query[0, 0], w_key[0, 0], w_value[0, 0], w_out[0, 0], w_gate[0, 0], w_up[0, 0], w_down[0, 0],
    )
    output, input_grad, gain_one, gain_two, down, out, cols, gate, up = results
    done = pl.pallas_call(
        functools.partial(finish, Z, QR, C, H),
        out_shape=(
            shape((R, 1, D), f32), shape((QR, D), f32), shape((QR, D), f32), shape((QR, D), f32),
            shape((QR, Z * H), f32), shape((QR, Z * H), f32), shape((R, D), bf), shape((HR, D), f32),
            shape((QR, D), f32), shape((1, QR), f32), shape((1, QR), f32),
        ),
        in_specs=[anyw] * 9,
        out_specs=(anyw,) * 11,
        scratch_shapes=[
            V((Z, QR, H), bf), V((Z, QR, H), bf), V((Z, QR, 3 * C), bf), V((R, D), f32), V((HR, D), f32),
            V((QR, D), f32), V((R, D), bf), V((1, QR), f32), V((1, QR), f32),
            V((R, 1, D), f32), V((QR, D), f32), V((QR, D), f32), V((QR, D), f32), V((QR, Z * H), f32), V((QR, Z * H), f32),
            pltpu.SemaphoreType.DMA((9,)), pltpu.SemaphoreType.DMA((9 + 2 * Z,)),
        ],
        compiler_params=pltpu.CompilerParams(vmem_limit_bytes=VMEM_LIMIT),
        name="finish",
    )(output, input_grad, gain_one, gain_two, down, out, cols, gate, up)
    input_grad, query, key, value, gate, up, output, down, out, gain_one, gain_two = done
    return (
        output[:, None, :], input_grad, gain_one[None],
        query[None, None], key[None, None], value[None, None], out[None, None], gain_two[None],
        gate[None, None], up[None, None], down[None, None],
    )


def solution(mesh):
    placed = (
        P("frames", "section", None),
        P("frames"),
        P("frames", "section", None),
        P(None, "section", "frames"),
        P(None, "section", "frames", None),
        P(None, "section", "frames", None),
        P(None, "section", "frames", None),
        P(None, "section", "frames", None),
        P(None, "section", "frames"),
        P(None, "section", "frames", None),
        P(None, "section", "frames", None),
        P(None, "section", "frames", None),
    )
    lines = mesh.shape["frames"] == 8 and mesh.shape["section"] == 4

    def per_device(*arrays):
        width = arrays[0].shape[2]
        fits = lines and arrays[4].shape[0] == 1 and arrays[0].shape[1] == 1 and width % 1024 == 0
        return line_plan(*arrays) if fits else gather_plan(*arrays)

    return jax.shard_map(
        per_device,
        mesh=mesh,
        in_specs=placed,
        out_specs=(
            P("frames", "section", None),
            P("frames", "section", None),
            P(None, "section", "frames"),
            P(None, "section", "frames", None),
            P(None, "section", "frames", None),
            P(None, "section", "frames", None),
            P(None, "section", "frames", None),
            P(None, "section", "frames"),
            P(None, "section", "frames", None),
            P(None, "section", "frames", None),
            P(None, "section", "frames", None),
        ),
        check_vma=False,
    )
```
